32 devices in a mesh: sfc: 32 (over z, y, x, core).
Axes of the slice: x: 2, y: 2, z: 4, core: 2. Of those that a mesh axis runs over, the one named last changes fastest.
Arguments:
- fraction: float32 [256, 4096], P('sfc'), may hold values from 0 to 1
- centroid: float32 [256, 3, 4096], P('sfc'), may hold values from -0.5 to 0.5
- velocity: float32 [256, 3, 4096], P('sfc'), may hold values from -4 to 4
- neighbours: int32 [256, 6], P('sfc'), may hold values from -1 to 255, as said below
- refinement: int32 [512, 4], P('sfc'), may hold values from -1 to 255, as said below
Outputs:
- planes: float32 [256, 4, 4096], P('sfc')
- reflux: float32 [256, 6, 2, 256], P('sfc')
The draws below stay inside these ranges and needn't reach their ends.
Inputs may be any that keep to these rules, and one draw needn't show every extreme that they name: `neighbours`: -1 marks the domain boundary; any other entry is a block on a device at most 2 away along the curve. `refinement`: each row is fine block, direction 0 to 5, coarse block, quadrant 0 to 3. A fine block of -1 marks an empty slot and a device's live slots come first; a live fine block is held by the device that holds the row; the coarse block lies on a device at most 2 away along the curve; every device has a live slot and some device has all 16 live.
All inputs are finite; a program needn't handle non-finite values.
Results may differ from the reference program's by a relative error of at most 0.0003.
Values sent between devices are 32-bit elements; how exact they have to be, the bound alone decides.
A program may use at most 64 MiB of HBM per device.

```python
import jax
import jax.numpy as jnp
from jax import lax

EDGE = 16
CELLS = 4096
FACE = 256
BLK = 8
REF_DEV = 16
REACH = 2
PASSES = 6
NB = 256
NREF = 512
N_SFC = 32


def draw_neighbours(key, part):
    devices = NB // BLK
    subkeys = jax.random.split(jax.random.fold_in(key, 11), 3)
    block_ids = jnp.arange(NB, dtype=jnp.int32)[:, None]
    direction_ids = jnp.arange(6, dtype=jnp.int32)[None, :]
    device_of = block_ids // BLK
    step_dev = jax.random.randint(subkeys[0], (NB, 6), -REACH, REACH + 1)
    target_dev = jnp.clip(device_of + step_dev, 0, devices - 1)
    local_slot = jax.random.randint(subkeys[1], (NB, 6), 0, BLK)
    chosen = target_dev * BLK + local_slot
    boundary = jax.random.randint(subkeys[2], (NB, 6), 0, 16) == 0
    chosen = jnp.where(boundary, -1, chosen)
    chosen = jnp.where((block_ids == 0) & (direction_ids == 0), -1, chosen)
    chosen = jnp.where((block_ids == NB - 1) & (direction_ids == 1), NB - 1, chosen)
    return chosen.astype(jnp.int32)


def draw_refinement(key, part):
    devices = NREF // REF_DEV
    subkeys = jax.random.split(jax.random.fold_in(key, 23), 7)
    slot_ids = jnp.arange(NREF, dtype=jnp.int32)
    device_of = slot_ids // REF_DEV
    within = slot_ids % REF_DEV
    counts = jax.random.randint(subkeys[0], (devices,), REF_DEV // 4 + 1, REF_DEV * 5 // 8 + 1)
    full_device = jax.random.randint(subkeys[1], (), 0, devices)
    counts = jnp.where(jnp.arange(devices, dtype=jnp.int32) == full_device, REF_DEV, counts)
    live = within < counts[device_of]
    fine = jnp.where(live, device_of * BLK + jax.random.randint(subkeys[2], (NREF,), 0, BLK), -1)
    direction = jax.random.randint(subkeys[3], (NREF,), 0, 6)
    coarse_dev = jnp.clip(device_of + jax.random.randint(subkeys[4], (NREF,), -REACH, REACH + 1), 0, devices - 1)
    coarse = coarse_dev * BLK + jax.random.randint(subkeys[5], (NREF,), 0, BLK)
    coarse = jnp.where(slot_ids == NREF - 1, devices * BLK - 1, coarse)
    quadrant = jax.random.randint(subkeys[6], (NREF,), 0, 4)
    return jnp.stack([fine, direction, coarse, quadrant], axis=1).astype(jnp.int32)


def level_of(own_key, dims, cuts, low, top_value):
    loudness, own = 1.0, jax.random.fold_in(own_key, 6)
    for axis_at, blocks in cuts:
        heights = jnp.exp(jax.random.uniform(jax.random.fold_in(own, axis_at), (blocks,), jnp.float32, low / len(cuts), top_value / len(cuts)))
        loudness = loudness * jnp.repeat(heights, dims[axis_at] // blocks).reshape([-1 if axis == axis_at else 1 for axis in range(len(dims))])
    return loudness


def bell_draw(key, extent, width, bound, cuts=(), held_as=jnp.bfloat16):
    loudness = level_of(key, extent, cuts, -0.22, 0.18) if cuts else 1.0
    drawn = jax.random.normal(key, extent, jnp.float32) * width * loudness
    return jnp.minimum(jnp.maximum(drawn, -bound), bound).astype(held_as)


def setup_inputs(seed: int = 0) -> dict:
    seeds = jax.random.split(jax.random.key(seed), 6)
    fraction = jnp.clip(1.0 * jax.random.uniform(seeds[0], (NB, CELLS), jnp.float32) ** level_of(seeds[0], (NB, CELLS), ((0, 32),), -0.2, 0.2), 0.0, 1.0)
    centroid = jnp.clip(jax.random.uniform(seeds[1], (NB, 3, CELLS), jnp.float32, -0.5, 0.5) * level_of(seeds[1], (NB, 3, CELLS), ((0, 32),), -0.4, 0.0), -0.5, 0.5)
    velocity = bell_draw(seeds[2], (NB, 3, CELLS), 1.0, 4.0, ((0, 32),), jnp.float32)
    neighbours = draw_neighbours(jax.random.fold_in(seeds[5], 71), 0)
    refinement = draw_refinement(jax.random.fold_in(seeds[5], 71), 0)
    return {"fraction": fraction, "centroid": centroid, "velocity": velocity, "neighbours": neighbours, "refinement": refinement}


time_step = 0.25
damping = 0.1

def faces_of(values):
    leading = values.shape[:-1]
    blocks_cube = values.reshape(leading + (EDGE, EDGE, EDGE))
    layers = [blocks_cube[..., 0, :, :], blocks_cube[..., EDGE - 1, :, :], blocks_cube[..., :, 0, :], blocks_cube[..., :, EDGE - 1, :], blocks_cube[..., :, :, 0], blocks_cube[..., :, :, EDGE - 1]]
    return jnp.stack([face_layer.reshape(leading + (EDGE * EDGE,)) for face_layer in layers], axis=len(leading) - 1)

def opposite_of(direction):
    return direction + 1 - 2 * (direction % 2)

def neighbour_fields(own_cells, ghost_faces):
    count_blocks, fields = (own_cells.shape[0], own_cells.shape[1])
    blocks_cube = own_cells.reshape(count_blocks, fields, EDGE, EDGE, EDGE)
    ghost_cube = ghost_faces.reshape(count_blocks, 6, fields, EDGE, EDGE)
    minus_x = jnp.concatenate([ghost_cube[:, 0][:, :, None], blocks_cube[:, :, :-1]], 2)
    plus_x = jnp.concatenate([blocks_cube[:, :, 1:], ghost_cube[:, 1][:, :, None]], 2)
    minus_y = jnp.concatenate([ghost_cube[:, 2][:, :, :, None], blocks_cube[:, :, :, :-1]], 3)
    plus_y = jnp.concatenate([blocks_cube[:, :, :, 1:], ghost_cube[:, 3][:, :, :, None]], 3)
    minus_z = jnp.concatenate([ghost_cube[:, 4][..., None], blocks_cube[..., :-1]], 4)
    plus_z = jnp.concatenate([blocks_cube[..., 1:], ghost_cube[:, 5][..., None]], 4)
    return [field.reshape(count_blocks, fields, -1) for field in (minus_x, plus_x, minus_y, plus_y, minus_z, plus_z)]

def cholesky_solve(matrix, vector):
    order_size = len(vector)
    lower = [[None] * order_size for _unused in range(order_size)]
    for row_index in range(order_size):
        for column_index in range(row_index + 1):
            running = matrix[row_index][column_index]
            for middle in range(column_index):
                running = running - lower[row_index][middle] * lower[column_index][middle]
            if row_index == column_index:
                lower[row_index][row_index] = jnp.sqrt(running)
            else:
                lower[row_index][column_index] = running / lower[column_index][column_index]
    forward = []
    for row_index in range(order_size):
        running = vector[row_index]
        for middle in range(row_index):
            running = running - lower[row_index][middle] * forward[middle]
        forward.append(running / lower[row_index][row_index])
    result = [None] * order_size
    for row_index in reversed(range(order_size)):
        running = forward[row_index]
        for middle in range(row_index + 1, order_size):
            running = running - lower[middle][row_index] * result[middle]
        result[row_index] = running / lower[row_index][row_index]
    return result

def fit_planes(center, neighbours_list):
    frac_center = center[:, 0]
    points = [(center[:, 1], center[:, 2], center[:, 3], frac_center)]
    for direction in range(6):
        axis_index = direction // 2
        offset = 2.0 * (direction % 2) - 1.0
        values = neighbours_list[direction]
        coords = [values[:, 1], values[:, 2], values[:, 3]]
        coords[axis_index] = coords[axis_index] + offset
        points.append((coords[0], coords[1], coords[2], values[:, 0]))
    params = [2.0 * (neighbours_list[2 * axis_index + 1][:, 0] - neighbours_list[2 * axis_index][:, 0]) for axis_index in range(3)]
    params.append(2.0 * (2.0 * frac_center - 1.0) - params[0] * center[:, 1] - params[1] * center[:, 2] - params[2] * center[:, 3])
    for _unused in range(PASSES):
        jacobian = []
        residual = []
        for point in points:
            phase = params[0] * point[0] + params[1] * point[1] + params[2] * point[2] + params[3]
            tanh_value = jnp.tanh(phase)
            residual.append(0.5 * (1.0 + tanh_value) - point[3])
            slope = 0.5 * (1.0 - tanh_value * tanh_value)
            jacobian.append([slope * point[0], slope * point[1], slope * point[2], slope])
        matrix = [[sum((row_entry[first_index] * row_entry[second_index] for row_entry in jacobian)) + (damping if first_index == second_index else 0.0) for second_index in range(4)] for first_index in range(4)]
        vector = [sum((jacobian[point_index][first_index] * residual[point_index] for point_index in range(7))) for first_index in range(4)]
        update = cholesky_solve(matrix, vector)
        params = [params[index_value] - update[index_value] for index_value in range(4)]
    return jnp.stack(params, axis=1)

def build_plane_faces(planes, velocity):
    coef_faces = faces_of(planes)
    speed_faces = faces_of(velocity)
    normal_speed = jnp.stack([speed_faces[:, direction, direction // 2] for direction in range(6)], axis=1)
    return jnp.concatenate([coef_faces, normal_speed[:, :, None]], 2)

def pick_component(coefs, which):
    picked = jnp.zeros_like(coefs[:, 0])
    for axis_index in range(3):
        picked = picked + (which[:, None] == axis_index).astype(coefs.dtype) * coefs[:, axis_index]
    return picked

def slot_moments(fine_face, coarse_face, direction, quadrant, live):
    face_index = jnp.arange(EDGE * EDGE, dtype=jnp.int32)
    first_pos = face_index // EDGE
    second_pos = face_index % EDGE
    half_edge = EDGE // 2
    coarse_cell = ((quadrant // 2)[:, None] * half_edge + first_pos[None] // 2) * EDGE + (quadrant % 2)[:, None] * half_edge + second_pos[None] // 2
    mapped = jnp.take_along_axis(coarse_face, coarse_cell[:, None, :], axis=2)
    axis_index = direction // 2
    first_tangent = jnp.where(axis_index == 0, 1, 0)
    second_tangent = jnp.where(axis_index == 2, 1, 2)
    sign = (2 * (direction % 2) - 1).astype(fine_face.dtype)[:, None]
    normal_fine = pick_component(fine_face, axis_index)
    normal_coarse = pick_component(mapped, axis_index)
    tangent_one = pick_component(mapped, first_tangent)
    tangent_two = pick_component(mapped, second_tangent)
    offset_one = ((first_pos % 2).astype(fine_face.dtype) - 0.5) * 0.5
    offset_two = ((second_pos % 2).astype(fine_face.dtype) - 0.5) * 0.5
    speed = sign * 0.5 * (fine_face[:, 4] + mapped[:, 4])
    depth = jnp.abs(speed) * time_step
    outflow = jnp.maximum(speed, 0.0)
    inflow = jnp.minimum(speed, 0.0)
    volume = jnp.zeros_like(speed)
    moment = jnp.zeros_like(speed)
    for node in (0.5 - 3.0 ** 0.5 / 6.0, 0.5 + 3.0 ** 0.5 / 6.0):
        fine_phase = normal_fine * (sign * (0.5 - node * depth)) + fine_face[:, 3]
        coarse_phase = normal_coarse * (-sign * (0.5 - 0.5 * node * depth)) + tangent_one * offset_one + tangent_two * offset_two + mapped[:, 3]
        fine_model = 0.5 * (1.0 + jnp.tanh(fine_phase))
        coarse_model = 0.5 * (1.0 + jnp.tanh(coarse_phase))
        volume = volume + 0.5 * time_step * (outflow * fine_model + inflow * coarse_model)
        moment = moment + 0.5 * time_step * node * depth * sign * (inflow * coarse_model - outflow * fine_model)
    weight = live.astype(fine_face.dtype)[:, None]
    return (jnp.stack([volume * weight, moment * weight], axis=1), coarse_cell)

def fit_group(group):
    center, ghosts = group
    return fit_planes(center, neighbour_fields(center, ghosts))

def reference(fraction, centroid, velocity, neighbours, refinement):
    own = jnp.concatenate([fraction[:, None], centroid], 1)
    own_faces = faces_of(own)
    opposite = opposite_of(jnp.arange(6, dtype=jnp.int32))
    safe = jnp.clip(neighbours, 0, NB - 1)
    ghost = jnp.where((neighbours >= 0)[:, :, None, None], own_faces[safe, opposite[None, :]], own_faces)
    grouped = lax.map(fit_group, (own.reshape(N_SFC, BLK, 4, CELLS), ghost.reshape(N_SFC, BLK, 6, 4, FACE)))
    planes = grouped.reshape(NB, 4, CELLS)
    plane_faces = build_plane_faces(planes, velocity)
    fine = refinement[:, 0]
    live = fine >= 0
    direction = refinement[:, 1]
    coarse = refinement[:, 2]
    quadrant = refinement[:, 3]
    fine_face = plane_faces[jnp.clip(fine, 0, NB - 1), direction]
    coarse_face = plane_faces[coarse, opposite_of(direction)]
    moments, coarse_cell = slot_moments(fine_face, coarse_face, direction, quadrant, live)
    target = (coarse * 6 + opposite_of(direction))[:, None] * FACE + coarse_cell
    flat = jnp.zeros((NB * 6 * FACE, 2), jnp.float32).at[target.reshape(-1)].add(jnp.swapaxes(moments, 1, 2).reshape(-1, 2))
    reflux = jnp.swapaxes(flat.reshape(NB, 6, FACE, 2), 2, 3)
    return (planes, reflux)
```

```python
import jax
import jax.numpy as jnp
from jax import lax
from jax.experimental import pallas as pl
from jax.experimental.pallas import tpu as pltpu
from jax.sharding import PartitionSpec as P

EDGE = 16
CELLS = 4096
REACH = 2
PASSES = 6
BLK = 8
NODES = (0.5 - 3.0**0.5 / 6.0, 0.5 + 3.0**0.5 / 6.0)
TIME_STEP = 0.25
DAMPING = 0.1
SHIFTS = (1, -1, 2, -2)
VEC = (8, 128)
ITEMS = 6
BLOCK_ROWS = ITEMS * 8
FINE_ROWS = 5 * 2 * 8
COARSE_ROWS = 5 * 2 * 2 * 16


def lanes():
    return lax.broadcasted_iota(jnp.int32, VEC, 1)


def take(values, index):
    return jnp.take_along_axis(values, index, axis=1, mode="promise_in_bounds")


def edge_index(swap):
    lane = lanes()
    kind = lane // 32
    if swap:
        kind = kind + 1 - 2 * (kind % 2)
    j = lane % 16
    source = jnp.where(
        kind == 0, j, jnp.where(kind == 1, 112 + j, (j % 8) * 16 + jnp.where(kind == 3, 15, 0))
    )
    upper = jnp.where(kind == 0, 0, jnp.where(kind == 1, 1, j // 8))
    return source, upper == 1, (lane // 16) % 2 == 1


def edges(tiles, index):
    source, upper, odd = index
    first = jnp.where(upper, take(tiles[1], source), take(tiles[0], source))
    second = jnp.where(upper, take(tiles[3], source), take(tiles[2], source))
    return jnp.where(odd, second, first)


def field_rows(fraction_ref, centroid_ref, field, start, size):
    if field == 0:
        return fraction_ref[:, pl.ds(start, size)]
    return centroid_ref[field - 1, :, pl.ds(start, size)]


def greet(count, me):
    barrier = pltpu.get_barrier_semaphore()
    for shift in SHIFTS:
        other = me + shift

        @pl.when((other >= 0) & (other < count))
        def _signal():
            pl.semaphore_signal(
                barrier, inc=1, device_id=(other,), device_id_type=pl.DeviceIdType.MESH
            )

    peers = sum(
        ((me + shift >= 0) & (me + shift < count)).astype(jnp.int32) for shift in SHIFTS
    )
    pl.semaphore_wait(barrier, peers)


def each_neighbour(count, me, action):
    for place, shift in enumerate(SHIFTS):
        other = me + shift

        @pl.when((other >= 0) & (other < count))
        def _act():
            action(place, shift, other)


def remote(src, dst, send, recv, other):
    return pltpu.make_async_remote_copy(
        src_ref=src,
        dst_ref=dst,
        send_sem=send,
        recv_sem=recv,
        device_id=(other,),
        device_id_type=pl.DeviceIdType.MESH,
    )


def faces_kernel(
    count, fraction_ref, centroid_ref, refine_ref, near_ref, table_ref, send, recv, send2, recv2
):
    me = lax.axis_index("sfc")
    near_own = REACH
    swapped = edge_index(True)
    plain = edge_index(False)

    def extract(slot, index, swap):
        for field in range(4):
            for pair in range(8):
                chunk = field_rows(fraction_ref, centroid_ref, field, pair * 512, 512)
                tiles = [chunk[:, 128 * t : 128 * t + 128] for t in range(4)]
                near_ref[slot, pl.ds(field * 8 + pair, 8, stride=BLOCK_ROWS), :] = edges(
                    tiles, index
                )
            for side in range(2):
                start = (1 - side if swap else side) * 3840
                for half in range(2):
                    near_ref[
                        slot, pl.ds(32 + half * 8 + side * 4 + field, 8, stride=BLOCK_ROWS), :
                    ] = field_rows(fraction_ref, centroid_ref, field, start + half * 128, 128)

    extract(near_own, swapped, True)
    table_ref[near_own] = refine_ref[...]
    greet(count, me)

    def start(place, shift, other):
        remote(
            near_ref.at[near_own], near_ref.at[REACH - shift], send.at[place], recv.at[place], other
        ).start()
        remote(
            refine_ref, table_ref.at[REACH - shift], send2.at[place], recv2.at[place], other
        ).start()

    each_neighbour(count, me, start)
    extract(2 * REACH + 1, plain, False)

    def finish_send(place, shift, other):
        remote(
            near_ref.at[near_own], near_ref.at[REACH - shift], send.at[place], recv.at[place], other
        ).wait_send()
        remote(
            refine_ref, table_ref.at[REACH - shift], send2.at[place], recv2.at[place], other
        ).wait_send()

    def finish_recv(place, shift, other):
        remote(
            near_ref.at[near_own], near_ref.at[REACH - shift], send.at[place], recv.at[place], other
        ).wait_recv()
        remote(
            refine_ref, table_ref.at[REACH - shift], send2.at[place], recv2.at[place], other
        ).wait_recv()

    each_neighbour(count, me, finish_send)
    for place, shift in enumerate(SHIFTS):
        other = me - shift

        @pl.when((other >= 0) & (other < count))
        def _recv():
            finish_recv(place, shift, other)


def packets_kernel(count, own_ref, near_ref, send, recv):
    me = lax.axis_index("sfc")
    greet(count, me)
    near_ref[REACH] = own_ref[...]

    def start(place, shift, other):
        remote(own_ref, near_ref.at[REACH - shift], send.at[place], recv.at[place], other).start()

    each_neighbour(count, me, start)

    def finish_send(place, shift, other):
        remote(
            own_ref, near_ref.at[REACH - shift], send.at[place], recv.at[place], other
        ).wait_send()

    each_neighbour(count, me, finish_send)
    for place, shift in enumerate(SHIFTS):
        other = me - shift

        @pl.when((other >= 0) & (other < count))
        def _recv():
            remote(
                own_ref, near_ref.at[REACH - shift], send.at[place], recv.at[place], other
            ).wait_recv()


def solve(h, g):
    (h00, h01, h02, h03, h11, h12, h13, h22, h23, h33) = h
    i0 = 1.0 / h00
    l10, l20, l30 = h01 * i0, h02 * i0, h03 * i0
    d1 = h11 - l10 * h01
    a21, a31 = h12 - l10 * h02, h13 - l10 * h03
    i1 = 1.0 / d1
    l21, l31 = a21 * i1, a31 * i1
    d2 = h22 - l20 * h02 - l21 * a21
    a32 = h23 - l20 * h03 - l21 * a31
    i2 = 1.0 / d2
    l32 = a32 * i2
    d3 = h33 - l30 * h03 - l31 * a31 - l32 * a32
    y1 = g[1] - l10 * g[0]
    y2 = g[2] - l20 * g[0] - l21 * y1
    y3 = g[3] - l30 * g[0] - l31 * y1 - l32 * y2
    x3 = y3 / d3
    x2 = y2 * i2 - l32 * x3
    x1 = y1 * i1 - l21 * x2 - l31 * x3
    x0 = g[0] * i0 - l10 * x1 - l20 * x2 - l30 * x3
    return x0, x1, x2, x3


def fit(points, params):
    def one_pass(_unused, params):
        a, b, c, d = params
        h = [None] * 10
        g = [None] * 4

        def add(total, place, term):
            total[place] = term if total[place] is None else total[place] + term

        for px, py, pz, f in points:
            t = jnp.tanh(a * px + b * py + c * pz + d)
            s = 1.0 - t * t
            q = s * s
            w = s * (t - f)
            qx, qy, qz = q * px, q * py, q * pz
            for place, term in enumerate(
                (qx * px, qx * py, qx * pz, qx, qy * py, qy * pz, qy, qz * pz, qz, q)
            ):
                add(h, place, term)
            for place, term in enumerate((w * px, w * py, w * pz, w)):
                add(g, place, term)
        for place in (0, 4, 7, 9):
            h[place] = h[place] + 4.0 * DAMPING
        step = solve(h, g)
        return tuple(p - s for p, s in zip(params, step))

    return lax.fori_loop(0, PASSES, one_pass, params)


def fit_kernel(
    fraction_ref,
    centroid_ref,
    velocity_ref,
    near_ref,
    neighbours_ref,
    refine_ref,
    planes_ref,
    comps_ref,
    packets_ref,
    padded,
    ghost_edges,
    ghost_layers,
    fine_table,
):
    me = lax.axis_index("sfc")
    lane = lanes()
    row = lax.broadcasted_iota(jnp.int32, VEC, 0)
    first_block = (me - REACH) * BLK

    for block in range(BLK):
        place = []
        for k in range(6):
            other = neighbours_ref[block, k]
            place.append(
                jnp.where(
                    other >= 0,
                    jnp.clip(other - first_block, 0, (2 * REACH + 1) * BLK - 1),
                    (2 * REACH + 1) * BLK + block,
                )
            )
        for field in range(4):
            value = near_ref[place[5], field]
            for k in (4, 3, 2):
                value = jnp.where(lane < (k - 1) * 32, near_ref[place[k], field], value)
            ghost_edges[block * 32 + field * 8 : block * 32 + field * 8 + 8, :] = value
        for half in range(2):
            ghost_layers[half, block * 8 : block * 8 + 8, :] = jnp.where(
                row < 4, near_ref[place[0], 4 + half], near_ref[place[1], 4 + half]
            )

    for field in range(4):
        for half in range(2):
            for side in range(2):
                start = side * 4352 + half * 128
                padded[field, :, start : start + 128] = ghost_layers[
                    half, pl.ds(side * 4 + field, 8, stride=8), :
                ]
        padded[field, :, 256:4352] = field_rows(fraction_ref, centroid_ref, field, 0, CELLS)

    wide = lax.broadcasted_iota(jnp.int32, (8, 512), 1)
    y_pos = wide // 16 % 16
    z_pos = wide % 16
    plain = edge_index(False)
    y_source, z_source = [], []
    for tile in range(4):
        odd, upper = tile // 2, tile % 2
        y_source.append(upper * 32 + odd * 16 + lane % 16)
        z_source.append(
            jnp.where(lane % 16 < 8, 64, 96) + odd * 16 + upper * 8 + lane // 16
        )

    def one_pair(pair, carry):
        start = pl.multiple_of(pair * 512, 512)
        fields = [[] for _unused in range(7)]
        for field in range(4):
            center = padded[field, :, pl.ds(start + 256, 512)]
            ghost = ghost_edges[pl.ds(field * 8 + pair, 8, stride=32), :]
            ghost_y = jnp.concatenate([take(ghost, i) for i in y_source], 1)
            ghost_z = jnp.concatenate([take(ghost, i) for i in z_source], 1)
            fields[0].append(center)
            fields[1].append(padded[field, :, pl.ds(start, 512)])
            fields[2].append(padded[field, :, pl.ds(start + 512, 512)])
            fields[3].append(jnp.where(y_pos == 0, ghost_y, pltpu.roll(center, 16, 1)))
            fields[4].append(jnp.where(y_pos == 15, ghost_y, pltpu.roll(center, 496, 1)))
            fields[5].append(jnp.where(z_pos == 0, ghost_z, pltpu.roll(center, 1, 1)))
            fields[6].append(jnp.where(z_pos == 15, ghost_z, pltpu.roll(center, 511, 1)))
        a, b, c = [2.0 * (fields[2 + 2 * i][0] - fields[1 + 2 * i][0]) for i in range(3)]
        frac, cx, cy, cz = fields[0]
        d = 2.0 * (2.0 * frac - 1.0) - a * cx - b * cy - c * cz
        points = [(cx, cy, cz, 2.0 * frac - 1.0)]
        for k in range(6):
            f, *coords = fields[k + 1]
            coords[k // 2] = coords[k // 2] + (2.0 * (k % 2) - 1.0)
            points.append((*coords, 2.0 * f - 1.0))
        params = fit(points, (a, b, c, d))
        for comp in range(4):
            planes_ref[:, comp, pl.ds(start, 512)] = params[comp]
            comps_ref[comp, :, pl.ds(start, 512)] = params[comp]
            tiles = [params[comp][:, 128 * t : 128 * t + 128] for t in range(4)]
            fine_table[pl.ds(comp * 16 + 8 + pair, 8, stride=FINE_ROWS), :] = edges(tiles, plain)
        speeds = []
        for axis in (1, 2):
            chunk = velocity_ref[axis, :, pl.ds(start, 512)]
            speeds.append(edges([chunk[:, 128 * t : 128 * t + 128] for t in range(4)], plain))
        fine_table[pl.ds(4 * 16 + 8 + pair, 8, stride=FINE_ROWS), :] = jnp.where(
            lane < 64, speeds[0], speeds[1]
        )
        return carry

    lax.fori_loop(0, 8, one_pair, 0)

    for comp in range(5):
        for half in range(2):
            sides = []
            for side in range(2):
                start = side * 3840 + half * 128
                if comp < 4:
                    sides.append(comps_ref[comp, :, start : start + 128])
                else:
                    sides.append(velocity_ref[0, :, start : start + 128])
            for part in range(4):
                low = sides[0] if part == 0 else pltpu.roll(sides[0], 128 - 32 * part, 1)
                high = sides[1] if part == 1 else pltpu.roll(sides[1], (160 - 32 * part) % 128, 1)
                fine_table[pl.ds(comp * 16 + half * 4 + part, 8, stride=FINE_ROWS), :] = jnp.where(
                    lane < 32, low, high
                )

    for slot in range(refine_ref.shape[0]):
        block = jnp.clip(refine_ref[slot, 0] - me * BLK, 0, BLK - 1)
        k = jnp.clip(refine_ref[slot, 1], 0, 5)
        yz = (k >= 2).astype(jnp.int32)
        base = block * FINE_ROWS + yz * 8
        group = k - 2 * yz
        parts = []
        for target, comp in enumerate((k // 2, 3, 4)):
            value = fine_table[pl.ds(pl.multiple_of(base + comp * 16, 8), 8), :]
            parts.append(pltpu.roll(value, (128 + 32 * target - 32 * group) % 128, 1))
        packets_ref[slot] = jnp.where(
            lane < 32, parts[0], jnp.where(lane < 64, parts[1], parts[2])
        )


def flux_kernel(
    comps_ref, velocity_ref, packets_ref, table_ref, reflux_ref, coarse_table, sums, live_list
):
    me = lax.axis_index("sfc")
    lane = lanes()
    kind = lane // 32
    pos = lane % 32
    cell = pos % 16 // 2
    slots = packets_ref.shape[1]
    total = packets_ref.shape[0] * slots

    def collect(item, found):
        offset = item // slots
        slot = item % slots
        coarse = table_ref[offset, slot, 2]
        other = me + offset - REACH
        there = (other >= 0) & (other < lax.axis_size("sfc"))
        mine = there & (table_ref[offset, slot, 0] >= 0) & (coarse >= 0) & (coarse // BLK == me)

        @pl.when(mine)
        def _keep():
            live_list[found] = item

        return found + mine.astype(jnp.int32)

    found = lax.fori_loop(0, total, collect, 0)
    for extra in range(3):
        live_list[found + extra] = REACH * slots

    sums[...] = jnp.zeros_like(sums)

    def build(x, carry):
        start = pl.multiple_of(x * 256, 256)
        x_tile = pl.multiple_of(x // 8 * 128, 128)
        for qb in range(2):
            source = jnp.where(
                kind == 0,
                qb * 8 + cell,
                jnp.where(kind == 1, 112 + qb * 8 + cell, cell * 16 + jnp.where(kind == 3, 15, 0)),
            )
            upper = jnp.where(kind == 0, 0, jnp.where(kind == 1, 1, qb)) == 1
            layer_source = x % 8 * 16 + qb * 8 + cell
            for comp in range(5):
                if comp < 4:
                    value = jnp.where(
                        upper,
                        take(comps_ref[comp, :, pl.ds(start + 128, 128)], source),
                        take(comps_ref[comp, :, pl.ds(start, 128)], source),
                    )
                    low = comps_ref[comp, :, pl.ds(x_tile, 128)]
                    high = comps_ref[comp, :, pl.ds(x_tile + 3840, 128)]
                else:
                    by_axis = [
                        jnp.where(
                            upper,
                            take(velocity_ref[axis, :, pl.ds(start + 128, 128)], source),
                            take(velocity_ref[axis, :, pl.ds(start, 128)], source),
                        )
                        for axis in (1, 2)
                    ]
                    value = jnp.where(lane < 64, by_axis[0], by_axis[1])
                    low = velocity_ref[0, :, pl.ds(x_tile, 128)]
                    high = velocity_ref[0, :, pl.ds(x_tile + 3840, 128)]
                layer = jnp.where(lane < 32, take(low, layer_source), take(high, layer_source))
                base = comp * 64 + qb * 16
                coarse_table[pl.ds(base + x, 8, stride=COARSE_ROWS), :] = layer
                coarse_table[pl.ds(base + 32 + x, 8, stride=COARSE_ROWS), :] = value
        return carry

    lax.fori_loop(0, 16, build, 0)

    offset_one = ((pos // 16).astype(jnp.float32) - 0.5) * 0.5
    offset_two = ((pos % 2).astype(jnp.float32) - 0.5) * 0.5

    def moments(item, weight):
        offset = item // slots
        slot = item % slots
        k = jnp.clip(table_ref[offset, slot, 1], 0, 5)
        block = jnp.clip(table_ref[offset, slot, 2] - me * BLK, 0, BLK - 1)
        quadrant = jnp.clip(table_ref[offset, slot, 3], 0, 3)
        qa, qb = quadrant // 2, quadrant % 2
        facing = k + 1 - 2 * (k % 2)
        axis = k // 2
        sign = (2 * (k % 2) - 1).astype(jnp.float32)
        yz = (k >= 2).astype(jnp.int32)
        shift = (128 - 32 * (facing - 2 * yz)) % 128
        base = block * COARSE_ROWS + yz * 32 + qb * 16 + qa * 8
        first = jnp.where(axis == 0, 1, 0)
        second = jnp.where(axis == 2, 1, 2)
        normal_c, one_c, two_c, d_c, u_c = [
            pltpu.roll(
                coarse_table[pl.ds(pl.multiple_of(base + comp * 64, 8), 8), :], shift, 1
            )
            for comp in (axis, first, second, 3, 4)
        ]
        packet = packets_ref[offset, slot]
        normal_f = packet
        d_f = pltpu.roll(packet, 96, 1)
        u_f = pltpu.roll(packet, 64, 1)
        speed = sign * 0.5 * (u_f + u_c)
        depth = jnp.abs(speed) * TIME_STEP
        outflow = jnp.maximum(speed, 0.0)
        inflow = jnp.minimum(speed, 0.0)
        tangent = one_c * offset_one + two_c * offset_two + d_c
        volume = jnp.zeros(VEC, jnp.float32)
        moment = jnp.zeros(VEC, jnp.float32)
        for node in NODES:
            fine_model = 0.5 * (
                1.0 + jnp.tanh(normal_f * (sign * (0.5 - node * depth)) + d_f)
            )
            coarse_model = 0.5 * (
                1.0 + jnp.tanh(normal_c * (-sign * (0.5 - 0.5 * node * depth)) + tangent)
            )
            volume = volume + 0.5 * TIME_STEP * (outflow * fine_model + inflow * coarse_model)
            moment = moment + 0.5 * TIME_STEP * node * depth * sign * (
                inflow * coarse_model - outflow * fine_model
            )
        both = jnp.where(
            lane < 32, volume, jnp.where((lane >= 64) & (lane < 96), pltpu.roll(moment, 64, 1), 0.0)
        )
        both = jnp.where(weight, both, 0.0)
        target = pl.multiple_of((block * 6 + facing) * 16 + qa * 8, 8)
        return pltpu.roll(both, 32 * qb, 1), target

    def group(number, carry):
        results = [
            moments(live_list[number * 4 + i], number * 4 + i < found) for i in range(4)
        ]
        for value, target in results:
            sums[pl.ds(target, 8), :] += value
        return carry

    lax.fori_loop(0, (found + 3) // 4, group, 0)

    j = lane % 16
    for tile in range(6):
        outs = [[jnp.zeros(VEC, jnp.float32)] * 2 for _unused in range(2)]
        for i in range(16):
            value = sums[pl.ds(tile * 128 + i, 8, stride=16), :]
            value = value + pltpu.roll(value, 127, 1)
            value = value + pltpu.roll(value, 112, 1)
            for m in range(2):
                placed = take(value, m * 64 + j // 8 * 32 + 2 * (j % 8))
                outs[m][i // 8] = jnp.where(lane // 16 == i % 8, placed, outs[m][i // 8])
        for m in range(2):
            for half in range(2):
                start = m * 256 + half * 128
                reflux_ref[tile * 8 : tile * 8 + 8, start : start + 128] = outs[m][half]


def spec(space):
    return pl.BlockSpec(memory_space=space)


def per_device(fraction, centroid, velocity, neighbours, refinement):
    count = lax.axis_size("sfc")
    slots = refinement.shape[0]
    vmem, smem = spec(pltpu.VMEM), spec(pltpu.SMEM)
    f32 = jnp.float32
    centroid, velocity = jnp.swapaxes(centroid, 0, 1), jnp.swapaxes(velocity, 0, 1)
    near, table = pl.pallas_call(
        lambda *refs: faces_kernel(count, *refs),
        out_shape=(
            jax.ShapeDtypeStruct((6, BLK * BLOCK_ROWS, 128), f32),
            jax.ShapeDtypeStruct((5, slots, 4), jnp.int32),
        ),
        in_specs=[vmem] * 3,
        out_specs=(vmem, vmem),
        scratch_shapes=[pltpu.SemaphoreType.DMA((4,))] * 4,
        compiler_params=pltpu.CompilerParams(collective_id=0, has_side_effects=True),
        name="exchange_faces",
    )(fraction, centroid, refinement)
    planes, comps, packets = pl.pallas_call(
        fit_kernel,
        out_shape=(
            jax.ShapeDtypeStruct((BLK, 4, CELLS), f32),
            jax.ShapeDtypeStruct((4, BLK, CELLS), f32),
            jax.ShapeDtypeStruct((slots, 8, 128), f32),
        ),
        in_specs=[vmem] * 4 + [smem] * 2,
        out_specs=(vmem,) * 3,
        scratch_shapes=[
            pltpu.VMEM((4, 8, CELLS + 512), f32),
            pltpu.VMEM((256, 128), f32),
            pltpu.VMEM((2, 64, 128), f32),
            pltpu.VMEM((BLK * FINE_ROWS, 128), f32),
        ],
        name="fit_planes",
    )(fraction, centroid, velocity, near.reshape(48, ITEMS, 8, 128), neighbours, refinement)
    near_packets = pl.pallas_call(
        lambda *refs: packets_kernel(count, *refs),
        out_shape=jax.ShapeDtypeStruct((5, slots, 8, 128), f32),
        in_specs=[vmem],
        out_specs=vmem,
        scratch_shapes=[pltpu.SemaphoreType.DMA((4,))] * 2,
        compiler_params=pltpu.CompilerParams(collective_id=1, has_side_effects=True),
        name="exchange_packets",
    )(packets)
    reflux = pl.pallas_call(
        flux_kernel,
        out_shape=jax.ShapeDtypeStruct((BLK * 6, 512), f32),
        in_specs=[vmem] * 3 + [smem],
        out_specs=vmem,
        scratch_shapes=[
            pltpu.VMEM((BLK * COARSE_ROWS, 128), f32),
            pltpu.VMEM((BLK * 6 * 16, 128), f32),
            pltpu.SMEM((5 * slots + 4,), jnp.int32),
        ],
        name="reflux_moments",
    )(comps, velocity, near_packets, table)
    return planes, reflux.reshape(BLK, 6, 2, 256)


def solution(mesh):
    return jax.shard_map(
        per_device,
        mesh=mesh,
        in_specs=(
            P("sfc", None),
            P("sfc", None, None),
            P("sfc", None, None),
            P("sfc", None),
            P("sfc", None),
        ),
        out_specs=(P("sfc", None, None), P("sfc", None, None, None)),
        check_vma=False,
    )
```

```python
import jax
import jax.numpy as jnp
from jax import lax
from jax.experimental import pallas as pl
from jax.experimental.pallas import tpu as pltpu
from jax.sharding import PartitionSpec as P

EDGE = 16
CELLS = 4096
REACH = 2
PASSES = 6
BLK = 8
NODES = (0.5 - 3.0**0.5 / 6.0, 0.5 + 3.0**0.5 / 6.0)
TIME_STEP = 0.25
DAMPING = 0.1
SHIFTS = (1, -1, 2, -2)
VEC = (8, 128)
ITEMS = 6
BLOCK_ROWS = ITEMS * 8
FINE_ROWS = 5 * 2 * 8


def lanes():
    return lax.broadcasted_iota(jnp.int32, VEC, 1)


def take(values, index):
    return jnp.take_along_axis(values, index, axis=1, mode="promise_in_bounds")


def edge_index(swap):
    lane = lanes()
    kind = lane // 32
    if swap:
        kind = kind + 1 - 2 * (kind % 2)
    j = lane % 16
    source = jnp.where(
        kind == 0, j, jnp.where(kind == 1, 112 + j, (j % 8) * 16 + jnp.where(kind == 3, 15, 0))
    )
    upper = jnp.where(kind == 0, 0, jnp.where(kind == 1, 1, j // 8))
    return source, upper == 1, (lane // 16) % 2 == 1


def edges(tiles, index):
    source, upper, odd = index
    first = jnp.where(upper, take(tiles[1], source), take(tiles[0], source))
    second = jnp.where(upper, take(tiles[3], source), take(tiles[2], source))
    return jnp.where(odd, second, first)


def field_rows(fraction_ref, centroid_ref, field, start, size):
    if field == 0:
        return fraction_ref[:, pl.ds(start, size)]
    return centroid_ref[field - 1, :, pl.ds(start, size)]


def greet(count, me):
    barrier = pltpu.get_barrier_semaphore()
    for shift in SHIFTS:
        other = me + shift

        @pl.when((other >= 0) & (other < count))
        def _signal():
            pl.semaphore_signal(
                barrier, inc=1, device_id=(other,), device_id_type=pl.DeviceIdType.MESH
            )

    peers = sum(
        ((me + shift >= 0) & (me + shift < count)).astype(jnp.int32) for shift in SHIFTS
    )
    pl.semaphore_wait(barrier, peers)


def each_neighbour(count, me, action):
    for place, shift in enumerate(SHIFTS):
        other = me + shift

        @pl.when((other >= 0) & (other < count))
        def _act():
            action(place, shift, other)


def remote(src, dst, send, recv, other):
    return pltpu.make_async_remote_copy(
        src_ref=src,
        dst_ref=dst,
        send_sem=send,
        recv_sem=recv,
        device_id=(other,),
        device_id_type=pl.DeviceIdType.MESH,
    )


def faces_kernel(
    count, fraction_ref, centroid_ref, refine_ref, near_ref, table_ref, send, recv, send2, recv2
):
    me = lax.axis_index("sfc")
    near_own = REACH
    swapped = edge_index(True)
    plain = edge_index(False)

    def extract(slot, index, swap):
        for field in range(4):
            for pair in range(8):
                chunk = field_rows(fraction_ref, centroid_ref, field, pair * 512, 512)
                tiles = [chunk[:, 128 * t : 128 * t + 128] for t in range(4)]
                near_ref[slot, pl.ds(field * 8 + pair, 8, stride=BLOCK_ROWS), :] = edges(
                    tiles, index
                )
            for side in range(2):
                start = (1 - side if swap else side) * 3840
                for half in range(2):
                    near_ref[
                        slot, pl.ds(32 + half * 8 + side * 4 + field, 8, stride=BLOCK_ROWS), :
                    ] = field_rows(fraction_ref, centroid_ref, field, start + half * 128, 128)

    extract(near_own, swapped, True)
    table_ref[near_own] = refine_ref[...]
    greet(count, me)

    def start(place, shift, other):
        remote(
            near_ref.at[near_own], near_ref.at[REACH - shift], send.at[place], recv.at[place], other
        ).start()
        remote(
            refine_ref, table_ref.at[REACH - shift], send2.at[place], recv2.at[place], other
        ).start()

    each_neighbour(count, me, start)
    extract(2 * REACH + 1, plain, False)

    def finish_send(place, shift, other):
        remote(
            near_ref.at[near_own], near_ref.at[REACH - shift], send.at[place], recv.at[place], other
        ).wait_send()
        remote(
            refine_ref, table_ref.at[REACH - shift], send2.at[place], recv2.at[place], other
        ).wait_send()

    def finish_recv(place, shift, other):
        remote(
            near_ref.at[near_own], near_ref.at[REACH - shift], send.at[place], recv.at[place], other
        ).wait_recv()
        remote(
            refine_ref, table_ref.at[REACH - shift], send2.at[place], recv2.at[place], other
        ).wait_recv()

    each_neighbour(count, me, finish_send)
    for place, shift in enumerate(SHIFTS):
        other = me - shift

        @pl.when((other >= 0) & (other < count))
        def _recv():
            finish_recv(place, shift, other)


def packets_kernel(count, own_ref, near_ref, send, recv):
    me = lax.axis_index("sfc")
    greet(count, me)
    near_ref[REACH] = own_ref[...]

    def start(place, shift, other):
        remote(own_ref, near_ref.at[REACH - shift], send.at[place], recv.at[place], other).start()

    each_neighbour(count, me, start)

    def finish_send(place, shift, other):
        remote(
            own_ref, near_ref.at[REACH - shift], send.at[place], recv.at[place], other
        ).wait_send()

    each_neighbour(count, me, finish_send)
    for place, shift in enumerate(SHIFTS):
        other = me - shift

        @pl.when((other >= 0) & (other < count))
        def _recv():
            remote(
                own_ref, near_ref.at[REACH - shift], send.at[place], recv.at[place], other
            ).wait_recv()


def solve(h, g):
    (h00, h01, h02, h03, h11, h12, h13, h22, h23, h33) = h
    i0 = 1.0 / h00
    l10, l20, l30 = h01 * i0, h02 * i0, h03 * i0
    d1 = h11 - l10 * h01
    a21, a31 = h12 - l10 * h02, h13 - l10 * h03
    i1 = 1.0 / d1
    l21, l31 = a21 * i1, a31 * i1
    d2 = h22 - l20 * h02 - l21 * a21
    a32 = h23 - l20 * h03 - l21 * a31
    i2 = 1.0 / d2
    l32 = a32 * i2
    d3 = h33 - l30 * h03 - l31 * a31 - l32 * a32
    y1 = g[1] - l10 * g[0]
    y2 = g[2] - l20 * g[0] - l21 * y1
    y3 = g[3] - l30 * g[0] - l31 * y1 - l32 * y2
    x3 = y3 / d3
    x2 = y2 * i2 - l32 * x3
    x1 = y1 * i1 - l21 * x2 - l31 * x3
    x0 = g[0] * i0 - l10 * x1 - l20 * x2 - l30 * x3
    return x0, x1, x2, x3


def fit(points, params):
    def one_pass(_unused, params):
        a, b, c, d = params
        h = [None] * 10
        g = [None] * 4

        def add(total, place, term):
            total[place] = term if total[place] is None else total[place] + term

        for px, py, pz, f in points:
            t = jnp.tanh(a * px + b * py + c * pz + d)
            s = 1.0 - t * t
            q = s * s
            w = s * (t - f)
            qx, qy, qz = q * px, q * py, q * pz
            for place, term in enumerate(
                (qx * px, qx * py, qx * pz, qx, qy * py, qy * pz, qy, qz * pz, qz, q)
            ):
                add(h, place, term)
            for place, term in enumerate((w * px, w * py, w * pz, w)):
                add(g, place, term)
        for place in (0, 4, 7, 9):
            h[place] = h[place] + 4.0 * DAMPING
        step = solve(h, g)
        return tuple(p - s for p, s in zip(params, step))

    return lax.fori_loop(0, PASSES, one_pass, params)


def fit_kernel(
    fraction_ref,
    centroid_ref,
    velocity_ref,
    near_ref,
    neighbours_ref,
    refine_ref,
    planes_ref,
    fine_table,
    packets_ref,
    padded,
    ghost_edges,
    ghost_layers,
):
    me = lax.axis_index("sfc")
    lane = lanes()
    row = lax.broadcasted_iota(jnp.int32, VEC, 0)
    first_block = (me - REACH) * BLK

    for block in range(BLK):
        place = []
        for k in range(6):
            other = neighbours_ref[block, k]
            place.append(
                jnp.where(
                    other >= 0,
                    jnp.clip(other - first_block, 0, (2 * REACH + 1) * BLK - 1),
                    (2 * REACH + 1) * BLK + block,
                )
            )
        for field in range(4):
            value = near_ref[place[5], field]
            for k in (4, 3, 2):
                value = jnp.where(lane < (k - 1) * 32, near_ref[place[k], field], value)
            ghost_edges[block * 32 + field * 8 : block * 32 + field * 8 + 8, :] = value
        for half in range(2):
            ghost_layers[half, block * 8 : block * 8 + 8, :] = jnp.where(
                row < 4, near_ref[place[0], 4 + half], near_ref[place[1], 4 + half]
            )

    for field in range(4):
        for half in range(2):
            for side in range(2):
                start = side * 4352 + half * 128
                padded[field, :, start : start + 128] = ghost_layers[
                    half, pl.ds(side * 4 + field, 8, stride=8), :
                ]
        padded[field, :, 256:4352] = field_rows(fraction_ref, centroid_ref, field, 0, CELLS)

    wide = lax.broadcasted_iota(jnp.int32, (8, 512), 1)
    y_pos = wide // 16 % 16
    z_pos = wide % 16
    plain = edge_index(False)
    y_source, z_source = [], []
    for tile in range(4):
        odd, upper = tile // 2, tile % 2
        y_source.append(upper * 32 + odd * 16 + lane % 16)
        z_source.append(
            jnp.where(lane % 16 < 8, 64, 96) + odd * 16 + upper * 8 + lane // 16
        )

    def one_pair(pair, carry):
        start = pl.multiple_of(pair * 512, 512)
        fields = [[] for _unused in range(7)]
        for field in range(4):
            center = padded[field, :, pl.ds(start + 256, 512)]
            ghost = ghost_edges[pl.ds(field * 8 + pair, 8, stride=32), :]
            ghost_y = jnp.concatenate([take(ghost, i) for i in y_source], 1)
            ghost_z = jnp.concatenate([take(ghost, i) for i in z_source], 1)
            fields[0].append(center)
            fields[1].append(padded[field, :, pl.ds(start, 512)])
            fields[2].append(padded[field, :, pl.ds(start + 512, 512)])
            fields[3].append(jnp.where(y_pos == 0, ghost_y, pltpu.roll(center, 16, 1)))
            fields[4].append(jnp.where(y_pos == 15, ghost_y, pltpu.roll(center, 496, 1)))
            fields[5].append(jnp.where(z_pos == 0, ghost_z, pltpu.roll(center, 1, 1)))
            fields[6].append(jnp.where(z_pos == 15, ghost_z, pltpu.roll(center, 511, 1)))
        a, b, c = [2.0 * (fields[2 + 2 * i][0] - fields[1 + 2 * i][0]) for i in range(3)]
        frac, cx, cy, cz = fields[0]
        d = 2.0 * (2.0 * frac - 1.0) - a * cx - b * cy - c * cz
        points = [(cx, cy, cz, 2.0 * frac - 1.0)]
        for k in range(6):
            f, *coords = fields[k + 1]
            coords[k // 2] = coords[k // 2] + (2.0 * (k % 2) - 1.0)
            points.append((*coords, 2.0 * f - 1.0))
        params = fit(points, (a, b, c, d))
        for comp in range(4):
            planes_ref[:, comp, pl.ds(start, 512)] = params[comp]
            tiles = [params[comp][:, 128 * t : 128 * t + 128] for t in range(4)]
            fine_table[pl.ds(comp * 16 + 8 + pair, 8, stride=FINE_ROWS), :] = edges(tiles, plain)
        speeds = []
        for axis in (1, 2):
            chunk = velocity_ref[axis, :, pl.ds(start, 512)]
            speeds.append(edges([chunk[:, 128 * t : 128 * t + 128] for t in range(4)], plain))
        fine_table[pl.ds(4 * 16 + 8 + pair, 8, stride=FINE_ROWS), :] = jnp.where(
            lane < 64, speeds[0], speeds[1]
        )
        return carry

    lax.fori_loop(0, 8, one_pair, 0)

    for comp in range(5):
        for half in range(2):
            sides = []
            for side in range(2):
                start = side * 3840 + half * 128
                if comp < 4:
                    sides.append(planes_ref[:, comp, start : start + 128])
                else:
                    sides.append(velocity_ref[0, :, start : start + 128])
            for part in range(4):
                low = sides[0] if part == 0 else pltpu.roll(sides[0], 128 - 32 * part, 1)
                high = sides[1] if part == 1 else pltpu.roll(sides[1], (160 - 32 * part) % 128, 1)
                fine_table[pl.ds(comp * 16 + half * 4 + part, 8, stride=FINE_ROWS), :] = jnp.where(
                    lane < 32, low, high
                )

    for slot in range(refine_ref.shape[1]):
        block = jnp.clip(refine_ref[0, slot] - me * BLK, 0, BLK - 1)
        k = jnp.clip(refine_ref[1, slot], 0, 5)
        yz = (k >= 2).astype(jnp.int32)
        base = block * FINE_ROWS + yz * 8
        group = k - 2 * yz
        parts = []
        for target, comp in enumerate((k // 2, 3, 4)):
            value = fine_table[pl.ds(pl.multiple_of(base + comp * 16, 8), 8), :]
            parts.append(pltpu.roll(value, (128 + 32 * target - 32 * group) % 128, 1))
        packets_ref[slot] = jnp.where(
            lane < 32, parts[0], jnp.where(lane < 64, parts[1], parts[2])
        )


def flux_kernel(faces_ref, packets_ref, table_ref, reflux_ref, live_list):
    me = lax.axis_index("sfc")
    lane = lanes()
    row = lax.broadcasted_iota(jnp.int32, VEC, 0)
    pos = lane % 32
    cell = pos % 16 // 2
    slots = packets_ref.shape[1]

    found = 0
    for offset in range(2 * REACH + 1):
        other = me + offset - REACH
        there = (other >= 0) & (other < lax.axis_size("sfc"))

        def collect(slot, found):
            local = table_ref[offset, 2, slot] - me * BLK
            mine = there & (table_ref[offset, 0, slot] >= 0) & (local >= 0) & (local < BLK)
            live_list[found] = offset * slots + slot
            return found + mine.astype(jnp.int32)

        found = lax.fori_loop(0, slots, collect, found, unroll=4 if slots % 4 == 0 else 1)
    for extra in range(3):
        live_list[found + extra] = REACH * slots

    reflux_ref[...] = jnp.zeros_like(reflux_ref)

    offset_one = ((pos // 16).astype(jnp.float32) - 0.5) * 0.5
    offset_two = ((pos % 2).astype(jnp.float32) - 0.5) * 0.5

    def moments(item, weight):
        offset = item // slots
        slot = item % slots
        k = jnp.clip(table_ref[offset, 1, slot], 0, 5)
        block = jnp.clip(table_ref[offset, 2, slot] - me * BLK, 0, BLK - 1)
        quadrant = jnp.clip(table_ref[offset, 3, slot], 0, 3)
        qa, qb = quadrant // 2, quadrant % 2
        facing = k + 1 - 2 * (k % 2)
        axis = k // 2
        sign = (2 * (k % 2) - 1).astype(jnp.float32)
        yz = (k >= 2).astype(jnp.int32)
        from_row = qa * 4 + row // 2
        from_lane = (facing - 2 * yz) * 32 + row % 2 * 16 + qb * 8 + cell
        base = block * FINE_ROWS + yz * 8
        first = jnp.where(axis == 0, 1, 0)
        second = jnp.where(axis == 2, 1, 2)
        normal_c, one_c, two_c, d_c, u_c = [
            take(
                jnp.take_along_axis(
                    faces_ref[pl.ds(pl.multiple_of(base + comp * 16, 8), 8), :],
                    from_row,
                    axis=0,
                    mode="promise_in_bounds",
                ),
                from_lane,
            )
            for comp in (axis, first, second, 3, 4)
        ]
        packet = packets_ref[offset, slot]
        normal_f = packet
        d_f = pltpu.roll(packet, 96, 1)
        u_f = pltpu.roll(packet, 64, 1)
        speed = sign * 0.5 * (u_f + u_c)
        depth = jnp.abs(speed) * TIME_STEP
        outflow = jnp.maximum(speed, 0.0)
        inflow = jnp.minimum(speed, 0.0)
        tangent = one_c * offset_one + two_c * offset_two + d_c
        volume = jnp.zeros(VEC, jnp.float32)
        moment = jnp.zeros(VEC, jnp.float32)
        for node in NODES:
            fine_model = 0.5 * (
                1.0 + jnp.tanh(normal_f * (sign * (0.5 - node * depth)) + d_f)
            )
            coarse_model = 0.5 * (
                1.0 + jnp.tanh(normal_c * (-sign * (0.5 - 0.5 * node * depth)) + tangent)
            )
            volume = volume + 0.5 * TIME_STEP * (outflow * fine_model + inflow * coarse_model)
            moment = moment + 0.5 * TIME_STEP * node * depth * sign * (
                inflow * coarse_model - outflow * fine_model
            )
        both = jnp.where(lane < 32, volume, pltpu.roll(moment, 32, 1))
        both = both + pltpu.roll(both, 127, 1)
        both = both + pltpu.roll(both, 112, 1)
        keep = (lane // 16 == row) & (lane % 16 // 8 == qb) & weight
        rows = []
        for m in range(2):
            placed = jnp.where(keep, take(both, m * 32 + 2 * (lane % 8)), 0.0)
            rows.append(jnp.sum(placed, axis=0, keepdims=True))
        return rows, block, facing, qa

    def group(number, carry):
        results = [
            moments(live_list[number * 4 + i], number * 4 + i < found) for i in range(4)
        ]
        for rows, block, facing, qa in results:
            start = pl.multiple_of(qa * 128, 128)
            for m in range(2):
                reflux_ref[block, facing, m : m + 1, pl.ds(start, 128)] += rows[m]
        return carry

    lax.fori_loop(0, (found + 3) // 4, group, 0)


def spec(space):
    return pl.BlockSpec(memory_space=space)


def per_device(fraction, centroid, velocity, neighbours, refinement):
    count = lax.axis_size("sfc")
    slots = refinement.shape[0]
    vmem, smem = spec(pltpu.VMEM), spec(pltpu.SMEM)
    f32 = jnp.float32
    refinement = refinement.T
    centroid, velocity = jnp.swapaxes(centroid, 0, 1), jnp.swapaxes(velocity, 0, 1)
    near, table = pl.pallas_call(
        lambda *refs: faces_kernel(count, *refs),
        out_shape=(
            jax.ShapeDtypeStruct((6, BLK * BLOCK_ROWS, 128), f32),
            jax.ShapeDtypeStruct((5, 4, slots), jnp.int32),
        ),
        in_specs=[vmem] * 3,
        out_specs=(vmem, vmem),
        scratch_shapes=[pltpu.SemaphoreType.DMA((4,))] * 4,
        compiler_params=pltpu.CompilerParams(collective_id=0, has_side_effects=True),
        name="exchange_faces",
    )(fraction, centroid, refinement)
    planes, faces, packets = pl.pallas_call(
        fit_kernel,
        out_shape=(
            jax.ShapeDtypeStruct((BLK, 4, CELLS), f32),
            jax.ShapeDtypeStruct((BLK * FINE_ROWS, 128), f32),
            jax.ShapeDtypeStruct((slots, 8, 128), f32),
        ),
        in_specs=[vmem] * 4 + [smem] * 2,
        out_specs=(vmem,) * 3,
        scratch_shapes=[
            pltpu.VMEM((4, 8, CELLS + 512), f32),
            pltpu.VMEM((256, 128), f32),
            pltpu.VMEM((2, 64, 128), f32),
        ],
        name="fit_planes",
    )(fraction, centroid, velocity, near.reshape(48, ITEMS, 8, 128), neighbours, refinement)
    near_packets = pl.pallas_call(
        lambda *refs: packets_kernel(count, *refs),
        out_shape=jax.ShapeDtypeStruct((5, slots, 8, 128), f32),
        in_specs=[vmem],
        out_specs=vmem,
        scratch_shapes=[pltpu.SemaphoreType.DMA((4,))] * 2,
        compiler_params=pltpu.CompilerParams(collective_id=1, has_side_effects=True),
        name="exchange_packets",
    )(packets)
    reflux = pl.pallas_call(
        flux_kernel,
        out_shape=jax.ShapeDtypeStruct((BLK, 6, 2, 256), f32),
        in_specs=[vmem] * 2 + [smem],
        out_specs=vmem,
        scratch_shapes=[pltpu.SMEM((5 * slots + 4,), jnp.int32)],
        name="reflux_moments",
    )(faces, near_packets, table)
    return planes, reflux


def solution(mesh):
    return jax.shard_map(
        per_device,
        mesh=mesh,
        in_specs=(
            P("sfc", None),
            P("sfc", None, None),
            P("sfc", None, None),
            P("sfc", None),
            P("sfc", None),
        ),
        out_specs=(P("sfc", None, None), P("sfc", None, None, None)),
        check_vma=False,
    )
```

```python
import jax
import jax.numpy as jnp
from jax import lax
from jax.experimental import pallas as pl
from jax.experimental.pallas import tpu as pltpu
from jax.sharding import PartitionSpec as P

EDGE = 16
CELLS = 4096
REACH = 2
PASSES = 6
BLK = 8
NODES = (0.5 - 3.0**0.5 / 6.0, 0.5 + 3.0**0.5 / 6.0)
TIME_STEP = 0.25
DAMPING = 0.1
SHIFTS = (1, -1, 2, -2)
VEC = (8, 128)
ITEMS = 6
FINE_ROWS = 5 * 2 * 8


def lanes():
    return lax.broadcasted_iota(jnp.int32, VEC, 1)


def take(values, index):
    return jnp.take_along_axis(values, index, axis=1, mode="promise_in_bounds")


def edge_index(swap):
    lane = lanes()
    kind = lane // 32
    if swap:
        kind = kind + 1 - 2 * (kind % 2)
    j = lane % 16
    source = jnp.where(
        kind == 0, j, jnp.where(kind == 1, 112 + j, (j % 8) * 16 + jnp.where(kind == 3, 15, 0))
    )
    upper = jnp.where(kind == 0, 0, jnp.where(kind == 1, 1, j // 8))
    return source, upper == 1, (lane // 16) % 2 == 1


def edges(tiles, index):
    source, upper, odd = index
    first = jnp.where(upper, take(tiles[1], source), take(tiles[0], source))
    second = jnp.where(upper, take(tiles[3], source), take(tiles[2], source))
    return jnp.where(odd, second, first)


def field_rows(fraction_ref, centroid_ref, field, start, size):
    if field == 0:
        return fraction_ref[:, pl.ds(start, size)]
    return centroid_ref[field - 1, :, pl.ds(start, size)]


def within(device, count):
    return (device >= 0) & (device < count)


def greet(me, peers):
    barrier = pltpu.get_barrier_semaphore()
    number = 0
    for other, there in peers:

        @pl.when(there)
        def _signal():
            pl.semaphore_signal(
                barrier, inc=1, device_id=(other,), device_id_type=pl.DeviceIdType.MESH
            )

        number = number + there.astype(jnp.int32)
    return barrier, number


def direct_peers(me, count):
    return [(me + shift, within(me + shift, count)) for shift in SHIFTS]


def remote(src, dst, send, recv, other):
    return pltpu.make_async_remote_copy(
        src_ref=src,
        dst_ref=dst,
        send_sem=send,
        recv_sem=recv,
        device_id=(other,),
        device_id_type=pl.DeviceIdType.MESH,
    )


class Direct:
    def __init__(self, me, count, buffer, pieces, send, recv):
        self.me, self.count = me, count
        self.buffer, self.pieces, self.send, self.recv = buffer, pieces, send, recv

    def peers(self):
        return direct_peers(self.me, self.count)

    def copy(self, place, piece):
        shift = SHIFTS[place]
        return remote(
            self.buffer.at[REACH, piece],
            self.buffer.at[REACH - shift, piece],
            self.send.at[place, piece],
            self.recv.at[place, piece],
            self.me + shift,
        )

    def start(self, piece):
        for place, shift in enumerate(SHIFTS):
            pl.when(within(self.me + shift, self.count))(self.copy(place, piece).start)

    def forward(self, piece):
        pass

    def finish(self):
        for piece in self.pieces:
            for place, shift in enumerate(SHIFTS):
                pl.when(within(self.me + shift, self.count))(self.copy(place, piece).wait_send)
                pl.when(within(self.me - shift, self.count))(self.copy(place, piece).wait_recv)


class Relay:
    def __init__(self, me, count, buffer, pieces, send, recv):
        self.me, self.buffer, self.pieces, self.send, self.recv = me, buffer, pieces, send, recv
        core, x, y = me % 2, me // 2 % 2, me // 4 % 2
        unlike = (x + y) % 2
        self.x, self.core = x, core
        spare = 2 * REACH + 2
        self.by_z = unlike == 0
        z_to, z_from = me + 8 - 16 * x, me - 8 + 16 * x
        self.z_send = self.by_z & within(z_to, count)
        self.z_recv = self.by_z & within(z_from, count)
        self.second = (unlike == 1) | within(z_from, count)
        self.others = [(me + 4 - 8 * y, me >= 0)] + [
            (me + shift, self.by_z & within(me + shift, count)) for shift in (8, -8)
        ]
        y_there = unlike * spare + (1 - unlike) * 4 * x
        y_here = (1 - unlike) * spare + unlike * 4 * x
        self.steps = (
            (me + 2 - 4 * x, REACH, 4 * x, 4 * (1 - x)),
            (me + 1 - 2 * core, REACH, 1 + 2 * core, 3 - 2 * core),
            (me + 4 - 8 * y, 4 * (1 - x), y_there, y_here),
            (z_to, spare, 4 * x, 4 * x),
            (me + 1 - 2 * core, 4 * (1 - core), 3 - 2 * core, 1 + 2 * core),
        )

    def peers(self):
        near = [(self.steps[0][0], self.me >= 0), (self.steps[1][0], self.me >= 0)]
        return near + self.others

    def sent(self, step, piece):
        other, source, there, _here = self.steps[step]
        return remote(
            self.buffer.at[source, piece],
            self.buffer.at[there, piece],
            self.send.at[step, piece],
            self.recv.at[step, piece],
            other,
        )

    def arrived(self, step, piece):
        other, source, _there, here = self.steps[step]
        return remote(
            self.buffer.at[source, piece],
            self.buffer.at[here, piece],
            self.send.at[step, piece],
            self.recv.at[step, piece],
            other,
        )

    def start(self, piece):
        self.sent(0, piece).start()
        self.sent(1, piece).start()

    def forward(self, piece):
        self.arrived(0, piece).wait_recv()
        self.sent(2, piece).start()
        pl.when(self.x == self.core)(self.sent(4, piece).start)

    def finish(self):
        late = self.x != self.core
        for piece in self.pieces:
            self.arrived(2, piece).wait_recv()
            pl.when(self.z_send)(self.sent(3, piece).start)
            pl.when(jnp.logical_not(self.by_z) & late)(self.sent(4, piece).start)
        for piece in self.pieces:

            @pl.when(self.z_recv)
            def _last():
                self.arrived(3, piece).wait_recv()
                pl.when(late)(self.sent(4, piece).start)

        for piece in self.pieces:
            self.arrived(1, piece).wait_recv()
            pl.when(self.second | late)(self.arrived(4, piece).wait_recv)
            for step in range(3):
                self.sent(step, piece).wait_send()
            pl.when(self.z_send)(self.sent(3, piece).wait_send)
            pl.when(self.second | jnp.logical_not(late))(self.sent(4, piece).wait_send)


def way(count):
    return Relay if count == 32 else Direct


def faces_kernel(
    count, fraction_ref, centroid_ref, refine_ref, near_ref, table_ref, send, recv, send2, recv2
):
    me = lax.axis_index("sfc")
    order = (4, 5, 0, 1, 2, 3)
    faces = way(count)(me, count, near_ref, order, send, recv)
    peers = direct_peers(me, count)
    if count == 32:
        peers = peers + faces.others
    barrier, number = greet(me, peers)
    swapped = edge_index(True)
    plain = edge_index(False)

    def extract(slot, item, index, swap):
        if item < 4:
            for pair in range(8):
                chunk = field_rows(fraction_ref, centroid_ref, item, pair * 512, 512)
                tiles = [chunk[:, 128 * t : 128 * t + 128] for t in range(4)]
                near_ref[slot, item, pl.ds(pair, 8, stride=8), :] = edges(tiles, index)
        else:
            for side in range(2):
                start = (1 - side if swap else side) * 3840 + (item - 4) * 128
                for field in range(4):
                    near_ref[slot, item, pl.ds(side * 4 + field, 8, stride=8), :] = field_rows(
                        fraction_ref, centroid_ref, field, start, 128
                    )

    table_ref[REACH] = refine_ref[...]
    for piece in order:
        extract(REACH, piece, swapped, True)
        if piece == order[0]:
            pl.semaphore_wait(barrier, number)
        faces.start(piece)

    def table_copy(place):
        shift = SHIFTS[place]
        return remote(
            refine_ref, table_ref.at[REACH - shift], send2.at[place], recv2.at[place], me + shift
        )

    for place, shift in enumerate(SHIFTS):
        pl.when(within(me + shift, count))(table_copy(place).start)
    for piece in order:
        faces.forward(piece)
        extract(2 * REACH + 1, piece, plain, False)
    faces.finish()
    for place, shift in enumerate(SHIFTS):
        pl.when(within(me + shift, count))(table_copy(place).wait_send)
        pl.when(within(me - shift, count))(table_copy(place).wait_recv)


def packets_kernel(count, own_ref, near_ref, send, recv):
    me = lax.axis_index("sfc")
    pieces = range(own_ref.shape[0])
    packets = way(count)(me, count, near_ref, pieces, send, recv)
    barrier, number = greet(me, packets.peers())
    near_ref[REACH] = own_ref[...]
    pl.semaphore_wait(barrier, number)
    for piece in pieces:
        packets.start(piece)
    for piece in pieces:
        packets.forward(piece)
    packets.finish()


def solve(h, g):
    (h00, h01, h02, h03, h11, h12, h13, h22, h23, h33) = h
    i0 = 1.0 / h00
    l10, l20, l30 = h01 * i0, h02 * i0, h03 * i0
    d1 = h11 - l10 * h01
    a21, a31 = h12 - l10 * h02, h13 - l10 * h03
    i1 = 1.0 / d1
    l21, l31 = a21 * i1, a31 * i1
    d2 = h22 - l20 * h02 - l21 * a21
    a32 = h23 - l20 * h03 - l21 * a31
    i2 = 1.0 / d2
    l32 = a32 * i2
    d3 = h33 - l30 * h03 - l31 * a31 - l32 * a32
    y1 = g[1] - l10 * g[0]
    y2 = g[2] - l20 * g[0] - l21 * y1
    y3 = g[3] - l30 * g[0] - l31 * y1 - l32 * y2
    x3 = y3 / d3
    x2 = y2 * i2 - l32 * x3
    x1 = y1 * i1 - l21 * x2 - l31 * x3
    x0 = g[0] * i0 - l10 * x1 - l20 * x2 - l30 * x3
    return x0, x1, x2, x3


def fit(points, params):
    def one_pass(_unused, params):
        a, b, c, d = params
        h = [None] * 10
        g = [None] * 4

        def add(total, place, term):
            total[place] = term if total[place] is None else total[place] + term

        for px, py, pz, f in points:
            t = jnp.tanh(a * px + b * py + c * pz + d)
            s = 1.0 - t * t
            q = s * s
            w = s * (t - f)
            qx, qy, qz = q * px, q * py, q * pz
            for place, term in enumerate(
                (qx * px, qx * py, qx * pz, qx, qy * py, qy * pz, qy, qz * pz, qz, q)
            ):
                add(h, place, term)
            for place, term in enumerate((w * px, w * py, w * pz, w)):
                add(g, place, term)
        for place in (0, 4, 7, 9):
            h[place] = h[place] + 4.0 * DAMPING
        step = solve(h, g)
        return tuple(p - s for p, s in zip(params, step))

    return lax.fori_loop(0, PASSES, one_pass, params)


def fit_kernel(
    fraction_ref,
    centroid_ref,
    velocity_ref,
    near_ref,
    neighbours_ref,
    refine_ref,
    planes_ref,
    fine_table,
    packets_ref,
    padded,
    ghost_edges,
    ghost_layers,
):
    me = lax.axis_index("sfc")
    lane = lanes()
    row = lax.broadcasted_iota(jnp.int32, VEC, 0)
    first_block = (me - REACH) * BLK

    for block in range(BLK):
        place = []
        for k in range(6):
            other = neighbours_ref[block, k]
            place.append(
                jnp.where(
                    other >= 0,
                    jnp.clip(other - first_block, 0, (2 * REACH + 1) * BLK - 1),
                    (2 * REACH + 1) * BLK + block,
                )
            )

        def face(k, item):
            return near_ref[place[k] // BLK, item, place[k] % BLK]

        for field in range(4):
            value = face(5, field)
            for k in (4, 3, 2):
                value = jnp.where(lane < (k - 1) * 32, face(k, field), value)
            ghost_edges[block * 32 + field * 8 : block * 32 + field * 8 + 8, :] = value
        for half in range(2):
            ghost_layers[half, block * 8 : block * 8 + 8, :] = jnp.where(
                row < 4, face(0, 4 + half), face(1, 4 + half)
            )

    for field in range(4):
        for half in range(2):
            for side in range(2):
                start = side * 4352 + half * 128
                padded[field, :, start : start + 128] = ghost_layers[
                    half, pl.ds(side * 4 + field, 8, stride=8), :
                ]
        padded[field, :, 256:4352] = field_rows(fraction_ref, centroid_ref, field, 0, CELLS)

    wide = lax.broadcasted_iota(jnp.int32, (8, 512), 1)
    y_pos = wide // 16 % 16
    z_pos = wide % 16
    plain = edge_index(False)
    y_source, z_source = [], []
    for tile in range(4):
        odd, upper = tile // 2, tile % 2
        y_source.append(upper * 32 + odd * 16 + lane % 16)
        z_source.append(
            jnp.where(lane % 16 < 8, 64, 96) + odd * 16 + upper * 8 + lane // 16
        )

    def one_pair(pair, carry):
        start = pl.multiple_of(pair * 512, 512)
        fields = [[] for _unused in range(7)]
        for field in range(4):
            center = padded[field, :, pl.ds(start + 256, 512)]
            ghost = ghost_edges[pl.ds(field * 8 + pair, 8, stride=32), :]
            ghost_y = jnp.concatenate([take(ghost, i) for i in y_source], 1)
            ghost_z = jnp.concatenate([take(ghost, i) for i in z_source], 1)
            fields[0].append(center)
            fields[1].append(padded[field, :, pl.ds(start, 512)])
            fields[2].append(padded[field, :, pl.ds(start + 512, 512)])
            fields[3].append(jnp.where(y_pos == 0, ghost_y, pltpu.roll(center, 16, 1)))
            fields[4].append(jnp.where(y_pos == 15, ghost_y, pltpu.roll(center, 496, 1)))
            fields[5].append(jnp.where(z_pos == 0, ghost_z, pltpu.roll(center, 1, 1)))
            fields[6].append(jnp.where(z_pos == 15, ghost_z, pltpu.roll(center, 511, 1)))
        a, b, c = [2.0 * (fields[2 + 2 * i][0] - fields[1 + 2 * i][0]) for i in range(3)]
        frac, cx, cy, cz = fields[0]
        d = 2.0 * (2.0 * frac - 1.0) - a * cx - b * cy - c * cz
        points = [(cx, cy, cz, 2.0 * frac - 1.0)]
        for k in range(6):
            f, *coords = fields[k + 1]
            coords[k // 2] = coords[k // 2] + (2.0 * (k % 2) - 1.0)
            points.append((*coords, 2.0 * f - 1.0))
        params = fit(points, (a, b, c, d))
        for comp in range(4):
            planes_ref[:, comp, pl.ds(start, 512)] = params[comp]
            tiles = [params[comp][:, 128 * t : 128 * t + 128] for t in range(4)]
            fine_table[pl.ds(comp * 16 + 8 + pair, 8, stride=FINE_ROWS), :] = edges(tiles, plain)
        speeds = []
        for axis in (1, 2):
            chunk = velocity_ref[axis, :, pl.ds(start, 512)]
            speeds.append(edges([chunk[:, 128 * t : 128 * t + 128] for t in range(4)], plain))
        fine_table[pl.ds(4 * 16 + 8 + pair, 8, stride=FINE_ROWS), :] = jnp.where(
            lane < 64, speeds[0], speeds[1]
        )
        return carry

    lax.fori_loop(0, 8, one_pair, 0)

    for comp in range(5):
        for half in range(2):
            sides = []
            for side in range(2):
                start = side * 3840 + half * 128
                if comp < 4:
                    sides.append(planes_ref[:, comp, start : start + 128])
                else:
                    sides.append(velocity_ref[0, :, start : start + 128])
            for part in range(4):
                low = sides[0] if part == 0 else pltpu.roll(sides[0], 128 - 32 * part, 1)
                high = sides[1] if part == 1 else pltpu.roll(sides[1], (160 - 32 * part) % 128, 1)
                fine_table[pl.ds(comp * 16 + half * 4 + part, 8, stride=FINE_ROWS), :] = jnp.where(
                    lane < 32, low, high
                )

    for slot in range(refine_ref.shape[1]):
        block = jnp.clip(refine_ref[0, slot] - me * BLK, 0, BLK - 1)
        k = jnp.clip(refine_ref[1, slot], 0, 5)
        yz = (k >= 2).astype(jnp.int32)
        base = block * FINE_ROWS + yz * 8
        group = k - 2 * yz
        parts = []
        for target, comp in enumerate((k // 2, 3, 4)):
            value = fine_table[pl.ds(pl.multiple_of(base + comp * 16, 8), 8), :]
            parts.append(pltpu.roll(value, (128 + 32 * target - 32 * group) % 128, 1))
        packets_ref[slot] = jnp.where(
            lane < 32, parts[0], jnp.where(lane < 64, parts[1], parts[2])
        )


def flux_kernel(faces_ref, packets_ref, table_ref, reflux_ref, live_list):
    me = lax.axis_index("sfc")
    lane = lanes()
    row = lax.broadcasted_iota(jnp.int32, VEC, 0)
    pos = lane % 32
    cell = pos % 16 // 2
    slots = packets_ref.shape[1]

    found = 0
    for offset in range(2 * REACH + 1):
        other = me + offset - REACH
        there = (other >= 0) & (other < lax.axis_size("sfc"))

        def collect(slot, found):
            local = table_ref[offset, 2, slot] - me * BLK
            mine = there & (table_ref[offset, 0, slot] >= 0) & (local >= 0) & (local < BLK)
            live_list[found] = offset * slots + slot
            return found + mine.astype(jnp.int32)

        found = lax.fori_loop(0, slots, collect, found, unroll=4 if slots % 4 == 0 else 1)
    for extra in range(3):
        live_list[found + extra] = REACH * slots

    reflux_ref[...] = jnp.zeros_like(reflux_ref)

    offset_one = ((pos // 16).astype(jnp.float32) - 0.5) * 0.5
    offset_two = ((pos % 2).astype(jnp.float32) - 0.5) * 0.5

    def moments(item, weight):
        offset = item // slots
        slot = item % slots
        k = jnp.clip(table_ref[offset, 1, slot], 0, 5)
        block = jnp.clip(table_ref[offset, 2, slot] - me * BLK, 0, BLK - 1)
        quadrant = jnp.clip(table_ref[offset, 3, slot], 0, 3)
        qa, qb = quadrant // 2, quadrant % 2
        facing = k + 1 - 2 * (k % 2)
        axis = k // 2
        sign = (2 * (k % 2) - 1).astype(jnp.float32)
        yz = (k >= 2).astype(jnp.int32)
        from_row = qa * 4 + row // 2
        from_lane = (facing - 2 * yz) * 32 + row % 2 * 16 + qb * 8 + cell
        base = block * FINE_ROWS + yz * 8
        first = jnp.where(axis == 0, 1, 0)
        second = jnp.where(axis == 2, 1, 2)
        normal_c, one_c, two_c, d_c, u_c = [
            take(
                jnp.take_along_axis(
                    faces_ref[pl.ds(pl.multiple_of(base + comp * 16, 8), 8), :],
                    from_row,
                    axis=0,
                    mode="promise_in_bounds",
                ),
                from_lane,
            )
            for comp in (axis, first, second, 3, 4)
        ]
        packet = packets_ref[offset, slot]
        normal_f = packet
        d_f = pltpu.roll(packet, 96, 1)
        u_f = pltpu.roll(packet, 64, 1)
        speed = sign * 0.5 * (u_f + u_c)
        depth = jnp.abs(speed) * TIME_STEP
        outflow = jnp.maximum(speed, 0.0)
        inflow = jnp.minimum(speed, 0.0)
        tangent = one_c * offset_one + two_c * offset_two + d_c
        volume = jnp.zeros(VEC, jnp.float32)
        moment = jnp.zeros(VEC, jnp.float32)
        for node in NODES:
            fine_model = 0.5 * (
                1.0 + jnp.tanh(normal_f * (sign * (0.5 - node * depth)) + d_f)
            )
            coarse_model = 0.5 * (
                1.0 + jnp.tanh(normal_c * (-sign * (0.5 - 0.5 * node * depth)) + tangent)
            )
            volume = volume + 0.5 * TIME_STEP * (outflow * fine_model + inflow * coarse_model)
            moment = moment + 0.5 * TIME_STEP * node * depth * sign * (
                inflow * coarse_model - outflow * fine_model
            )
        both = jnp.where(lane < 32, volume, pltpu.roll(moment, 32, 1))
        both = both + pltpu.roll(both, 127, 1)
        both = both + pltpu.roll(both, 112, 1)
        keep = (lane // 16 == row) & (lane % 16 // 8 == qb) & weight
        rows = []
        for m in range(2):
            placed = jnp.where(keep, take(both, m * 32 + 2 * (lane % 8)), 0.0)
            rows.append(jnp.sum(placed, axis=0, keepdims=True))
        return rows, block, facing, qa

    def group(number, carry):
        results = [
            moments(live_list[number * 4 + i], number * 4 + i < found) for i in range(4)
        ]
        for rows, block, facing, qa in results:
            start = pl.multiple_of(qa * 128, 128)
            for m in range(2):
                reflux_ref[block, facing, m : m + 1, pl.ds(start, 128)] += rows[m]
        return carry

    lax.fori_loop(0, (found + 3) // 4, group, 0)


def spec(space):
    return pl.BlockSpec(memory_space=space)


def per_device(fraction, centroid, velocity, neighbours, refinement):
    count = lax.axis_size("sfc")
    slots = refinement.shape[0]
    pieces = 4 if slots % 4 == 0 else 1
    vmem, smem = spec(pltpu.VMEM), spec(pltpu.SMEM)
    f32 = jnp.float32
    refinement = refinement.T
    centroid, velocity = jnp.swapaxes(centroid, 0, 1), jnp.swapaxes(velocity, 0, 1)
    near, table = pl.pallas_call(
        lambda *refs: faces_kernel(count, *refs),
        out_shape=(
            jax.ShapeDtypeStruct((7, ITEMS, BLK * 8, 128), f32),
            jax.ShapeDtypeStruct((5, 4, slots), jnp.int32),
        ),
        in_specs=[vmem] * 3,
        out_specs=(vmem, vmem),
        scratch_shapes=[pltpu.SemaphoreType.DMA((5, ITEMS))] * 2
        + [pltpu.SemaphoreType.DMA((4,))] * 2,
        compiler_params=pltpu.CompilerParams(collective_id=0, has_side_effects=True),
        name="exchange_faces",
    )(fraction, centroid, refinement)
    planes, faces, packets = pl.pallas_call(
        fit_kernel,
        out_shape=(
            jax.ShapeDtypeStruct((BLK, 4, CELLS), f32),
            jax.ShapeDtypeStruct((BLK * FINE_ROWS, 128), f32),
            jax.ShapeDtypeStruct((slots, 8, 128), f32),
        ),
        in_specs=[vmem] * 4 + [smem] * 2,
        out_specs=(vmem,) * 3,
        scratch_shapes=[
            pltpu.VMEM((4, 8, CELLS + 512), f32),
            pltpu.VMEM((256, 128), f32),
            pltpu.VMEM((2, 64, 128), f32),
        ],
        name="fit_planes",
    )(fraction, centroid, velocity, near.reshape(7, ITEMS, BLK, 8, 128), neighbours, refinement)
    near_packets = pl.pallas_call(
        lambda *refs: packets_kernel(count, *refs),
        out_shape=jax.ShapeDtypeStruct((7, pieces, slots // pieces * 8, 128), f32),
        in_specs=[vmem],
        out_specs=vmem,
        scratch_shapes=[pltpu.SemaphoreType.DMA((5, pieces))] * 2,
        compiler_params=pltpu.CompilerParams(collective_id=1, has_side_effects=True),
        name="exchange_packets",
    )(packets.reshape(pieces, slots // pieces * 8, 128))
    reflux = pl.pallas_call(
        flux_kernel,
        out_shape=jax.ShapeDtypeStruct((BLK, 6, 2, 256), f32),
        in_specs=[vmem] * 2 + [smem],
        out_specs=vmem,
        scratch_shapes=[pltpu.SMEM((5 * slots + 4,), jnp.int32)],
        name="reflux_moments",
    )(faces, near_packets.reshape(7, slots, 8, 128), table)
    return planes, reflux


def solution(mesh):
    return jax.shard_map(
        per_device,
        mesh=mesh,
        in_specs=(
            P("sfc", None),
            P("sfc", None, None),
            P("sfc", None, None),
            P("sfc", None),
            P("sfc", None),
        ),
        out_specs=(P("sfc", None, None), P("sfc", None, None, None)),
        check_vma=False,
    )
```

```python
import jax
import jax.numpy as jnp
import numpy as np
from jax import lax
from jax.experimental import pallas as pl
from jax.experimental.pallas import tpu as pltpu
from jax.sharding import PartitionSpec as P

EDGE = 16
CELLS = 4096
REACH = 2
PASSES = 6
BLK = 8
NODES = (0.5 - 3.0**0.5 / 6.0, 0.5 + 3.0**0.5 / 6.0)
TIME_STEP = 0.25
DAMPING = 0.1
SHIFTS = (1, -1, 2, -2)
VEC = (8, 128)
ITEMS = 6
FINE_ROWS = 4 * 2 * 8


def lanes():
    return lax.broadcasted_iota(jnp.int32, VEC, 1)


def take(values, index):
    return jnp.take_along_axis(values, index, axis=1, mode="promise_in_bounds")


def edge_place(kind, odd, j):
    y, z = ((0, j), (15, j), (j, 0), (j, 15))[kind]
    return odd * 256 + y * 16 + z


def edge_matrix():
    matrix = np.zeros((512, 256), np.float32)
    for lane in range(128):
        kind, odd, j = lane // 32, lane // 16 % 2, lane % 16
        matrix[edge_place(kind + 1 - 2 * (kind % 2), odd, j), lane] = 1
        matrix[edge_place(kind, odd, j), 128 + lane] = 1
    return jnp.asarray(matrix, jnp.bfloat16)


def ghost_matrix():
    matrix = np.zeros((128, 512), np.float32)
    for lane in range(64, 128):
        matrix[lane, edge_place(lane // 32, lane // 16 % 2, lane % 16)] = 1
    return jnp.asarray(matrix, jnp.bfloat16)


def select(values, matrix):
    high = values.astype(jnp.bfloat16)
    rest = values - high.astype(jnp.float32)
    middle = rest.astype(jnp.bfloat16)
    low = (rest - middle.astype(jnp.float32)).astype(jnp.bfloat16)
    parts = [
        jnp.dot(part, matrix, preferred_element_type=jnp.float32) for part in (low, middle, high)
    ]
    return parts[0] + parts[1] + parts[2]


def layer_parts(low, high, part):
    first = low if part == 0 else pltpu.roll(low, 128 - 32 * part, 1)
    second = high if part == 1 else pltpu.roll(high, (160 - 32 * part) % 128, 1)
    return jnp.where(lanes() < 32, first, second)


def field_rows(fraction_ref, centroid_ref, field, start, size):
    if field == 0:
        return fraction_ref[:, pl.ds(start, size)]
    return centroid_ref[field - 1, :, pl.ds(start, size)]


def within(device, count):
    return (device >= 0) & (device < count)


def greet(me, peers):
    barrier = pltpu.get_barrier_semaphore()
    number = 0
    for other, there in peers:

        @pl.when(there)
        def _signal():
            pl.semaphore_signal(
                barrier, inc=1, device_id=(other,), device_id_type=pl.DeviceIdType.MESH
            )

        number = number + there.astype(jnp.int32)
    return barrier, number


def direct_peers(me, count):
    return [(me + shift, within(me + shift, count)) for shift in SHIFTS]


def remote(src, dst, send, recv, other):
    return pltpu.make_async_remote_copy(
        src_ref=src,
        dst_ref=dst,
        send_sem=send,
        recv_sem=recv,
        device_id=(other,),
        device_id_type=pl.DeviceIdType.MESH,
    )


class Direct:
    def __init__(self, me, count, buffer, pieces, send, recv):
        self.me, self.count = me, count
        self.buffer, self.pieces, self.send, self.recv = buffer, pieces, send, recv

    def peers(self):
        return direct_peers(self.me, self.count)

    def copy(self, place, piece):
        shift = SHIFTS[place]
        return remote(
            self.buffer.at[REACH, piece],
            self.buffer.at[REACH - shift, piece],
            self.send.at[place, piece],
            self.recv.at[place, piece],
            self.me + shift,
        )

    def start(self, piece):
        for place, shift in enumerate(SHIFTS):
            pl.when(within(self.me + shift, self.count))(self.copy(place, piece).start)

    def forward(self, piece):
        pass

    def finish(self):
        for piece in self.pieces:
            for place, shift in enumerate(SHIFTS):
                pl.when(within(self.me + shift, self.count))(self.copy(place, piece).wait_send)
                pl.when(within(self.me - shift, self.count))(self.copy(place, piece).wait_recv)


class Relay:
    def __init__(self, me, count, buffer, pieces, send, recv):
        self.me, self.buffer, self.pieces, self.send, self.recv = me, buffer, pieces, send, recv
        core, x, y = me % 2, me // 2 % 2, me // 4 % 2
        unlike = (x + y) % 2
        self.x, self.core = x, core
        spare = 2 * REACH + 2
        self.by_z = unlike == 0
        z_to, z_from = me + 8 - 16 * x, me - 8 + 16 * x
        self.z_send = self.by_z & within(z_to, count)
        self.z_recv = self.by_z & within(z_from, count)
        self.second = (unlike == 1) | within(z_from, count)
        self.others = [(me + 4 - 8 * y, me >= 0)] + [
            (me + shift, self.by_z & within(me + shift, count)) for shift in (8, -8)
        ]
        y_there = unlike * spare + (1 - unlike) * 4 * x
        y_here = (1 - unlike) * spare + unlike * 4 * x
        self.steps = (
            (me + 2 - 4 * x, REACH, 4 * x, 4 * (1 - x)),
            (me + 1 - 2 * core, REACH, 1 + 2 * core, 3 - 2 * core),
            (me + 4 - 8 * y, 4 * (1 - x), y_there, y_here),
            (z_to, spare, 4 * x, 4 * x),
            (me + 1 - 2 * core, 4 * (1 - core), 3 - 2 * core, 1 + 2 * core),
        )

    def peers(self):
        near = [(self.steps[0][0], self.me >= 0), (self.steps[1][0], self.me >= 0)]
        return near + self.others

    def sent(self, step, piece):
        other, source, there, _here = self.steps[step]
        return remote(
            self.buffer.at[source, piece],
            self.buffer.at[there, piece],
            self.send.at[step, piece],
            self.recv.at[step, piece],
            other,
        )

    def arrived(self, step, piece):
        other, source, _there, here = self.steps[step]
        return remote(
            self.buffer.at[source, piece],
            self.buffer.at[here, piece],
            self.send.at[step, piece],
            self.recv.at[step, piece],
            other,
        )

    def start(self, piece):
        self.sent(0, piece).start()
        self.sent(1, piece).start()

    def forward(self, piece):
        self.arrived(0, piece).wait_recv()
        self.sent(2, piece).start()
        pl.when(self.x == self.core)(self.sent(4, piece).start)

    def finish(self):
        late = self.x != self.core
        for piece in self.pieces:
            self.arrived(2, piece).wait_recv()
            pl.when(self.z_send)(self.sent(3, piece).start)
            pl.when(jnp.logical_not(self.by_z) & late)(self.sent(4, piece).start)
        for piece in self.pieces:

            @pl.when(self.z_recv)
            def _last():
                self.arrived(3, piece).wait_recv()
                pl.when(late)(self.sent(4, piece).start)

        for piece in self.pieces:
            self.arrived(1, piece).wait_recv()
            pl.when(self.second | late)(self.arrived(4, piece).wait_recv)
            for step in range(3):
                self.sent(step, piece).wait_send()
            pl.when(self.z_send)(self.sent(3, piece).wait_send)
            pl.when(self.second | jnp.logical_not(late))(self.sent(4, piece).wait_send)


def way(count):
    return Relay if count == 32 else Direct


def faces_kernel(
    count,
    fraction_ref,
    centroid_ref,
    velocity_ref,
    refine_ref,
    edge_ref,
    near_ref,
    table_ref,
    speed_ref,
    send,
    recv,
    send2,
    recv2,
):
    me = lax.axis_index("sfc")
    order = (4, 5, 0, 1, 2, 3)
    faces = way(count)(me, count, near_ref, order, send, recv)
    peers = direct_peers(me, count)
    if count == 32:
        peers = peers + faces.others
    barrier, number = greet(me, peers)

    def extract_layers(slot, item, swap):
        for side in range(2):
            start = (1 - side if swap else side) * 3840 + (item - 4) * 128
            for field in range(4):
                near_ref[slot, item, pl.ds(side * 4 + field, 8, stride=8), :] = field_rows(
                    fraction_ref, centroid_ref, field, start, 128
                )

    extract_layers(REACH, 4, True)
    extract_layers(REACH, 5, True)
    pl.semaphore_wait(barrier, number)
    faces.start(4)
    faces.start(5)
    both = select(
        jnp.concatenate(
            [
                field_rows(fraction_ref, centroid_ref, field, pair * 512, 512)
                for field in range(4)
                for pair in range(8)
            ],
            0,
        ),
        edge_ref[...],
    )

    def put(slot, field, start):
        for pair in range(8):
            row = field * 64 + pair * 8
            near_ref[slot, field, pl.ds(pair, 8, stride=8), :] = both[
                row : row + 8, start : start + 128
            ]

    for field in range(4):
        put(REACH, field, 0)
        faces.start(field)

    def table_copy(place):
        shift = SHIFTS[place]
        return remote(
            refine_ref, table_ref.at[REACH - shift], send2.at[place], recv2.at[place], me + shift
        )

    table_ref[REACH] = refine_ref[...]
    for place, shift in enumerate(SHIFTS):
        pl.when(within(me + shift, count))(table_copy(place).start)

    for field in range(4):
        put(2 * REACH + 1, field, 128)
    faces.forward(4)
    extract_layers(2 * REACH + 1, 4, False)
    faces.forward(5)
    extract_layers(2 * REACH + 1, 5, False)
    faces.forward(0)
    speeds = select(
        jnp.concatenate(
            [velocity_ref[axis, :, pl.ds(pair * 512, 512)] for axis in (1, 2) for pair in range(8)],
            0,
        ),
        edge_ref[:, 128:],
    )
    for pair in range(8):
        speed_ref[pl.ds(8 + pair, 8, stride=16), :] = jnp.where(
            lanes() < 64, speeds[pair * 8 : pair * 8 + 8], speeds[64 + pair * 8 : 72 + pair * 8]
        )
    faces.forward(1)
    for part in range(8):
        start = part // 4 * 128
        speed_ref[pl.ds(part, 8, stride=16), :] = layer_parts(
            velocity_ref[0, :, start : start + 128],
            velocity_ref[0, :, 3840 + start : 3968 + start],
            part % 4,
        )
    faces.forward(2)
    faces.forward(3)
    faces.finish()
    for place, shift in enumerate(SHIFTS):
        pl.when(within(me + shift, count))(table_copy(place).wait_send)
        pl.when(within(me - shift, count))(table_copy(place).wait_recv)


def packets_kernel(count, own_ref, near_ref, send, recv):
    me = lax.axis_index("sfc")
    pieces = range(own_ref.shape[0])
    packets = Direct(me, count, near_ref, pieces, send, recv)
    barrier, number = greet(me, packets.peers())
    near_ref[REACH] = own_ref[...]
    pl.semaphore_wait(barrier, number)
    for piece in pieces:
        packets.start(piece)
    for piece in pieces:
        packets.forward(piece)
    packets.finish()


def solve(h, g):
    (h00, h01, h02, h03, h11, h12, h13, h22, h23, h33) = h
    i0 = 1.0 / h00
    l10, l20, l30 = h01 * i0, h02 * i0, h03 * i0
    d1 = h11 - l10 * h01
    a21, a31 = h12 - l10 * h02, h13 - l10 * h03
    i1 = 1.0 / d1
    l21, l31 = a21 * i1, a31 * i1
    d2 = h22 - l20 * h02 - l21 * a21
    a32 = h23 - l20 * h03 - l21 * a31
    i2 = 1.0 / d2
    l32 = a32 * i2
    d3 = h33 - l30 * h03 - l31 * a31 - l32 * a32
    y1 = g[1] - l10 * g[0]
    y2 = g[2] - l20 * g[0] - l21 * y1
    y3 = g[3] - l30 * g[0] - l31 * y1 - l32 * y2
    x3 = y3 / d3
    x2 = y2 * i2 - l32 * x3
    x1 = y1 * i1 - l21 * x2 - l31 * x3
    x0 = g[0] * i0 - l10 * x1 - l20 * x2 - l30 * x3
    return x0, x1, x2, x3


def fit(points, params):
    def one_pass(_unused, params):
        a, b, c, d = params
        h = [None] * 10
        g = [None] * 4

        def add(total, place, term):
            total[place] = term if total[place] is None else total[place] + term

        for px, py, pz, f in points:
            t = jnp.tanh(a * px + b * py + c * pz + d)
            s = 1.0 - t * t
            q = s * s
            w = s * (t - f)
            qx, qy, qz = q * px, q * py, q * pz
            for place, term in enumerate(
                (qx * px, qx * py, qx * pz, qx, qy * py, qy * pz, qy, qz * pz, qz, q)
            ):
                add(h, place, term)
            for place, term in enumerate((w * px, w * py, w * pz, w)):
                add(g, place, term)
        for place in (0, 4, 7, 9):
            h[place] = h[place] + 4.0 * DAMPING
        step = solve(h, g)
        return tuple(p - s for p, s in zip(params, step))

    return lax.fori_loop(0, PASSES, one_pass, params)


def fit_kernel(
    fraction_ref,
    centroid_ref,
    speed_ref,
    edge_ref,
    ghost_ref,
    near_ref,
    neighbours_ref,
    refine_ref,
    planes_ref,
    fine_table,
    packets_ref,
    padded,
    ghost_edges,
    ghost_layers,
    ghost_z_cells,
    layers,
):
    me = lax.axis_index("sfc")
    lane = lanes()
    row = lax.broadcasted_iota(jnp.int32, VEC, 0)
    first_block = (me - REACH) * BLK

    for block in range(BLK):
        place = []
        for k in range(6):
            other = neighbours_ref[block, k]
            place.append(
                jnp.where(
                    other >= 0,
                    jnp.clip(other - first_block, 0, (2 * REACH + 1) * BLK - 1),
                    (2 * REACH + 1) * BLK + block,
                )
            )

        def face(k, item):
            return near_ref[place[k] // BLK, item, place[k] % BLK]

        for field in range(4):
            value = face(5, field)
            for k in (4, 3, 2):
                value = jnp.where(lane < (k - 1) * 32, face(k, field), value)
            ghost_edges[block * 32 + field * 8 : block * 32 + field * 8 + 8, :] = value
        for half in range(2):
            ghost_layers[half, block * 8 : block * 8 + 8, :] = jnp.where(
                row < 4, face(0, 4 + half), face(1, 4 + half)
            )

    for field in range(4):
        for half in range(2):
            for side in range(2):
                start = side * 4352 + half * 128
                padded[field, :, start : start + 128] = ghost_layers[
                    half, pl.ds(side * 4 + field, 8, stride=8), :
                ]
        padded[field, :, 256:4352] = field_rows(fraction_ref, centroid_ref, field, 0, CELLS)

    wide = lax.broadcasted_iota(jnp.int32, (8, 512), 1)
    y_pos = wide // 16 % 16
    z_pos = wide % 16
    z_cells = select(ghost_edges[...], ghost_ref[...])
    for tile in range(4):
        ghost_z_cells[tile] = z_cells[:, tile * 128 : tile * 128 + 128]

    def side_ghosts(ghost):
        shifts = (0, 80, 112, 64)
        return jnp.concatenate([pltpu.roll(ghost, i, 1) if i else ghost for i in shifts], 1)

    def one_pair(pair, carry):
        start = pl.multiple_of(pair * 512, 512)
        fields = [[] for _unused in range(7)]
        for field in range(4):
            center = padded[field, :, pl.ds(start + 256, 512)]
            ghost = ghost_edges[pl.ds(field * 8 + pair, 8, stride=32), :]
            ghost_y = side_ghosts(ghost)
            ghost_z = jnp.concatenate(
                [ghost_z_cells[i, pl.ds(field * 8 + pair, 8, stride=32), :] for i in range(4)], 1
            )
            fields[0].append(center)
            fields[1].append(padded[field, :, pl.ds(start, 512)])
            fields[2].append(padded[field, :, pl.ds(start + 512, 512)])
            fields[3].append(jnp.where(y_pos == 0, ghost_y, pltpu.roll(center, 16, 1)))
            fields[4].append(jnp.where(y_pos == 15, ghost_y, pltpu.roll(center, 496, 1)))
            fields[5].append(jnp.where(z_pos == 0, ghost_z, pltpu.roll(center, 1, 1)))
            fields[6].append(jnp.where(z_pos == 15, ghost_z, pltpu.roll(center, 511, 1)))
        a, b, c = [2.0 * (fields[2 + 2 * i][0] - fields[1 + 2 * i][0]) for i in range(3)]
        frac, cx, cy, cz = fields[0]
        d = 2.0 * (2.0 * frac - 1.0) - a * cx - b * cy - c * cz
        points = [(cx, cy, cz, 2.0 * frac - 1.0)]
        for k in range(6):
            f, *coords = fields[k + 1]
            coords[k // 2] = coords[k // 2] + (2.0 * (k % 2) - 1.0)
            points.append((*coords, 2.0 * f - 1.0))
        params = fit(points, (a, b, c, d))
        for comp in range(4):
            planes_ref[:, comp, pl.ds(start, 512)] = params[comp]
            layers[pl.ds(pl.multiple_of(pair * 32 + comp * 8, 8), 8), :] = params[comp]
        return carry

    lax.fori_loop(0, 8, one_pair, 0)

    edge_values = select(layers[...], edge_ref[:, 128:])
    for pair in range(8):
        for comp in range(4):
            row_at = pair * 32 + comp * 8
            fine_table[pl.ds(comp * 16 + 8 + pair, 8, stride=FINE_ROWS), :] = edge_values[
                row_at : row_at + 8
            ]
    for comp in range(4):
        for part in range(8):
            start = part // 4 * 128
            fine_table[pl.ds(comp * 16 + part, 8, stride=FINE_ROWS), :] = layer_parts(
                layers[comp * 8 : comp * 8 + 8, start : start + 128],
                layers[224 + comp * 8 : 232 + comp * 8, 256 + start : 384 + start],
                part % 4,
            )

    for slot in range(refine_ref.shape[1]):
        block = jnp.clip(refine_ref[0, slot] - me * BLK, 0, BLK - 1)
        k = jnp.clip(refine_ref[1, slot], 0, 5)
        yz = (k >= 2).astype(jnp.int32)
        base = block * FINE_ROWS + yz * 8
        group = k - 2 * yz
        parts = []
        for target in range(3):
            if target < 2:
                comp = (k // 2, 3)[target]
                value = fine_table[pl.ds(pl.multiple_of(base + comp * 16, 8), 8), :]
            else:
                value = speed_ref[pl.ds(pl.multiple_of(block * 16 + yz * 8, 8), 8), :]
            parts.append(pltpu.roll(value, (128 + 32 * target - 32 * group) % 128, 1))
        packets_ref[slot] = jnp.where(
            lane < 32, parts[0], jnp.where(lane < 64, parts[1], parts[2])
        )


def flux_kernel(faces_ref, speed_ref, packets_ref, table_ref, reflux_ref, live_list):
    me = lax.axis_index("sfc")
    lane = lanes()
    row = lax.broadcasted_iota(jnp.int32, VEC, 0)
    pos = lane % 32
    cell = pos % 16 // 2
    slots = packets_ref.shape[1]

    found = 0
    for offset in range(2 * REACH + 1):
        other = me + offset - REACH
        there = (other >= 0) & (other < lax.axis_size("sfc"))

        def collect(slot, found):
            local = table_ref[offset, 2, slot] - me * BLK
            mine = there & (table_ref[offset, 0, slot] >= 0) & (local >= 0) & (local < BLK)
            live_list[found] = offset * slots + slot
            return found + mine.astype(jnp.int32)

        found = lax.fori_loop(0, slots, collect, found, unroll=4 if slots % 4 == 0 else 1)
    for extra in range(3):
        live_list[found + extra] = REACH * slots

    reflux_ref[...] = jnp.zeros_like(reflux_ref)

    offset_one = ((pos // 16).astype(jnp.float32) - 0.5) * 0.5
    offset_two = ((pos % 2).astype(jnp.float32) - 0.5) * 0.5

    def moments(item, weight):
        offset = item // slots
        slot = item % slots
        k = jnp.clip(table_ref[offset, 1, slot], 0, 5)
        block = jnp.clip(table_ref[offset, 2, slot] - me * BLK, 0, BLK - 1)
        quadrant = jnp.clip(table_ref[offset, 3, slot], 0, 3)
        qa, qb = quadrant // 2, quadrant % 2
        facing = k + 1 - 2 * (k % 2)
        axis = k // 2
        sign = (2 * (k % 2) - 1).astype(jnp.float32)
        yz = (k >= 2).astype(jnp.int32)
        from_row = qa * 4 + row // 2
        from_lane = (facing - 2 * yz) * 32 + row % 2 * 16 + qb * 8 + cell
        base = block * FINE_ROWS + yz * 8
        first = jnp.where(axis == 0, 1, 0)
        second = jnp.where(axis == 2, 1, 2)
        sources = [
            faces_ref[pl.ds(pl.multiple_of(base + comp * 16, 8), 8), :]
            for comp in (axis, first, second, 3)
        ]
        sources.append(speed_ref[pl.ds(pl.multiple_of(block * 16 + yz * 8, 8), 8), :])
        normal_c, one_c, two_c, d_c, u_c = [
            take(
                jnp.take_along_axis(source, from_row, axis=0, mode="promise_in_bounds"), from_lane
            )
            for source in sources
        ]
        packet = packets_ref[offset, slot]
        normal_f = packet
        d_f = pltpu.roll(packet, 96, 1)
        u_f = pltpu.roll(packet, 64, 1)
        speed = sign * 0.5 * (u_f + u_c)
        depth = jnp.abs(speed) * TIME_STEP
        outflow = jnp.maximum(speed, 0.0)
        inflow = jnp.minimum(speed, 0.0)
        tangent = one_c * offset_one + two_c * offset_two + d_c
        volume = jnp.zeros(VEC, jnp.float32)
        moment = jnp.zeros(VEC, jnp.float32)
        for node in NODES:
            fine_model = 0.5 * (
                1.0 + jnp.tanh(normal_f * (sign * (0.5 - node * depth)) + d_f)
            )
            coarse_model = 0.5 * (
                1.0 + jnp.tanh(normal_c * (-sign * (0.5 - 0.5 * node * depth)) + tangent)
            )
            volume = volume + 0.5 * TIME_STEP * (outflow * fine_model + inflow * coarse_model)
            moment = moment + 0.5 * TIME_STEP * node * depth * sign * (
                inflow * coarse_model - outflow * fine_model
            )
        both = jnp.where(lane < 32, volume, pltpu.roll(moment, 32, 1))
        both = both + pltpu.roll(both, 127, 1)
        both = both + pltpu.roll(both, 112, 1)
        keep = (lane // 16 == row) & (lane % 16 // 8 == qb) & weight
        rows = []
        for m in range(2):
            placed = jnp.where(keep, take(both, m * 32 + 2 * (lane % 8)), 0.0)
            rows.append(jnp.sum(placed, axis=0, keepdims=True))
        return rows, block, facing, qa

    def group(number, carry):
        results = [
            moments(live_list[number * 4 + i], number * 4 + i < found) for i in range(4)
        ]
        for rows, block, facing, qa in results:
            start = pl.multiple_of(qa * 128, 128)
            for m in range(2):
                reflux_ref[block, facing, m : m + 1, pl.ds(start, 128)] += rows[m]
        return carry

    lax.fori_loop(0, (found + 3) // 4, group, 0)


def spec(space):
    return pl.BlockSpec(memory_space=space)


def per_device(fraction, centroid, velocity, neighbours, refinement):
    count = lax.axis_size("sfc")
    slots = refinement.shape[0]
    pieces = 4 if slots % 4 == 0 else 1
    vmem, smem = spec(pltpu.VMEM), spec(pltpu.SMEM)
    f32 = jnp.float32
    refinement = refinement.T
    centroid, velocity = jnp.swapaxes(centroid, 0, 1), jnp.swapaxes(velocity, 0, 1)
    edge = edge_matrix()
    near, table, speeds = pl.pallas_call(
        lambda *refs: faces_kernel(count, *refs),
        out_shape=(
            jax.ShapeDtypeStruct((7, ITEMS, BLK * 8, 128), f32),
            jax.ShapeDtypeStruct((5, 4, slots), jnp.int32),
            jax.ShapeDtypeStruct((BLK * 16, 128), f32),
        ),
        in_specs=[vmem] * 5,
        out_specs=(vmem,) * 3,
        scratch_shapes=[pltpu.SemaphoreType.DMA((5, ITEMS))] * 2
        + [pltpu.SemaphoreType.DMA((4,))] * 2,
        compiler_params=pltpu.CompilerParams(collective_id=0, has_side_effects=True),
        name="exchange_faces",
    )(fraction, centroid, velocity, refinement, edge)
    planes, faces, packets = pl.pallas_call(
        fit_kernel,
        out_shape=(
            jax.ShapeDtypeStruct((BLK, 4, CELLS), f32),
            jax.ShapeDtypeStruct((BLK * FINE_ROWS, 128), f32),
            jax.ShapeDtypeStruct((slots, 8, 128), f32),
        ),
        in_specs=[vmem] * 6 + [smem] * 2,
        out_specs=(vmem,) * 3,
        scratch_shapes=[
            pltpu.VMEM((4, 8, CELLS + 512), f32),
            pltpu.VMEM((256, 128), f32),
            pltpu.VMEM((2, 64, 128), f32),
            pltpu.VMEM((4, 256, 128), f32),
            pltpu.VMEM((256, 512), f32),
        ],
        name="fit_planes",
    )(
        fraction,
        centroid,
        speeds,
        edge,
        ghost_matrix(),
        near.reshape(7, ITEMS, BLK, 8, 128),
        neighbours,
        refinement,
    )
    near_packets = pl.pallas_call(
        lambda *refs: packets_kernel(count, *refs),
        out_shape=jax.ShapeDtypeStruct((7, pieces, slots // pieces * 8, 128), f32),
        in_specs=[vmem],
        out_specs=vmem,
        scratch_shapes=[pltpu.SemaphoreType.DMA((5, pieces))] * 2,
        compiler_params=pltpu.CompilerParams(collective_id=1, has_side_effects=True),
        name="exchange_packets",
    )(packets.reshape(pieces, slots // pieces * 8, 128))
    reflux = pl.pallas_call(
        flux_kernel,
        out_shape=jax.ShapeDtypeStruct((BLK, 6, 2, 256), f32),
        in_specs=[vmem] * 3 + [smem],
        out_specs=vmem,
        scratch_shapes=[pltpu.SMEM((5 * slots + 4,), jnp.int32)],
        name="reflux_moments",
    )(faces, speeds, near_packets.reshape(7, slots, 8, 128), table)
    return planes, reflux


def solution(mesh):
    return jax.shard_map(
        per_device,
        mesh=mesh,
        in_specs=(
            P("sfc", None),
            P("sfc", None, None),
            P("sfc", None, None),
            P("sfc", None),
            P("sfc", None),
        ),
        out_specs=(P("sfc", None, None), P("sfc", None, None, None)),
        check_vma=False,
    )
```

```python
import jax
import jax.numpy as jnp
import numpy as np
from jax import lax
from jax.experimental import pallas as pl
from jax.experimental.pallas import tpu as pltpu
from jax.sharding import PartitionSpec as P

EDGE = 16
CELLS = 4096
REACH = 2
PASSES = 6
BLK = 8
NODES = (0.5 - 3.0**0.5 / 6.0, 0.5 + 3.0**0.5 / 6.0)
TIME_STEP = 0.25
DAMPING = 0.1
SHIFTS = (1, -1, 2, -2)
VEC = (8, 128)
ITEMS = 6
FINE_ROWS = 4 * 2 * 8


def lanes():
    return lax.broadcasted_iota(jnp.int32, VEC, 1)


def take(values, index):
    return jnp.take_along_axis(values, index, axis=1, mode="promise_in_bounds")


def edge_place(kind, odd, j):
    y, z = ((0, j), (15, j), (j, 0), (j, 15))[kind]
    return odd * 256 + y * 16 + z


def edge_matrix():
    matrix = np.zeros((512, 256), np.float32)
    for lane in range(128):
        kind, odd, j = lane // 32, lane // 16 % 2, lane % 16
        matrix[edge_place(kind + 1 - 2 * (kind % 2), odd, j), lane] = 1
        matrix[edge_place(kind, odd, j), 128 + lane] = 1
    return jnp.asarray(matrix, jnp.bfloat16)


def ghost_matrix():
    matrix = np.zeros((128, 512), np.float32)
    for lane in range(64, 128):
        matrix[lane, edge_place(lane // 32, lane // 16 % 2, lane % 16)] = 1
    return jnp.asarray(matrix, jnp.bfloat16)


def select(values, matrix):
    high = values.astype(jnp.bfloat16)
    rest = values - high.astype(jnp.float32)
    middle = rest.astype(jnp.bfloat16)
    low = (rest - middle.astype(jnp.float32)).astype(jnp.bfloat16)
    parts = [
        jnp.dot(part, matrix, preferred_element_type=jnp.float32) for part in (low, middle, high)
    ]
    return parts[0] + parts[1] + parts[2]


def layer_parts(low, high, part):
    first = low if part == 0 else pltpu.roll(low, 128 - 32 * part, 1)
    second = high if part == 1 else pltpu.roll(high, (160 - 32 * part) % 128, 1)
    return jnp.where(lanes() < 32, first, second)


def field_rows(fraction_ref, centroid_ref, field, start, size):
    if field == 0:
        return fraction_ref[:, pl.ds(start, size)]
    return centroid_ref[field - 1, :, pl.ds(start, size)]


def within(device, count):
    return (device >= 0) & (device < count)


def greet(me, peers):
    barrier = pltpu.get_barrier_semaphore()
    number = 0
    for other, there in peers:

        @pl.when(there)
        def _signal():
            pl.semaphore_signal(
                barrier, inc=1, device_id=(other,), device_id_type=pl.DeviceIdType.MESH
            )

        number = number + there.astype(jnp.int32)
    return barrier, number


def direct_peers(me, count):
    return [(me + shift, within(me + shift, count)) for shift in SHIFTS]


def remote(src, dst, send, recv, other):
    return pltpu.make_async_remote_copy(
        src_ref=src,
        dst_ref=dst,
        send_sem=send,
        recv_sem=recv,
        device_id=(other,),
        device_id_type=pl.DeviceIdType.MESH,
    )


class Direct:
    def __init__(self, me, count, buffer, pieces, send, recv):
        self.me, self.count = me, count
        self.buffer, self.pieces, self.send, self.recv = buffer, pieces, send, recv

    def peers(self):
        return direct_peers(self.me, self.count)

    def copy(self, place, piece):
        shift = SHIFTS[place]
        return remote(
            self.buffer.at[REACH, piece],
            self.buffer.at[REACH - shift, piece],
            self.send.at[place, piece],
            self.recv.at[place, piece],
            self.me + shift,
        )

    def start(self, piece):
        for place, shift in enumerate(SHIFTS):
            pl.when(within(self.me + shift, self.count))(self.copy(place, piece).start)

    def forward(self, piece):
        pass

    def finish(self):
        for piece in self.pieces:
            for place, shift in enumerate(SHIFTS):
                pl.when(within(self.me + shift, self.count))(self.copy(place, piece).wait_send)
                pl.when(within(self.me - shift, self.count))(self.copy(place, piece).wait_recv)


class Relay:
    def __init__(self, me, count, buffer, pieces, send, recv):
        self.me, self.buffer, self.pieces, self.send, self.recv = me, buffer, pieces, send, recv
        core, x, y = me % 2, me // 2 % 2, me // 4 % 2
        unlike = (x + y) % 2
        self.x, self.core = x, core
        spare = 2 * REACH + 2
        self.by_z = unlike == 0
        z_to, z_from = me + 8 - 16 * x, me - 8 + 16 * x
        self.z_send = self.by_z & within(z_to, count)
        self.z_recv = self.by_z & within(z_from, count)
        self.second = (unlike == 1) | within(z_from, count)
        self.others = [(me + 4 - 8 * y, me >= 0)] + [
            (me + shift, self.by_z & within(me + shift, count)) for shift in (8, -8)
        ]
        y_there = unlike * spare + (1 - unlike) * 4 * x
        y_here = (1 - unlike) * spare + unlike * 4 * x
        self.steps = (
            (me + 2 - 4 * x, REACH, 4 * x, 4 * (1 - x)),
            (me + 1 - 2 * core, REACH, 1 + 2 * core, 3 - 2 * core),
            (me + 4 - 8 * y, 4 * (1 - x), y_there, y_here),
            (z_to, spare, 4 * x, 4 * x),
            (me + 1 - 2 * core, 4 * (1 - core), 3 - 2 * core, 1 + 2 * core),
        )

    def peers(self):
        near = [(self.steps[0][0], self.me >= 0), (self.steps[1][0], self.me >= 0)]
        return near + self.others

    def sent(self, step, piece):
        other, source, there, _here = self.steps[step]
        return remote(
            self.buffer.at[source, piece],
            self.buffer.at[there, piece],
            self.send.at[step, piece],
            self.recv.at[step, piece],
            other,
        )

    def arrived(self, step, piece):
        other, source, _there, here = self.steps[step]
        return remote(
            self.buffer.at[source, piece],
            self.buffer.at[here, piece],
            self.send.at[step, piece],
            self.recv.at[step, piece],
            other,
        )

    def start(self, piece):
        self.sent(0, piece).start()

    def forward(self, piece):
        at = self.pieces.index(piece)
        self.hand_on(at, at - 1, at - 2)

    def hand_on(self, by_x, by_y, by_z):
        late = self.x != self.core
        if 0 <= by_x < len(self.pieces):
            piece = self.pieces[by_x]
            self.arrived(0, piece).wait_recv()
            self.sent(2, piece).start()
            pl.when(jnp.logical_not(late))(self.sent(4, piece).start)
            self.sent(1, piece).start()
        if 0 <= by_y < len(self.pieces):
            piece = self.pieces[by_y]
            self.arrived(2, piece).wait_recv()
            pl.when(self.z_send)(self.sent(3, piece).start)
            pl.when(jnp.logical_not(self.by_z) & late)(self.sent(4, piece).start)
        if 0 <= by_z < len(self.pieces):
            piece = self.pieces[by_z]

            @pl.when(self.z_recv)
            def _last():
                self.arrived(3, piece).wait_recv()
                pl.when(late)(self.sent(4, piece).start)

    def finish(self):
        late = self.x != self.core
        for at in range(len(self.pieces), len(self.pieces) + 2):
            self.hand_on(at, at - 1, at - 2)
        for piece in self.pieces:
            self.arrived(1, piece).wait_recv()
            pl.when(self.second | late)(self.arrived(4, piece).wait_recv)
            for step in range(3):
                self.sent(step, piece).wait_send()
            pl.when(self.z_send)(self.sent(3, piece).wait_send)
            pl.when(self.second | jnp.logical_not(late))(self.sent(4, piece).wait_send)


def way(count):
    return Relay if count == 32 else Direct


def faces_kernel(
    count,
    fraction_ref,
    centroid_ref,
    velocity_ref,
    refine_ref,
    edge_ref,
    near_ref,
    table_ref,
    speed_ref,
    send,
    recv,
    send2,
    recv2,
):
    me = lax.axis_index("sfc")
    order = (4, 5, 0, 1, 2, 3)
    faces = way(count)(me, count, near_ref, order, send, recv)
    peers = direct_peers(me, count)
    if count == 32:
        peers = peers + faces.others
    barrier, number = greet(me, peers)

    def extract_layers(slot, item, swap):
        for side in range(2):
            start = (1 - side if swap else side) * 3840 + (item - 4) * 128
            for field in range(4):
                near_ref[slot, item, pl.ds(side * 4 + field, 8, stride=8), :] = field_rows(
                    fraction_ref, centroid_ref, field, start, 128
                )

    extract_layers(REACH, 4, True)
    extract_layers(REACH, 5, True)
    pl.semaphore_wait(barrier, number)
    faces.start(4)
    faces.start(5)
    both = select(
        jnp.concatenate(
            [
                field_rows(fraction_ref, centroid_ref, field, pair * 512, 512)
                for field in range(4)
                for pair in range(8)
            ],
            0,
        ),
        edge_ref[...],
    )

    def put(slot, field, start):
        for pair in range(8):
            row = field * 64 + pair * 8
            near_ref[slot, field, pl.ds(pair, 8, stride=8), :] = both[
                row : row + 8, start : start + 128
            ]

    for field in range(4):
        put(REACH, field, 0)
        faces.start(field)

    def table_copy(place):
        shift = SHIFTS[place]
        return remote(
            refine_ref, table_ref.at[REACH - shift], send2.at[place], recv2.at[place], me + shift
        )

    table_ref[REACH] = refine_ref[...]
    for place, shift in enumerate(SHIFTS):
        pl.when(within(me + shift, count))(table_copy(place).start)

    for field in range(4):
        put(2 * REACH + 1, field, 128)
    extract_layers(2 * REACH + 1, 4, False)
    extract_layers(2 * REACH + 1, 5, False)
    faces.forward(4)
    faces.forward(5)
    faces.forward(0)
    speeds = select(
        jnp.concatenate(
            [velocity_ref[axis, :, pl.ds(pair * 512, 512)] for axis in (1, 2) for pair in range(8)],
            0,
        ),
        edge_ref[:, 128:],
    )
    for pair in range(8):
        speed_ref[pl.ds(8 + pair, 8, stride=16), :] = jnp.where(
            lanes() < 64, speeds[pair * 8 : pair * 8 + 8], speeds[64 + pair * 8 : 72 + pair * 8]
        )
    faces.forward(1)
    for part in range(8):
        start = part // 4 * 128
        speed_ref[pl.ds(part, 8, stride=16), :] = layer_parts(
            velocity_ref[0, :, start : start + 128],
            velocity_ref[0, :, 3840 + start : 3968 + start],
            part % 4,
        )
    faces.forward(2)
    faces.forward(3)
    faces.finish()
    for place, shift in enumerate(SHIFTS):
        pl.when(within(me + shift, count))(table_copy(place).wait_send)
        pl.when(within(me - shift, count))(table_copy(place).wait_recv)


def packets_kernel(count, own_ref, near_ref, send, recv):
    me = lax.axis_index("sfc")
    pieces = range(own_ref.shape[0])
    packets = Direct(me, count, near_ref, pieces, send, recv)
    barrier, number = greet(me, packets.peers())
    near_ref[REACH] = own_ref[...]
    pl.semaphore_wait(barrier, number)
    for piece in pieces:
        packets.start(piece)
    for piece in pieces:
        packets.forward(piece)
    packets.finish()


def solve(h, g):
    (h00, h01, h02, h03, h11, h12, h13, h22, h23, h33) = h
    i0 = 1.0 / h00
    l10, l20, l30 = h01 * i0, h02 * i0, h03 * i0
    d1 = h11 - l10 * h01
    a21, a31 = h12 - l10 * h02, h13 - l10 * h03
    i1 = 1.0 / d1
    l21, l31 = a21 * i1, a31 * i1
    d2 = h22 - l20 * h02 - l21 * a21
    a32 = h23 - l20 * h03 - l21 * a31
    i2 = 1.0 / d2
    l32 = a32 * i2
    d3 = h33 - l30 * h03 - l31 * a31 - l32 * a32
    y1 = g[1] - l10 * g[0]
    y2 = g[2] - l20 * g[0] - l21 * y1
    y3 = g[3] - l30 * g[0] - l31 * y1 - l32 * y2
    x3 = y3 / d3
    x2 = y2 * i2 - l32 * x3
    x1 = y1 * i1 - l21 * x2 - l31 * x3
    x0 = g[0] * i0 - l10 * x1 - l20 * x2 - l30 * x3
    return x0, x1, x2, x3


def fit(points, params):
    width = 256

    def normal_equations(start, params):
        a, b, c, d = [p[:, start : start + width] for p in params]
        h = [None] * 10
        g = [None] * 4

        def add(total, place, term):
            total[place] = term if total[place] is None else total[place] + term

        for point in points:
            px, py, pz, f = [value[:, start : start + width] for value in point]
            t = jnp.tanh(a * px + b * py + c * pz + d)
            s = 1.0 - t * t
            q = s * s
            w = s * (t - f)
            qx, qy, qz = q * px, q * py, q * pz
            for place, term in enumerate(
                (qx * px, qx * py, qx * pz, qx, qy * py, qy * pz, qy, qz * pz, qz, q)
            ):
                add(h, place, term)
            for place, term in enumerate((w * px, w * py, w * pz, w)):
                add(g, place, term)
        for place in (0, 4, 7, 9):
            h[place] = h[place] + 4.0 * DAMPING
        return h + g

    def one_pass(_unused, params):
        parts = [normal_equations(start, params) for start in range(0, 512, width)]
        sums = [jnp.concatenate(part, 1) for part in zip(*parts)]
        step = solve(sums[:10], sums[10:])
        return tuple(p - s for p, s in zip(params, step))

    return lax.fori_loop(0, PASSES, one_pass, params)


def fit_kernel(
    fraction_ref,
    centroid_ref,
    speed_ref,
    edge_ref,
    ghost_ref,
    near_ref,
    neighbours_ref,
    refine_ref,
    planes_ref,
    fine_table,
    packets_ref,
    padded,
    ghost_edges,
    ghost_layers,
    ghost_z_cells,
    layers,
):
    me = lax.axis_index("sfc")
    lane = lanes()
    row = lax.broadcasted_iota(jnp.int32, VEC, 0)
    first_block = (me - REACH) * BLK

    for block in range(BLK):
        place = []
        for k in range(6):
            other = neighbours_ref[block, k]
            place.append(
                jnp.where(
                    other >= 0,
                    jnp.clip(other - first_block, 0, (2 * REACH + 1) * BLK - 1),
                    (2 * REACH + 1) * BLK + block,
                )
            )

        def face(k, item):
            return near_ref[place[k] // BLK, item, place[k] % BLK]

        for field in range(4):
            value = face(5, field)
            for k in (4, 3, 2):
                value = jnp.where(lane < (k - 1) * 32, face(k, field), value)
            ghost_edges[block * 32 + field * 8 : block * 32 + field * 8 + 8, :] = value
        for half in range(2):
            ghost_layers[half, block * 8 : block * 8 + 8, :] = jnp.where(
                row < 4, face(0, 4 + half), face(1, 4 + half)
            )

    for field in range(4):
        for half in range(2):
            for side in range(2):
                start = side * 4352 + half * 128
                padded[field, :, start : start + 128] = ghost_layers[
                    half, pl.ds(side * 4 + field, 8, stride=8), :
                ]
        padded[field, :, 256:4352] = field_rows(fraction_ref, centroid_ref, field, 0, CELLS)

    wide = lax.broadcasted_iota(jnp.int32, (8, 512), 1)
    y_pos = wide // 16 % 16
    z_pos = wide % 16
    z_cells = select(ghost_edges[...], ghost_ref[...])
    for tile in range(4):
        ghost_z_cells[tile] = z_cells[:, tile * 128 : tile * 128 + 128]

    def side_ghosts(ghost):
        shifts = (0, 80, 112, 64)
        return jnp.concatenate([pltpu.roll(ghost, i, 1) if i else ghost for i in shifts], 1)

    def one_pair(pair, carry):
        start = pl.multiple_of(pair * 512, 512)
        fields = [[] for _unused in range(7)]
        for field in range(4):
            center = padded[field, :, pl.ds(start + 256, 512)]
            ghost = ghost_edges[pl.ds(field * 8 + pair, 8, stride=32), :]
            ghost_y = side_ghosts(ghost)
            ghost_z = jnp.concatenate(
                [ghost_z_cells[i, pl.ds(field * 8 + pair, 8, stride=32), :] for i in range(4)], 1
            )
            fields[0].append(center)
            fields[1].append(padded[field, :, pl.ds(start, 512)])
            fields[2].append(padded[field, :, pl.ds(start + 512, 512)])
            fields[3].append(jnp.where(y_pos == 0, ghost_y, pltpu.roll(center, 16, 1)))
            fields[4].append(jnp.where(y_pos == 15, ghost_y, pltpu.roll(center, 496, 1)))
            fields[5].append(jnp.where(z_pos == 0, ghost_z, pltpu.roll(center, 1, 1)))
            fields[6].append(jnp.where(z_pos == 15, ghost_z, pltpu.roll(center, 511, 1)))
        a, b, c = [2.0 * (fields[2 + 2 * i][0] - fields[1 + 2 * i][0]) for i in range(3)]
        frac, cx, cy, cz = fields[0]
        d = 2.0 * (2.0 * frac - 1.0) - a * cx - b * cy - c * cz
        points = [(cx, cy, cz, 2.0 * frac - 1.0)]
        for k in range(6):
            f, *coords = fields[k + 1]
            coords[k // 2] = coords[k // 2] + (2.0 * (k % 2) - 1.0)
            points.append((*coords, 2.0 * f - 1.0))
        params = fit(points, (a, b, c, d))
        for comp in range(4):
            planes_ref[:, comp, pl.ds(start, 512)] = params[comp]
            layers[pl.ds(pl.multiple_of(pair * 32 + comp * 8, 8), 8), :] = params[comp]
        return carry

    lax.fori_loop(0, 8, one_pair, 0)

    edge_values = select(layers[...], edge_ref[:, 128:])
    for pair in range(8):
        for comp in range(4):
            row_at = pair * 32 + comp * 8
            fine_table[pl.ds(comp * 16 + 8 + pair, 8, stride=FINE_ROWS), :] = edge_values[
                row_at : row_at + 8
            ]
    for comp in range(4):
        for part in range(8):
            start = part // 4 * 128
            fine_table[pl.ds(comp * 16 + part, 8, stride=FINE_ROWS), :] = layer_parts(
                layers[comp * 8 : comp * 8 + 8, start : start + 128],
                layers[224 + comp * 8 : 232 + comp * 8, 256 + start : 384 + start],
                part % 4,
            )

    for slot in range(refine_ref.shape[1]):
        block = jnp.clip(refine_ref[0, slot] - me * BLK, 0, BLK - 1)
        k = jnp.clip(refine_ref[1, slot], 0, 5)
        yz = (k >= 2).astype(jnp.int32)
        base = block * FINE_ROWS + yz * 8
        group = k - 2 * yz
        parts = []
        for target in range(3):
            if target < 2:
                comp = (k // 2, 3)[target]
                value = fine_table[pl.ds(pl.multiple_of(base + comp * 16, 8), 8), :]
            else:
                value = speed_ref[pl.ds(pl.multiple_of(block * 16 + yz * 8, 8), 8), :]
            parts.append(pltpu.roll(value, (128 + 32 * target - 32 * group) % 128, 1))
        packets_ref[slot] = jnp.where(
            lane < 32, parts[0], jnp.where(lane < 64, parts[1], parts[2])
        )


def flux_kernel(faces_ref, speed_ref, packets_ref, table_ref, reflux_ref, live_list):
    me = lax.axis_index("sfc")
    lane = lanes()
    row = lax.broadcasted_iota(jnp.int32, VEC, 0)
    pos = lane % 32
    cell = pos % 16 // 2
    slots = packets_ref.shape[1]

    found = 0
    for offset in range(2 * REACH + 1):
        other = me + offset - REACH
        there = (other >= 0) & (other < lax.axis_size("sfc"))

        def collect(slot, found):
            local = table_ref[offset, 2, slot] - me * BLK
            mine = there & (table_ref[offset, 0, slot] >= 0) & (local >= 0) & (local < BLK)
            live_list[found] = offset * slots + slot
            return found + mine.astype(jnp.int32)

        found = lax.fori_loop(0, slots, collect, found, unroll=4 if slots % 4 == 0 else 1)
    for extra in range(3):
        live_list[found + extra] = REACH * slots

    reflux_ref[...] = jnp.zeros_like(reflux_ref)

    offset_one = ((pos // 16).astype(jnp.float32) - 0.5) * 0.5
    offset_two = ((pos % 2).astype(jnp.float32) - 0.5) * 0.5

    def moments(item, weight):
        offset = item // slots
        slot = item % slots
        k = jnp.clip(table_ref[offset, 1, slot], 0, 5)
        block = jnp.clip(table_ref[offset, 2, slot] - me * BLK, 0, BLK - 1)
        quadrant = jnp.clip(table_ref[offset, 3, slot], 0, 3)
        qa, qb = quadrant // 2, quadrant % 2
        facing = k + 1 - 2 * (k % 2)
        axis = k // 2
        sign = (2 * (k % 2) - 1).astype(jnp.float32)
        yz = (k >= 2).astype(jnp.int32)
        from_row = qa * 4 + row // 2
        from_lane = (facing - 2 * yz) * 32 + row % 2 * 16 + qb * 8 + cell
        base = block * FINE_ROWS + yz * 8
        first = jnp.where(axis == 0, 1, 0)
        second = jnp.where(axis == 2, 1, 2)
        sources = [
            faces_ref[pl.ds(pl.multiple_of(base + comp * 16, 8), 8), :]
            for comp in (axis, first, second, 3)
        ]
        sources.append(speed_ref[pl.ds(pl.multiple_of(block * 16 + yz * 8, 8), 8), :])
        normal_c, one_c, two_c, d_c, u_c = [
            take(
                jnp.take_along_axis(source, from_row, axis=0, mode="promise_in_bounds"), from_lane
            )
            for source in sources
        ]
        packet = packets_ref[offset, slot]
        normal_f = packet
        d_f = pltpu.roll(packet, 96, 1)
        u_f = pltpu.roll(packet, 64, 1)
        speed = sign * 0.5 * (u_f + u_c)
        depth = jnp.abs(speed) * TIME_STEP
        outflow = jnp.maximum(speed, 0.0)
        inflow = jnp.minimum(speed, 0.0)
        tangent = one_c * offset_one + two_c * offset_two + d_c
        volume = jnp.zeros(VEC, jnp.float32)
        moment = jnp.zeros(VEC, jnp.float32)
        for node in NODES:
            fine_model = 0.5 * (
                1.0 + jnp.tanh(normal_f * (sign * (0.5 - node * depth)) + d_f)
            )
            coarse_model = 0.5 * (
                1.0 + jnp.tanh(normal_c * (-sign * (0.5 - 0.5 * node * depth)) + tangent)
            )
            volume = volume + 0.5 * TIME_STEP * (outflow * fine_model + inflow * coarse_model)
            moment = moment + 0.5 * TIME_STEP * node * depth * sign * (
                inflow * coarse_model - outflow * fine_model
            )
        both = jnp.where(lane < 32, volume, pltpu.roll(moment, 32, 1))
        both = both + pltpu.roll(both, 127, 1)
        both = both + pltpu.roll(both, 112, 1)
        keep = (lane // 16 == row) & (lane % 16 // 8 == qb) & weight
        rows = []
        for m in range(2):
            placed = jnp.where(keep, take(both, m * 32 + 2 * (lane % 8)), 0.0)
            rows.append(jnp.sum(placed, axis=0, keepdims=True))
        return rows, block, facing, qa

    def group(number, carry):
        results = [
            moments(live_list[number * 4 + i], number * 4 + i < found) for i in range(4)
        ]
        for rows, block, facing, qa in results:
            start = pl.multiple_of(qa * 128, 128)
            for m in range(2):
                reflux_ref[block, facing, m : m + 1, pl.ds(start, 128)] += rows[m]
        return carry

    lax.fori_loop(0, (found + 3) // 4, group, 0)


def spec(space):
    return pl.BlockSpec(memory_space=space)


def per_device(fraction, centroid, velocity, neighbours, refinement):
    count = lax.axis_size("sfc")
    slots = refinement.shape[0]
    pieces = 4 if slots % 4 == 0 else 1
    vmem, smem = spec(pltpu.VMEM), spec(pltpu.SMEM)
    f32 = jnp.float32
    refinement = refinement.T
    centroid, velocity = jnp.swapaxes(centroid, 0, 1), jnp.swapaxes(velocity, 0, 1)
    edge = edge_matrix()
    near, table, speeds = pl.pallas_call(
        lambda *refs: faces_kernel(count, *refs),
        out_shape=(
            jax.ShapeDtypeStruct((7, ITEMS, BLK * 8, 128), f32),
            jax.ShapeDtypeStruct((5, 4, slots), jnp.int32),
            jax.ShapeDtypeStruct((BLK * 16, 128), f32),
        ),
        in_specs=[vmem] * 5,
        out_specs=(vmem,) * 3,
        scratch_shapes=[pltpu.SemaphoreType.DMA((5, ITEMS))] * 2
        + [pltpu.SemaphoreType.DMA((4,))] * 2,
        compiler_params=pltpu.CompilerParams(collective_id=0, has_side_effects=True),
        name="exchange_faces",
    )(fraction, centroid, velocity, refinement, edge)
    planes, faces, packets = pl.pallas_call(
        fit_kernel,
        out_shape=(
            jax.ShapeDtypeStruct((BLK, 4, CELLS), f32),
            jax.ShapeDtypeStruct((BLK * FINE_ROWS, 128), f32),
            jax.ShapeDtypeStruct((slots, 8, 128), f32),
        ),
        in_specs=[vmem] * 6 + [smem] * 2,
        out_specs=(vmem,) * 3,
        scratch_shapes=[
            pltpu.VMEM((4, 8, CELLS + 512), f32),
            pltpu.VMEM((256, 128), f32),
            pltpu.VMEM((2, 64, 128), f32),
            pltpu.VMEM((4, 256, 128), f32),
            pltpu.VMEM((256, 512), f32),
        ],
        name="fit_planes",
    )(
        fraction,
        centroid,
        speeds,
        edge,
        ghost_matrix(),
        near.reshape(7, ITEMS, BLK, 8, 128),
        neighbours,
        refinement,
    )
    near_packets = pl.pallas_call(
        lambda *refs: packets_kernel(count, *refs),
        out_shape=jax.ShapeDtypeStruct((7, pieces, slots // pieces * 8, 128), f32),
        in_specs=[vmem],
        out_specs=vmem,
        scratch_shapes=[pltpu.SemaphoreType.DMA((5, pieces))] * 2,
        compiler_params=pltpu.CompilerParams(collective_id=1, has_side_effects=True),
        name="exchange_packets",
    )(packets.reshape(pieces, slots // pieces * 8, 128))
    reflux = pl.pallas_call(
        flux_kernel,
        out_shape=jax.ShapeDtypeStruct((BLK, 6, 2, 256), f32),
        in_specs=[vmem] * 3 + [smem],
        out_specs=vmem,
        scratch_shapes=[pltpu.SMEM((5 * slots + 4,), jnp.int32)],
        name="reflux_moments",
    )(faces, speeds, near_packets.reshape(7, slots, 8, 128), table)
    return planes, reflux


def solution(mesh):
    return jax.shard_map(
        per_device,
        mesh=mesh,
        in_specs=(
            P("sfc", None),
            P("sfc", None, None),
            P("sfc", None, None),
            P("sfc", None),
            P("sfc", None),
        ),
        out_specs=(P("sfc", None, None), P("sfc", None, None, None)),
        check_vma=False,
    )
```

```python
import jax
import jax.numpy as jnp
import numpy as np
from jax import lax
from jax.experimental import pallas as pl
from jax.experimental.pallas import tpu as pltpu
from jax.sharding import PartitionSpec as P

EDGE = 16
CELLS = 4096
REACH = 2
PASSES = 6
BLK = 8
NODES = (0.5 - 3.0**0.5 / 6.0, 0.5 + 3.0**0.5 / 6.0)
TIME_STEP = 0.25
DAMPING = 0.1
SHIFTS = (1, -1, 2, -2)
VEC = (8, 128)
ITEMS = 6
FINE_ROWS = 4 * 2 * 8


def lanes():
    return lax.broadcasted_iota(jnp.int32, VEC, 1)


def take(values, index):
    return jnp.take_along_axis(values, index, axis=1, mode="promise_in_bounds")


def edge_place(kind, odd, j):
    y, z = ((0, j), (15, j), (j, 0), (j, 15))[kind]
    return odd * 256 + y * 16 + z


def edge_matrix():
    matrix = np.zeros((512, 256), np.float32)
    for lane in range(128):
        kind, odd, j = lane // 32, lane // 16 % 2, lane % 16
        matrix[edge_place(kind + 1 - 2 * (kind % 2), odd, j), lane] = 1
        matrix[edge_place(kind, odd, j), 128 + lane] = 1
    return jnp.asarray(matrix, jnp.bfloat16)


def ghost_matrix():
    matrix = np.zeros((128, 512), np.float32)
    for lane in range(64, 128):
        matrix[lane, edge_place(lane // 32, lane // 16 % 2, lane % 16)] = 1
    return jnp.asarray(matrix, jnp.bfloat16)


def select(values, matrix):
    high = values.astype(jnp.bfloat16)
    rest = values - high.astype(jnp.float32)
    middle = rest.astype(jnp.bfloat16)
    low = (rest - middle.astype(jnp.float32)).astype(jnp.bfloat16)
    parts = [
        jnp.dot(part, matrix, preferred_element_type=jnp.float32) for part in (low, middle, high)
    ]
    return parts[0] + parts[1] + parts[2]


def layer_parts(low, high, part):
    first = low if part == 0 else pltpu.roll(low, 128 - 32 * part, 1)
    second = high if part == 1 else pltpu.roll(high, (160 - 32 * part) % 128, 1)
    return jnp.where(lanes() < 32, first, second)


def field_rows(fraction_ref, centroid_ref, field, start, size):
    if field == 0:
        return fraction_ref[:, pl.ds(start, size)]
    return centroid_ref[field - 1, :, pl.ds(start, size)]


def within(device, count):
    return (device >= 0) & (device < count)


def greet(me, peers):
    barrier = pltpu.get_barrier_semaphore()
    number = 0
    for other, there in peers:

        @pl.when(there)
        def _signal():
            pl.semaphore_signal(
                barrier, inc=1, device_id=(other,), device_id_type=pl.DeviceIdType.MESH
            )

        number = number + there.astype(jnp.int32)
    return barrier, number


def direct_peers(me, count):
    return [(me + shift, within(me + shift, count)) for shift in SHIFTS]


def remote(src, dst, send, recv, other):
    return pltpu.make_async_remote_copy(
        src_ref=src,
        dst_ref=dst,
        send_sem=send,
        recv_sem=recv,
        device_id=(other,),
        device_id_type=pl.DeviceIdType.MESH,
    )


class Direct:
    def __init__(self, me, count, buffer, pieces, send, recv):
        self.me, self.count = me, count
        self.buffer, self.pieces, self.send, self.recv = buffer, pieces, send, recv

    def peers(self):
        return direct_peers(self.me, self.count)

    def copy(self, place, piece):
        shift = SHIFTS[place]
        return remote(
            self.buffer.at[REACH, piece],
            self.buffer.at[REACH - shift, piece],
            self.send.at[place, piece],
            self.recv.at[place, piece],
            self.me + shift,
        )

    def start(self, piece):
        for place, shift in enumerate(SHIFTS):
            pl.when(within(self.me + shift, self.count))(self.copy(place, piece).start)

    def finish(self):
        for piece in self.pieces:
            for place, shift in enumerate(SHIFTS):
                pl.when(within(self.me + shift, self.count))(self.copy(place, piece).wait_send)
                pl.when(within(self.me - shift, self.count))(self.copy(place, piece).wait_recv)


class Relay:
    def __init__(self, me, count, buffer, pieces, send, recv):
        self.buffer, self.pieces, self.send, self.recv = buffer, pieces, send, recv
        core, x = me % 2, me // 2 % 2
        to, origin = me + 4 - 8 * x, me - 4 + 8 * x
        self.late = x != core
        self.onward, self.second = within(to, count), within(origin, count)
        self.others = [(me + shift, within(me + shift, count)) for shift in (4, -4)]
        self.steps = (
            (me + 2 - 4 * x, REACH, 4 * x, 4 * (1 - x)),
            (me + 1 - 2 * core, REACH, 1 + 2 * core, 3 - 2 * core),
            (to, 4 * (1 - x), 4 * x, 4 * x),
            (me + 1 - 2 * core, 4 * (1 - core), 3 - 2 * core, 1 + 2 * core),
        )

    def copy(self, step, piece, arrived):
        other, source, there, here = self.steps[step]
        return remote(
            self.buffer.at[source, piece],
            self.buffer.at[here if arrived else there, piece],
            self.send.at[step, piece],
            self.recv.at[step, piece],
            other,
        )

    def sent(self, step, piece):
        return self.copy(step, piece, False)

    def arrived(self, step, piece):
        return self.copy(step, piece, True)

    def start(self, piece):
        self.sent(0, piece).start()

    def forward(self, piece):
        self.arrived(0, piece).wait_recv()
        pl.when(self.onward)(self.sent(2, piece).start)
        pl.when(jnp.logical_not(self.late))(self.sent(3, piece).start)
        self.sent(1, piece).start()

    def finish(self):
        for piece in self.pieces:

            @pl.when(self.second)
            def _second():
                self.arrived(2, piece).wait_recv()
                pl.when(self.late)(self.sent(3, piece).start)

        for piece in self.pieces:
            self.arrived(1, piece).wait_recv()
            pl.when(self.second | self.late)(self.arrived(3, piece).wait_recv)
            self.sent(0, piece).wait_send()
            self.sent(1, piece).wait_send()
            pl.when(self.onward)(self.sent(2, piece).wait_send)
            pl.when(self.second | jnp.logical_not(self.late))(self.sent(3, piece).wait_send)


def faces_kernel(
    count,
    fraction_ref,
    centroid_ref,
    velocity_ref,
    refine_ref,
    edge_ref,
    near_ref,
    table_ref,
    speed_ref,
    send,
    recv,
    send2,
    recv2,
):
    me = lax.axis_index("sfc")
    order = (4, 5, 0, 1, 2, 3)
    faces = Relay(me, count, near_ref, order, send, recv)
    barrier, number = greet(me, direct_peers(me, count) + faces.others)

    def extract_layers(slot, item, swap):
        for side in range(2):
            start = (1 - side if swap else side) * 3840 + (item - 4) * 128
            for field in range(4):
                near_ref[slot, item, pl.ds(side * 4 + field, 8, stride=8), :] = field_rows(
                    fraction_ref, centroid_ref, field, start, 128
                )

    extract_layers(REACH, 4, True)
    extract_layers(REACH, 5, True)
    pl.semaphore_wait(barrier, number)
    faces.start(4)
    faces.start(5)
    both = select(
        jnp.concatenate(
            [
                field_rows(fraction_ref, centroid_ref, field, pair * 512, 512)
                for field in range(4)
                for pair in range(8)
            ],
            0,
        ),
        edge_ref[...],
    )

    def put(slot, field, start):
        for pair in range(8):
            row = field * 64 + pair * 8
            near_ref[slot, field, pl.ds(pair, 8, stride=8), :] = both[
                row : row + 8, start : start + 128
            ]

    for field in range(4):
        put(REACH, field, 0)
        faces.start(field)

    def table_copy(place):
        shift = SHIFTS[place]
        return remote(
            refine_ref, table_ref.at[REACH - shift], send2.at[place], recv2.at[place], me + shift
        )

    table_ref[REACH] = refine_ref[...]
    for place, shift in enumerate(SHIFTS):
        pl.when(within(me + shift, count))(table_copy(place).start)

    for field in range(4):
        put(2 * REACH + 1, field, 128)
    extract_layers(2 * REACH + 1, 4, False)
    extract_layers(2 * REACH + 1, 5, False)
    faces.forward(4)
    faces.forward(5)
    faces.forward(0)
    speeds = select(
        jnp.concatenate(
            [velocity_ref[axis, :, pl.ds(pair * 512, 512)] for axis in (1, 2) for pair in range(8)],
            0,
        ),
        edge_ref[:, 128:],
    )
    for pair in range(8):
        speed_ref[pl.ds(8 + pair, 8, stride=16), :] = jnp.where(
            lanes() < 64, speeds[pair * 8 : pair * 8 + 8], speeds[64 + pair * 8 : 72 + pair * 8]
        )
    faces.forward(1)
    for part in range(8):
        start = part // 4 * 128
        speed_ref[pl.ds(part, 8, stride=16), :] = layer_parts(
            velocity_ref[0, :, start : start + 128],
            velocity_ref[0, :, 3840 + start : 3968 + start],
            part % 4,
        )
    faces.forward(2)
    faces.forward(3)
    faces.finish()
    for place, shift in enumerate(SHIFTS):
        pl.when(within(me + shift, count))(table_copy(place).wait_send)
        pl.when(within(me - shift, count))(table_copy(place).wait_recv)


def packets_kernel(count, own_ref, near_ref, send, recv):
    me = lax.axis_index("sfc")
    pieces = range(own_ref.shape[0])
    packets = Direct(me, count, near_ref, pieces, send, recv)
    barrier, number = greet(me, packets.peers())
    near_ref[REACH] = own_ref[...]
    pl.semaphore_wait(barrier, number)
    for piece in pieces:
        packets.start(piece)
    packets.finish()


def solve(h, g):
    (h00, h01, h02, h03, h11, h12, h13, h22, h23, h33) = h
    i0 = 1.0 / h00
    l10, l20, l30 = h01 * i0, h02 * i0, h03 * i0
    d1 = h11 - l10 * h01
    a21, a31 = h12 - l10 * h02, h13 - l10 * h03
    i1 = 1.0 / d1
    l21, l31 = a21 * i1, a31 * i1
    d2 = h22 - l20 * h02 - l21 * a21
    a32 = h23 - l20 * h03 - l21 * a31
    i2 = 1.0 / d2
    l32 = a32 * i2
    d3 = h33 - l30 * h03 - l31 * a31 - l32 * a32
    y1 = g[1] - l10 * g[0]
    y2 = g[2] - l20 * g[0] - l21 * y1
    y3 = g[3] - l30 * g[0] - l31 * y1 - l32 * y2
    x3 = y3 / d3
    x2 = y2 * i2 - l32 * x3
    x1 = y1 * i1 - l21 * x2 - l31 * x3
    x0 = g[0] * i0 - l10 * x1 - l20 * x2 - l30 * x3
    return x0, x1, x2, x3


def fit(points, params):
    width = 128

    def normal_equations(start, params):
        a, b, c, d = [p[:, start : start + width] for p in params]
        h = [None] * 10
        g = [None] * 4

        def add(total, place, term):
            total[place] = term if total[place] is None else total[place] + term

        for point in points:
            px, py, pz, f = [value[:, start : start + width] for value in point]
            t = jnp.tanh(a * px + b * py + c * pz + d)
            s = 1.0 - t * t
            q = s * s
            w = s * (t - f)
            qx, qy, qz = q * px, q * py, q * pz
            for place, term in enumerate(
                (qx * px, qx * py, qx * pz, qx, qy * py, qy * pz, qy, qz * pz, qz, q)
            ):
                add(h, place, term)
            for place, term in enumerate((w * px, w * py, w * pz, w)):
                add(g, place, term)
        for place in (0, 4, 7, 9):
            h[place] = h[place] + 4.0 * DAMPING
        return h + g

    def one_pass(_unused, params):
        parts = [normal_equations(start, params) for start in range(0, 512, width)]
        sums = [jnp.concatenate(part, 1) for part in zip(*parts)]
        step = solve(sums[:10], sums[10:])
        return tuple(p - s for p, s in zip(params, step))

    return lax.fori_loop(0, PASSES, one_pass, params)


def fit_kernel(
    fraction_ref,
    centroid_ref,
    speed_ref,
    edge_ref,
    ghost_ref,
    near_ref,
    neighbours_ref,
    refine_ref,
    planes_ref,
    fine_table,
    packets_ref,
    padded,
    ghost_edges,
    ghost_layers,
    ghost_z_cells,
    layers,
):
    me = lax.axis_index("sfc")
    lane = lanes()
    row = lax.broadcasted_iota(jnp.int32, VEC, 0)
    first_block = (me - REACH) * BLK

    for block in range(BLK):
        place = []
        for k in range(6):
            other = neighbours_ref[block, k]
            place.append(
                jnp.where(
                    other >= 0,
                    jnp.clip(other - first_block, 0, (2 * REACH + 1) * BLK - 1),
                    (2 * REACH + 1) * BLK + block,
                )
            )

        def face(k, item):
            return near_ref[place[k] // BLK, item, place[k] % BLK]

        for field in range(4):
            value = face(5, field)
            for k in (4, 3, 2):
                value = jnp.where(lane < (k - 1) * 32, face(k, field), value)
            ghost_edges[block * 32 + field * 8 : block * 32 + field * 8 + 8, :] = value
        for half in range(2):
            ghost_layers[half, block * 8 : block * 8 + 8, :] = jnp.where(
                row < 4, face(0, 4 + half), face(1, 4 + half)
            )

    for field in range(4):
        for half in range(2):
            for side in range(2):
                start = side * 4352 + half * 128
                padded[field, :, start : start + 128] = ghost_layers[
                    half, pl.ds(side * 4 + field, 8, stride=8), :
                ]
        padded[field, :, 256:4352] = field_rows(fraction_ref, centroid_ref, field, 0, CELLS)

    wide = lax.broadcasted_iota(jnp.int32, (8, 512), 1)
    y_pos = wide // 16 % 16
    z_pos = wide % 16
    z_cells = select(ghost_edges[...], ghost_ref[...])
    for tile in range(4):
        ghost_z_cells[tile] = z_cells[:, tile * 128 : tile * 128 + 128]

    def side_ghosts(ghost):
        shifts = (0, 80, 112, 64)
        return jnp.concatenate([pltpu.roll(ghost, i, 1) if i else ghost for i in shifts], 1)

    def one_pair(pair, carry):
        start = pl.multiple_of(pair * 512, 512)
        fields = [[] for _unused in range(7)]
        for field in range(4):
            center = padded[field, :, pl.ds(start + 256, 512)]
            ghost = ghost_edges[pl.ds(field * 8 + pair, 8, stride=32), :]
            ghost_y = side_ghosts(ghost)
            ghost_z = jnp.concatenate(
                [ghost_z_cells[i, pl.ds(field * 8 + pair, 8, stride=32), :] for i in range(4)], 1
            )
            fields[0].append(center)
            fields[1].append(padded[field, :, pl.ds(start, 512)])
            fields[2].append(padded[field, :, pl.ds(start + 512, 512)])
            fields[3].append(jnp.where(y_pos == 0, ghost_y, pltpu.roll(center, 16, 1)))
            fields[4].append(jnp.where(y_pos == 15, ghost_y, pltpu.roll(center, 496, 1)))
            fields[5].append(jnp.where(z_pos == 0, ghost_z, pltpu.roll(center, 1, 1)))
            fields[6].append(jnp.where(z_pos == 15, ghost_z, pltpu.roll(center, 511, 1)))
        a, b, c = [2.0 * (fields[2 + 2 * i][0] - fields[1 + 2 * i][0]) for i in range(3)]
        frac, cx, cy, cz = fields[0]
        d = 2.0 * (2.0 * frac - 1.0) - a * cx - b * cy - c * cz
        points = [(cx, cy, cz, 2.0 * frac - 1.0)]
        for k in range(6):
            f, *coords = fields[k + 1]
            coords[k // 2] = coords[k // 2] + (2.0 * (k % 2) - 1.0)
            points.append((*coords, 2.0 * f - 1.0))
        params = fit(points, (a, b, c, d))
        for comp in range(4):
            planes_ref[:, comp, pl.ds(start, 512)] = params[comp]
            layers[pl.ds(pl.multiple_of(pair * 32 + comp * 8, 8), 8), :] = params[comp]
        return carry

    lax.fori_loop(0, 8, one_pair, 0)

    edge_values = select(layers[...], edge_ref[:, 128:])
    for pair in range(8):
        for comp in range(4):
            row_at = pair * 32 + comp * 8
            fine_table[pl.ds(comp * 16 + 8 + pair, 8, stride=FINE_ROWS), :] = edge_values[
                row_at : row_at + 8
            ]
    for comp in range(4):
        for part in range(8):
            start = part // 4 * 128
            fine_table[pl.ds(comp * 16 + part, 8, stride=FINE_ROWS), :] = layer_parts(
                layers[comp * 8 : comp * 8 + 8, start : start + 128],
                layers[224 + comp * 8 : 232 + comp * 8, 256 + start : 384 + start],
                part % 4,
            )

    slots = refine_ref.shape[1]
    for first in range(0, slots, 4):
        whole = [jnp.zeros(VEC, jnp.float32)] * 3
        for slot in range(first, min(first + 4, slots)):
            block = jnp.clip(refine_ref[0, slot] - me * BLK, 0, BLK - 1)
            k = jnp.clip(refine_ref[1, slot], 0, 5)
            yz = (k >= 2).astype(jnp.int32)
            base = block * FINE_ROWS + yz * 8
            shift = (128 + 32 * (slot - first) - 32 * (k - 2 * yz)) % 128
            values = [
                fine_table[pl.ds(pl.multiple_of(base + comp * 16, 8), 8), :] for comp in (k // 2, 3)
            ]
            values.append(speed_ref[pl.ds(pl.multiple_of(block * 16 + yz * 8, 8), 8), :])
            whole = [
                jnp.where(lane // 32 == slot - first, pltpu.roll(value, shift, 1), other)
                for value, other in zip(values, whole)
            ]
        for item in range(3):
            start = (first // 4 * 3 + item) * 8
            packets_ref[start : start + 8, :] = whole[item]


def flux_kernel(faces_ref, speed_ref, packets_ref, table_ref, reflux_ref, live_list):
    me = lax.axis_index("sfc")
    lane = lanes()
    row = lax.broadcasted_iota(jnp.int32, VEC, 0)
    pos = lane % 32
    cell = pos % 16 // 2
    slots = table_ref.shape[2]

    found = 0
    for offset in range(2 * REACH + 1):
        other = me + offset - REACH
        there = (other >= 0) & (other < lax.axis_size("sfc"))

        def collect(slot, found):
            local = table_ref[offset, 2, slot] - me * BLK
            mine = there & (table_ref[offset, 0, slot] >= 0) & (local >= 0) & (local < BLK)
            live_list[found] = offset * slots + slot
            return found + mine.astype(jnp.int32)

        found = lax.fori_loop(0, slots, collect, found, unroll=4 if slots % 4 == 0 else 1)
    for extra in range(3):
        live_list[found + extra] = REACH * slots

    reflux_ref[...] = jnp.zeros_like(reflux_ref)

    offset_one = ((pos // 16).astype(jnp.float32) - 0.5) * 0.5
    offset_two = ((pos % 2).astype(jnp.float32) - 0.5) * 0.5

    def moments(item, weight):
        offset = item // slots
        slot = item % slots
        k = jnp.clip(table_ref[offset, 1, slot], 0, 5)
        block = jnp.clip(table_ref[offset, 2, slot] - me * BLK, 0, BLK - 1)
        quadrant = jnp.clip(table_ref[offset, 3, slot], 0, 3)
        qa, qb = quadrant // 2, quadrant % 2
        facing = k + 1 - 2 * (k % 2)
        axis = k // 2
        sign = (2 * (k % 2) - 1).astype(jnp.float32)
        yz = (k >= 2).astype(jnp.int32)
        from_row = qa * 4 + row // 2
        from_lane = (facing - 2 * yz) * 32 + row % 2 * 16 + qb * 8 + cell
        base = block * FINE_ROWS + yz * 8
        first = jnp.where(axis == 0, 1, 0)
        second = jnp.where(axis == 2, 1, 2)
        sources = [
            faces_ref[pl.ds(pl.multiple_of(base + comp * 16, 8), 8), :]
            for comp in (axis, first, second, 3)
        ]
        sources.append(speed_ref[pl.ds(pl.multiple_of(block * 16 + yz * 8, 8), 8), :])
        normal_c, one_c, two_c, d_c, u_c = [
            take(
                jnp.take_along_axis(source, from_row, axis=0, mode="promise_in_bounds"), from_lane
            )
            for source in sources
        ]
        back = (128 - 32 * (slot % 4)) % 128
        normal_f, d_f, u_f = [
            pltpu.roll(packets_ref[offset, slot // 4 * 3 + item], back, 1) for item in range(3)
        ]
        speed = sign * 0.5 * (u_f + u_c)
        depth = jnp.abs(speed) * TIME_STEP
        outflow = jnp.maximum(speed, 0.0)
        inflow = jnp.minimum(speed, 0.0)
        tangent = one_c * offset_one + two_c * offset_two + d_c
        volume = jnp.zeros(VEC, jnp.float32)
        moment = jnp.zeros(VEC, jnp.float32)
        for node in NODES:
            fine_model = 0.5 * (
                1.0 + jnp.tanh(normal_f * (sign * (0.5 - node * depth)) + d_f)
            )
            coarse_model = 0.5 * (
                1.0 + jnp.tanh(normal_c * (-sign * (0.5 - 0.5 * node * depth)) + tangent)
            )
            volume = volume + 0.5 * TIME_STEP * (outflow * fine_model + inflow * coarse_model)
            moment = moment + 0.5 * TIME_STEP * node * depth * sign * (
                inflow * coarse_model - outflow * fine_model
            )
        both = jnp.where(lane < 32, volume, pltpu.roll(moment, 32, 1))
        both = both + pltpu.roll(both, 127, 1)
        both = both + pltpu.roll(both, 112, 1)
        keep = (lane // 16 == row) & (lane % 16 // 8 == qb) & weight
        rows = []
        for m in range(2):
            placed = jnp.where(keep, take(both, m * 32 + 2 * (lane % 8)), 0.0)
            rows.append(jnp.sum(placed, axis=0, keepdims=True))
        return rows, block, facing, qa

    def group(number, carry):
        results = [
            moments(live_list[number * 4 + i], number * 4 + i < found) for i in range(4)
        ]
        for rows, block, facing, qa in results:
            start = pl.multiple_of(qa * 128, 128)
            for m in range(2):
                reflux_ref[block, facing, m : m + 1, pl.ds(start, 128)] += rows[m]
        return carry

    lax.fori_loop(0, (found + 3) // 4, group, 0)


def spec(space):
    return pl.BlockSpec(memory_space=space)


def per_device(fraction, centroid, velocity, neighbours, refinement):
    count = lax.axis_size("sfc")
    slots = refinement.shape[0]
    packet_rows = -(-slots // 4) * 3 * 8
    vmem, smem = spec(pltpu.VMEM), spec(pltpu.SMEM)
    f32 = jnp.float32
    refinement = refinement.T
    centroid, velocity = jnp.swapaxes(centroid, 0, 1), jnp.swapaxes(velocity, 0, 1)
    edge = edge_matrix()
    near, table, speeds = pl.pallas_call(
        lambda *refs: faces_kernel(count, *refs),
        out_shape=(
            jax.ShapeDtypeStruct((6, ITEMS, BLK * 8, 128), f32),
            jax.ShapeDtypeStruct((5, 4, slots), jnp.int32),
            jax.ShapeDtypeStruct((BLK * 16, 128), f32),
        ),
        in_specs=[vmem] * 5,
        out_specs=(vmem,) * 3,
        scratch_shapes=[pltpu.SemaphoreType.DMA((4, ITEMS))] * 2
        + [pltpu.SemaphoreType.DMA((4,))] * 2,
        compiler_params=pltpu.CompilerParams(collective_id=0, has_side_effects=True),
        name="exchange_faces",
    )(fraction, centroid, velocity, refinement, edge)
    planes, faces, packets = pl.pallas_call(
        fit_kernel,
        out_shape=(
            jax.ShapeDtypeStruct((BLK, 4, CELLS), f32),
            jax.ShapeDtypeStruct((BLK * FINE_ROWS, 128), f32),
            jax.ShapeDtypeStruct((packet_rows, 128), f32),
        ),
        in_specs=[vmem] * 6 + [smem] * 2,
        out_specs=(vmem,) * 3,
        scratch_shapes=[
            pltpu.VMEM((4, 8, CELLS + 512), f32),
            pltpu.VMEM((256, 128), f32),
            pltpu.VMEM((2, 64, 128), f32),
            pltpu.VMEM((4, 256, 128), f32),
            pltpu.VMEM((256, 512), f32),
        ],
        name="fit_planes",
    )(
        fraction,
        centroid,
        speeds,
        edge,
        ghost_matrix(),
        near.reshape(6, ITEMS, BLK, 8, 128),
        neighbours,
        refinement,
    )
    near_packets = pl.pallas_call(
        lambda *refs: packets_kernel(count, *refs),
        out_shape=jax.ShapeDtypeStruct((5, 1, packet_rows, 128), f32),
        in_specs=[vmem],
        out_specs=vmem,
        scratch_shapes=[pltpu.SemaphoreType.DMA((4, 1))] * 2,
        compiler_params=pltpu.CompilerParams(collective_id=1, has_side_effects=True),
        name="exchange_packets",
    )(packets.reshape(1, packet_rows, 128))
    reflux = pl.pallas_call(
        flux_kernel,
        out_shape=jax.ShapeDtypeStruct((BLK, 6, 2, 256), f32),
        in_specs=[vmem] * 3 + [smem],
        out_specs=vmem,
        scratch_shapes=[pltpu.SMEM((5 * slots + 4,), jnp.int32)],
        name="reflux_moments",
    )(faces, speeds, near_packets.reshape(5, packet_rows // 8, 8, 128), table)
    return planes, reflux


def solution(mesh):
    return jax.shard_map(
        per_device,
        mesh=mesh,
        in_specs=(
            P("sfc", None),
            P("sfc", None, None),
            P("sfc", None, None),
            P("sfc", None),
            P("sfc", None),
        ),
        out_specs=(P("sfc", None, None), P("sfc", None, None, None)),
        check_vma=False,
    )
```

```python
import jax
import jax.numpy as jnp
import numpy as np
from jax import lax
from jax.experimental import pallas as pl
from jax.experimental.pallas import tpu as pltpu
from jax.sharding import PartitionSpec as P

EDGE = 16
CELLS = 4096
REACH = 2
PASSES = 6
BLK = 8
NODES = (0.5 - 3.0**0.5 / 6.0, 0.5 + 3.0**0.5 / 6.0)
TIME_STEP = 0.25
DAMPING = 0.1
SHIFTS = (1, -1, 2, -2)
VEC = (8, 128)
ITEMS = 6
FINE_ROWS = 4 * 2 * 8


def lanes():
    return lax.broadcasted_iota(jnp.int32, VEC, 1)


def take(values, index):
    return jnp.take_along_axis(values, index, axis=1, mode="promise_in_bounds")


def edge_place(kind, odd, j):
    y, z = ((0, j), (15, j), (j, 0), (j, 15))[kind]
    return odd * 256 + y * 16 + z


def edge_matrix():
    matrix = np.zeros((512, 256), np.float32)
    for lane in range(128):
        kind, odd, j = lane // 32, lane // 16 % 2, lane % 16
        matrix[edge_place(kind + 1 - 2 * (kind % 2), odd, j), lane] = 1
        matrix[edge_place(kind, odd, j), 128 + lane] = 1
    return jnp.asarray(matrix, jnp.bfloat16)


def ghost_matrix():
    matrix = np.zeros((128, 512), np.float32)
    for lane in range(64, 128):
        matrix[lane, edge_place(lane // 32, lane // 16 % 2, lane % 16)] = 1
    return jnp.asarray(matrix, jnp.bfloat16)


def select(values, matrix):
    high = values.astype(jnp.bfloat16)
    rest = values - high.astype(jnp.float32)
    middle = rest.astype(jnp.bfloat16)
    low = (rest - middle.astype(jnp.float32)).astype(jnp.bfloat16)
    parts = [
        jnp.dot(part, matrix, preferred_element_type=jnp.float32) for part in (low, middle, high)
    ]
    return parts[0] + parts[1] + parts[2]


def layer_parts(low, high, part):
    first = low if part == 0 else pltpu.roll(low, 128 - 32 * part, 1)
    second = high if part == 1 else pltpu.roll(high, (160 - 32 * part) % 128, 1)
    return jnp.where(lanes() < 32, first, second)


def field_rows(fraction_ref, centroid_ref, field, start, size):
    if field == 0:
        return fraction_ref[:, pl.ds(start, size)]
    return centroid_ref[field - 1, :, pl.ds(start, size)]


def within(device, count):
    return (device >= 0) & (device < count)


def greet(me, peers):
    barrier = pltpu.get_barrier_semaphore()
    number = 0
    for other, there in peers:

        @pl.when(there)
        def _signal():
            pl.semaphore_signal(
                barrier, inc=1, device_id=(other,), device_id_type=pl.DeviceIdType.MESH
            )

        number = number + there.astype(jnp.int32)
    return barrier, number


def direct_peers(me, count):
    return [(me + shift, within(me + shift, count)) for shift in SHIFTS]


def remote(src, dst, send, recv, other):
    return pltpu.make_async_remote_copy(
        src_ref=src,
        dst_ref=dst,
        send_sem=send,
        recv_sem=recv,
        device_id=(other,),
        device_id_type=pl.DeviceIdType.MESH,
    )


class Direct:
    def __init__(self, me, count, buffer, pieces, send, recv):
        self.me, self.count = me, count
        self.buffer, self.pieces, self.send, self.recv = buffer, pieces, send, recv

    def peers(self):
        return direct_peers(self.me, self.count)

    def copy(self, place, piece):
        shift = SHIFTS[place]
        return remote(
            self.buffer.at[REACH, piece],
            self.buffer.at[REACH - shift, piece],
            self.send.at[place, piece],
            self.recv.at[place, piece],
            self.me + shift,
        )

    def start(self, piece):
        for place, shift in enumerate(SHIFTS):
            pl.when(within(self.me + shift, self.count))(self.copy(place, piece).start)

    def finish(self):
        for piece in self.pieces:
            for place, shift in enumerate(SHIFTS):
                pl.when(within(self.me + shift, self.count))(self.copy(place, piece).wait_send)
                pl.when(within(self.me - shift, self.count))(self.copy(place, piece).wait_recv)


class Relay:
    def __init__(self, me, count, buffer, pieces, send, recv):
        self.buffer, self.pieces, self.send, self.recv = buffer, pieces, send, recv
        core, x = me % 2, me // 2 % 2
        to, origin = me + 4 - 8 * x, me - 4 + 8 * x
        self.late = x != core
        self.onward, self.second = within(to, count), within(origin, count)
        self.others = [(me + shift, within(me + shift, count)) for shift in (4, -4)]
        self.steps = (
            (me + 2 - 4 * x, REACH, 4 * x, 4 * (1 - x)),
            (me + 1 - 2 * core, REACH, 1 + 2 * core, 3 - 2 * core),
            (to, 4 * (1 - x), 4 * x, 4 * x),
            (me + 1 - 2 * core, 4 * (1 - core), 3 - 2 * core, 1 + 2 * core),
        )

    def copy(self, step, piece, arrived):
        other, source, there, here = self.steps[step]
        return remote(
            self.buffer.at[source, piece],
            self.buffer.at[here if arrived else there, piece],
            self.send.at[step, piece],
            self.recv.at[step, piece],
            other,
        )

    def sent(self, step, piece):
        return self.copy(step, piece, False)

    def arrived(self, step, piece):
        return self.copy(step, piece, True)

    def start(self, piece):
        self.sent(0, piece).start()

    def forward(self, piece):
        self.arrived(0, piece).wait_recv()
        pl.when(self.onward)(self.sent(2, piece).start)
        pl.when(jnp.logical_not(self.late))(self.sent(3, piece).start)
        self.sent(1, piece).start()

    def finish(self):
        for piece in self.pieces:

            @pl.when(self.second)
            def _second():
                self.arrived(2, piece).wait_recv()
                pl.when(self.late)(self.sent(3, piece).start)

        for piece in self.pieces:
            self.arrived(1, piece).wait_recv()
            pl.when(self.second | self.late)(self.arrived(3, piece).wait_recv)
            self.sent(0, piece).wait_send()
            self.sent(1, piece).wait_send()
            pl.when(self.onward)(self.sent(2, piece).wait_send)
            pl.when(self.second | jnp.logical_not(self.late))(self.sent(3, piece).wait_send)


def faces_kernel(
    count,
    fraction_ref,
    centroid_ref,
    velocity_ref,
    refine_ref,
    edge_ref,
    near_ref,
    table_ref,
    speed_ref,
    send,
    recv,
    send2,
    recv2,
):
    me = lax.axis_index("sfc")
    order = (4, 5, 0, 1, 2, 3)
    faces = Relay(me, count, near_ref, order, send, recv)
    barrier, number = greet(me, direct_peers(me, count) + faces.others)

    def extract_layers(slot, item, swap):
        for side in range(2):
            start = (1 - side if swap else side) * 3840 + (item - 4) * 128
            for field in range(4):
                near_ref[slot, item, pl.ds(side * 4 + field, 8, stride=8), :] = field_rows(
                    fraction_ref, centroid_ref, field, start, 128
                )

    extract_layers(REACH, 4, True)
    extract_layers(REACH, 5, True)
    pl.semaphore_wait(barrier, number)
    faces.start(4)
    faces.start(5)
    both = select(
        jnp.concatenate(
            [
                field_rows(fraction_ref, centroid_ref, field, pair * 512, 512)
                for field in range(4)
                for pair in range(8)
            ],
            0,
        ),
        edge_ref[...],
    )

    def put(slot, field, start):
        for pair in range(8):
            row = field * 64 + pair * 8
            near_ref[slot, field, pl.ds(pair, 8, stride=8), :] = both[
                row : row + 8, start : start + 128
            ]

    for field in range(4):
        put(REACH, field, 0)
        faces.start(field)

    def table_copy(place):
        shift = SHIFTS[place]
        return remote(
            refine_ref, table_ref.at[REACH - shift], send2.at[place], recv2.at[place], me + shift
        )

    table_ref[REACH] = refine_ref[...]
    for place, shift in enumerate(SHIFTS):
        pl.when(within(me + shift, count))(table_copy(place).start)

    for field in range(4):
        put(2 * REACH + 1, field, 128)
    extract_layers(2 * REACH + 1, 4, False)
    extract_layers(2 * REACH + 1, 5, False)
    faces.forward(4)
    faces.forward(5)
    faces.forward(0)
    speeds = select(
        jnp.concatenate(
            [velocity_ref[axis, :, pl.ds(pair * 512, 512)] for axis in (1, 2) for pair in range(8)],
            0,
        ),
        edge_ref[:, 128:],
    )
    for pair in range(8):
        speed_ref[pl.ds(8 + pair, 8, stride=16), :] = jnp.where(
            lanes() < 64, speeds[pair * 8 : pair * 8 + 8], speeds[64 + pair * 8 : 72 + pair * 8]
        )
    faces.forward(1)
    for part in range(8):
        start = part // 4 * 128
        speed_ref[pl.ds(part, 8, stride=16), :] = layer_parts(
            velocity_ref[0, :, start : start + 128],
            velocity_ref[0, :, 3840 + start : 3968 + start],
            part % 4,
        )
    faces.forward(2)
    faces.forward(3)
    faces.finish()
    for place, shift in enumerate(SHIFTS):
        pl.when(within(me + shift, count))(table_copy(place).wait_send)
        pl.when(within(me - shift, count))(table_copy(place).wait_recv)


def packets_kernel(count, own_ref, near_ref, send, recv):
    me = lax.axis_index("sfc")
    pieces = range(own_ref.shape[0])
    packets = Direct(me, count, near_ref, pieces, send, recv)
    barrier, number = greet(me, packets.peers())
    near_ref[REACH] = own_ref[...]
    pl.semaphore_wait(barrier, number)
    for piece in pieces:
        packets.start(piece)
    packets.finish()


def solve(h, g):
    (h00, h01, h02, h03, h11, h12, h13, h22, h23, h33) = h
    i0 = 1.0 / h00
    l10, l20, l30 = h01 * i0, h02 * i0, h03 * i0
    d1 = h11 - l10 * h01
    a21, a31 = h12 - l10 * h02, h13 - l10 * h03
    i1 = 1.0 / d1
    l21, l31 = a21 * i1, a31 * i1
    d2 = h22 - l20 * h02 - l21 * a21
    a32 = h23 - l20 * h03 - l21 * a31
    i2 = 1.0 / d2
    l32 = a32 * i2
    d3 = h33 - l30 * h03 - l31 * a31 - l32 * a32
    y1 = g[1] - l10 * g[0]
    y2 = g[2] - l20 * g[0] - l21 * y1
    y3 = g[3] - l30 * g[0] - l31 * y1 - l32 * y2
    x3 = y3 / d3
    x2 = y2 * i2 - l32 * x3
    x1 = y1 * i1 - l21 * x2 - l31 * x3
    x0 = g[0] * i0 - l10 * x1 - l20 * x2 - l30 * x3
    return x0, x1, x2, x3


def fit(points, params):
    width = 128

    def normal_equations(start, params):
        a, b, c, d = [p[:, start : start + width] for p in params]
        h = [None] * 10
        g = [None] * 4

        def add(total, place, term):
            total[place] = term if total[place] is None else total[place] + term

        for point in points:
            px, py, pz, f = [value[:, start : start + width] for value in point]
            t = jnp.tanh(a * px + b * py + c * pz + d)
            s = 1.0 - t * t
            q = s * s
            w = s * (t - f)
            qx, qy, qz = q * px, q * py, q * pz
            for place, term in enumerate(
                (qx * px, qx * py, qx * pz, qx, qy * py, qy * pz, qy, qz * pz, qz, q)
            ):
                add(h, place, term)
            for place, term in enumerate((w * px, w * py, w * pz, w)):
                add(g, place, term)
        for place in (0, 4, 7, 9):
            h[place] = h[place] + 4.0 * DAMPING
        return h + g

    def one_pass(_unused, params):
        parts = [normal_equations(start, params) for start in range(0, params[0].shape[1], width)]
        sums = [jnp.concatenate(part, 1) for part in zip(*parts)]
        step = solve(sums[:10], sums[10:])
        return tuple(p - s for p, s in zip(params, step))

    return lax.fori_loop(0, PASSES, one_pass, params)


def fit_kernel(
    fraction_ref,
    centroid_ref,
    speed_ref,
    edge_ref,
    ghost_ref,
    near_ref,
    neighbours_ref,
    refine_ref,
    planes_ref,
    fine_table,
    packets_ref,
    padded,
    ghost_edges,
    ghost_layers,
    ghost_z_cells,
    layers,
):
    me = lax.axis_index("sfc")
    lane = lanes()
    row = lax.broadcasted_iota(jnp.int32, VEC, 0)
    first_block = (me - REACH) * BLK

    for block in range(BLK):
        place = []
        for k in range(6):
            other = neighbours_ref[block, k]
            place.append(
                jnp.where(
                    other >= 0,
                    jnp.clip(other - first_block, 0, (2 * REACH + 1) * BLK - 1),
                    (2 * REACH + 1) * BLK + block,
                )
            )

        def face(k, item):
            return near_ref[place[k] // BLK, item, place[k] % BLK]

        for field in range(4):
            value = face(5, field)
            for k in (4, 3, 2):
                value = jnp.where(lane < (k - 1) * 32, face(k, field), value)
            ghost_edges[block * 32 + field * 8 : block * 32 + field * 8 + 8, :] = value
        for half in range(2):
            ghost_layers[half, block * 8 : block * 8 + 8, :] = jnp.where(
                row < 4, face(0, 4 + half), face(1, 4 + half)
            )

    for field in range(4):
        for half in range(2):
            for side in range(2):
                start = side * 4352 + half * 128
                padded[field, :, start : start + 128] = ghost_layers[
                    half, pl.ds(side * 4 + field, 8, stride=8), :
                ]
        padded[field, :, 256:4352] = field_rows(fraction_ref, centroid_ref, field, 0, CELLS)

    wide = lax.broadcasted_iota(jnp.int32, (8, 512), 1)
    y_pos = wide // 16 % 16
    z_pos = wide % 16
    z_cells = select(ghost_edges[...], ghost_ref[...])
    for tile in range(4):
        ghost_z_cells[tile] = z_cells[:, tile * 128 : tile * 128 + 128]

    def side_ghosts(ghost):
        shifts = (0, 80, 112, 64)
        return jnp.concatenate([pltpu.roll(ghost, i, 1) if i else ghost for i in shifts], 1)

    def stencil(pair):
        start = pl.multiple_of(pair * 512, 512)
        fields = [[] for _unused in range(7)]
        for field in range(4):
            center = padded[field, :, pl.ds(start + 256, 512)]
            ghost = ghost_edges[pl.ds(field * 8 + pair, 8, stride=32), :]
            ghost_y = side_ghosts(ghost)
            ghost_z = jnp.concatenate(
                [ghost_z_cells[i, pl.ds(field * 8 + pair, 8, stride=32), :] for i in range(4)], 1
            )
            fields[0].append(center)
            fields[1].append(padded[field, :, pl.ds(start, 512)])
            fields[2].append(padded[field, :, pl.ds(start + 512, 512)])
            fields[3].append(jnp.where(y_pos == 0, ghost_y, pltpu.roll(center, 16, 1)))
            fields[4].append(jnp.where(y_pos == 15, ghost_y, pltpu.roll(center, 496, 1)))
            fields[5].append(jnp.where(z_pos == 0, ghost_z, pltpu.roll(center, 1, 1)))
            fields[6].append(jnp.where(z_pos == 15, ghost_z, pltpu.roll(center, 511, 1)))
        a, b, c = [2.0 * (fields[2 + 2 * i][0] - fields[1 + 2 * i][0]) for i in range(3)]
        frac, cx, cy, cz = fields[0]
        d = 2.0 * (2.0 * frac - 1.0) - a * cx - b * cy - c * cz
        points = [(cx, cy, cz, 2.0 * frac - 1.0)]
        for k in range(6):
            f, *coords = fields[k + 1]
            coords[k // 2] = coords[k // 2] + (2.0 * (k % 2) - 1.0)
            points.append((*coords, 2.0 * f - 1.0))
        return points, (a, b, c, d)

    together = 2

    def some_pairs(number, carry):
        pairs = [number * together + i for i in range(together)]
        stencils = [stencil(pair) for pair in pairs]
        points = [
            tuple(jnp.concatenate(values, 1) for values in zip(*same))
            for same in zip(*[points for points, _unused in stencils])
        ]
        params = fit(
            points, tuple(jnp.concatenate(values, 1) for values in zip(*[p for _unused, p in stencils]))
        )
        for i, pair in enumerate(pairs):
            start = pl.multiple_of(pair * 512, 512)
            for comp in range(4):
                value = params[comp][:, i * 512 : i * 512 + 512]
                planes_ref[:, comp, pl.ds(start, 512)] = value
                layers[pl.ds(pl.multiple_of(pair * 32 + comp * 8, 8), 8), :] = value
        return carry

    lax.fori_loop(0, 8 // together, some_pairs, 0)

    edge_values = select(layers[...], edge_ref[:, 128:])
    for pair in range(8):
        for comp in range(4):
            row_at = pair * 32 + comp * 8
            fine_table[pl.ds(comp * 16 + 8 + pair, 8, stride=FINE_ROWS), :] = edge_values[
                row_at : row_at + 8
            ]
    for comp in range(4):
        for part in range(8):
            start = part // 4 * 128
            fine_table[pl.ds(comp * 16 + part, 8, stride=FINE_ROWS), :] = layer_parts(
                layers[comp * 8 : comp * 8 + 8, start : start + 128],
                layers[224 + comp * 8 : 232 + comp * 8, 256 + start : 384 + start],
                part % 4,
            )

    slots = refine_ref.shape[1]
    for first in range(0, slots, 4):
        whole = [jnp.zeros(VEC, jnp.float32)] * 3
        for slot in range(first, min(first + 4, slots)):
            block = jnp.clip(refine_ref[0, slot] - me * BLK, 0, BLK - 1)
            k = jnp.clip(refine_ref[1, slot], 0, 5)
            yz = (k >= 2).astype(jnp.int32)
            base = block * FINE_ROWS + yz * 8
            shift = (128 + 32 * (slot - first) - 32 * (k - 2 * yz)) % 128
            values = [
                fine_table[pl.ds(pl.multiple_of(base + comp * 16, 8), 8), :] for comp in (k // 2, 3)
            ]
            values.append(speed_ref[pl.ds(pl.multiple_of(block * 16 + yz * 8, 8), 8), :])
            whole = [
                jnp.where(lane // 32 == slot - first, pltpu.roll(value, shift, 1), other)
                for value, other in zip(values, whole)
            ]
        for item in range(3):
            start = (first // 4 * 3 + item) * 8
            packets_ref[start : start + 8, :] = whole[item]


def flux_kernel(faces_ref, speed_ref, packets_ref, table_ref, reflux_ref, live_list):
    me = lax.axis_index("sfc")
    lane = lanes()
    row = lax.broadcasted_iota(jnp.int32, VEC, 0)
    pos = lane % 32
    cell = pos % 16 // 2
    slots = table_ref.shape[2]

    found = 0
    for offset in range(2 * REACH + 1):
        other = me + offset - REACH
        there = (other >= 0) & (other < lax.axis_size("sfc"))

        def collect(slot, found):
            local = table_ref[offset, 2, slot] - me * BLK
            mine = there & (table_ref[offset, 0, slot] >= 0) & (local >= 0) & (local < BLK)
            live_list[found] = offset * slots + slot
            return found + mine.astype(jnp.int32)

        found = lax.fori_loop(0, slots, collect, found, unroll=4 if slots % 4 == 0 else 1)
    for extra in range(3):
        live_list[found + extra] = REACH * slots

    reflux_ref[...] = jnp.zeros_like(reflux_ref)

    offset_one = ((pos // 16).astype(jnp.float32) - 0.5) * 0.5
    offset_two = ((pos % 2).astype(jnp.float32) - 0.5) * 0.5

    def moments(item, weight):
        offset = item // slots
        slot = item % slots
        k = jnp.clip(table_ref[offset, 1, slot], 0, 5)
        block = jnp.clip(table_ref[offset, 2, slot] - me * BLK, 0, BLK - 1)
        quadrant = jnp.clip(table_ref[offset, 3, slot], 0, 3)
        qa, qb = quadrant // 2, quadrant % 2
        facing = k + 1 - 2 * (k % 2)
        axis = k // 2
        sign = (2 * (k % 2) - 1).astype(jnp.float32)
        yz = (k >= 2).astype(jnp.int32)
        from_row = qa * 4 + row // 2
        from_lane = (facing - 2 * yz) * 32 + row % 2 * 16 + qb * 8 + cell
        base = block * FINE_ROWS + yz * 8
        first = jnp.where(axis == 0, 1, 0)
        second = jnp.where(axis == 2, 1, 2)
        sources = [
            faces_ref[pl.ds(pl.multiple_of(base + comp * 16, 8), 8), :]
            for comp in (axis, first, second, 3)
        ]
        sources.append(speed_ref[pl.ds(pl.multiple_of(block * 16 + yz * 8, 8), 8), :])
        normal_c, one_c, two_c, d_c, u_c = [
            take(
                jnp.take_along_axis(source, from_row, axis=0, mode="promise_in_bounds"), from_lane
            )
            for source in sources
        ]
        back = (128 - 32 * (slot % 4)) % 128
        normal_f, d_f, u_f = [
            pltpu.roll(packets_ref[offset, slot // 4 * 3 + item], back, 1) for item in range(3)
        ]
        speed = sign * 0.5 * (u_f + u_c)
        depth = jnp.abs(speed) * TIME_STEP
        outflow = jnp.maximum(speed, 0.0)
        inflow = jnp.minimum(speed, 0.0)
        tangent = one_c * offset_one + two_c * offset_two + d_c
        volume = jnp.zeros(VEC, jnp.float32)
        moment = jnp.zeros(VEC, jnp.float32)
        for node in NODES:
            fine_model = 0.5 * (
                1.0 + jnp.tanh(normal_f * (sign * (0.5 - node * depth)) + d_f)
            )
            coarse_model = 0.5 * (
                1.0 + jnp.tanh(normal_c * (-sign * (0.5 - 0.5 * node * depth)) + tangent)
            )
            volume = volume + 0.5 * TIME_STEP * (outflow * fine_model + inflow * coarse_model)
            moment = moment + 0.5 * TIME_STEP * node * depth * sign * (
                inflow * coarse_model - outflow * fine_model
            )
        both = jnp.where(lane < 32, volume, pltpu.roll(moment, 32, 1))
        both = both + pltpu.roll(both, 127, 1)
        both = both + pltpu.roll(both, 112, 1)
        keep = (lane // 16 == row) & (lane % 16 // 8 == qb) & weight
        rows = []
        for m in range(2):
            placed = jnp.where(keep, take(both, m * 32 + 2 * (lane % 8)), 0.0)
            rows.append(jnp.sum(placed, axis=0, keepdims=True))
        return rows, block, facing, qa

    def group(number, carry):
        results = [
            moments(live_list[number * 4 + i], number * 4 + i < found) for i in range(4)
        ]
        for rows, block, facing, qa in results:
            start = pl.multiple_of(qa * 128, 128)
            for m in range(2):
                reflux_ref[block, facing, m : m + 1, pl.ds(start, 128)] += rows[m]
        return carry

    lax.fori_loop(0, (found + 3) // 4, group, 0)


def spec(space):
    return pl.BlockSpec(memory_space=space)


def per_device(fraction, centroid, velocity, neighbours, refinement):
    count = lax.axis_size("sfc")
    slots = refinement.shape[0]
    packet_rows = -(-slots // 4) * 3 * 8
    vmem, smem = spec(pltpu.VMEM), spec(pltpu.SMEM)
    f32 = jnp.float32
    refinement = refinement.T
    centroid, velocity = jnp.swapaxes(centroid, 0, 1), jnp.swapaxes(velocity, 0, 1)
    edge = edge_matrix()
    near, table, speeds = pl.pallas_call(
        lambda *refs: faces_kernel(count, *refs),
        out_shape=(
            jax.ShapeDtypeStruct((6, ITEMS, BLK * 8, 128), f32),
            jax.ShapeDtypeStruct((5, 4, slots), jnp.int32),
            jax.ShapeDtypeStruct((BLK * 16, 128), f32),
        ),
        in_specs=[vmem] * 5,
        out_specs=(vmem,) * 3,
        scratch_shapes=[pltpu.SemaphoreType.DMA((4, ITEMS))] * 2
        + [pltpu.SemaphoreType.DMA((4,))] * 2,
        compiler_params=pltpu.CompilerParams(collective_id=0, has_side_effects=True),
        name="exchange_faces",
    )(fraction, centroid, velocity, refinement, edge)
    planes, faces, packets = pl.pallas_call(
        fit_kernel,
        out_shape=(
            jax.ShapeDtypeStruct((BLK, 4, CELLS), f32),
            jax.ShapeDtypeStruct((BLK * FINE_ROWS, 128), f32),
            jax.ShapeDtypeStruct((packet_rows, 128), f32),
        ),
        in_specs=[vmem] * 6 + [smem] * 2,
        out_specs=(vmem,) * 3,
        scratch_shapes=[
            pltpu.VMEM((4, 8, CELLS + 512), f32),
            pltpu.VMEM((256, 128), f32),
            pltpu.VMEM((2, 64, 128), f32),
            pltpu.VMEM((4, 256, 128), f32),
            pltpu.VMEM((256, 512), f32),
        ],
        name="fit_planes",
    )(
        fraction,
        centroid,
        speeds,
        edge,
        ghost_matrix(),
        near.reshape(6, ITEMS, BLK, 8, 128),
        neighbours,
        refinement,
    )
    near_packets = pl.pallas_call(
        lambda *refs: packets_kernel(count, *refs),
        out_shape=jax.ShapeDtypeStruct((5, 1, packet_rows, 128), f32),
        in_specs=[vmem],
        out_specs=vmem,
        scratch_shapes=[pltpu.SemaphoreType.DMA((4, 1))] * 2,
        compiler_params=pltpu.CompilerParams(collective_id=1, has_side_effects=True),
        name="exchange_packets",
    )(packets.reshape(1, packet_rows, 128))
    reflux = pl.pallas_call(
        flux_kernel,
        out_shape=jax.ShapeDtypeStruct((BLK, 6, 2, 256), f32),
        in_specs=[vmem] * 3 + [smem],
        out_specs=vmem,
        scratch_shapes=[pltpu.SMEM((5 * slots + 4,), jnp.int32)],
        name="reflux_moments",
    )(faces, speeds, near_packets.reshape(5, packet_rows // 8, 8, 128), table)
    return planes, reflux


def solution(mesh):
    return jax.shard_map(
        per_device,
        mesh=mesh,
        in_specs=(
            P("sfc", None),
            P("sfc", None, None),
            P("sfc", None, None),
            P("sfc", None),
            P("sfc", None),
        ),
        out_specs=(P("sfc", None, None), P("sfc", None, None, None)),
        check_vma=False,
    )
```

```python
import jax
import jax.numpy as jnp
import numpy as np
from jax import lax
from jax.experimental import pallas as pl
from jax.experimental.pallas import tpu as pltpu
from jax.sharding import PartitionSpec as P

EDGE = 16
CELLS = 4096
REACH = 2
PASSES = 6
BLK = 8
NODES = (0.5 - 3.0**0.5 / 6.0, 0.5 + 3.0**0.5 / 6.0)
TIME_STEP = 0.25
DAMPING = 0.1
SHIFTS = (1, -1, 2, -2)
VEC = (8, 128)
ITEMS = 6
FINE_ROWS = 4 * 2 * 8


def lanes():
    return lax.broadcasted_iota(jnp.int32, VEC, 1)


def take(values, index):
    return jnp.take_along_axis(values, index, axis=1, mode="promise_in_bounds")


def edge_place(kind, odd, j):
    y, z = ((0, j), (15, j), (j, 0), (j, 15))[kind]
    return odd * 256 + y * 16 + z


def edge_matrix():
    matrix = np.zeros((512, 256), np.float32)
    for lane in range(128):
        kind, odd, j = lane // 32, lane // 16 % 2, lane % 16
        matrix[edge_place(kind + 1 - 2 * (kind % 2), odd, j), lane] = 1
        matrix[edge_place(kind, odd, j), 128 + lane] = 1
    return jnp.asarray(matrix, jnp.bfloat16)


def ghost_matrix():
    matrix = np.zeros((128, 512), np.float32)
    for lane in range(64, 128):
        matrix[lane, edge_place(lane // 32, lane // 16 % 2, lane % 16)] = 1
    return jnp.asarray(matrix, jnp.bfloat16)


def select(values, matrix):
    high = values.astype(jnp.bfloat16)
    rest = values - high.astype(jnp.float32)
    middle = rest.astype(jnp.bfloat16)
    low = (rest - middle.astype(jnp.float32)).astype(jnp.bfloat16)
    parts = [
        jnp.dot(part, matrix, preferred_element_type=jnp.float32) for part in (low, middle, high)
    ]
    return parts[0] + parts[1] + parts[2]


def layer_parts(low, high, part):
    first = low if part == 0 else pltpu.roll(low, 128 - 32 * part, 1)
    second = high if part == 1 else pltpu.roll(high, (160 - 32 * part) % 128, 1)
    return jnp.where(lanes() < 32, first, second)


def field_rows(fraction_ref, centroid_ref, field, start, size):
    if field == 0:
        return fraction_ref[:, pl.ds(start, size)]
    return centroid_ref[field - 1, :, pl.ds(start, size)]


def within(device, count):
    return (device >= 0) & (device < count)


def greet(me, peers):
    barrier = pltpu.get_barrier_semaphore()
    number = 0
    for other, there in peers:

        @pl.when(there)
        def _signal():
            pl.semaphore_signal(
                barrier, inc=1, device_id=(other,), device_id_type=pl.DeviceIdType.MESH
            )

        number = number + there.astype(jnp.int32)
    return barrier, number


def direct_peers(me, count):
    return [(me + shift, within(me + shift, count)) for shift in SHIFTS]


def remote(src, dst, send, recv, other):
    return pltpu.make_async_remote_copy(
        src_ref=src,
        dst_ref=dst,
        send_sem=send,
        recv_sem=recv,
        device_id=(other,),
        device_id_type=pl.DeviceIdType.MESH,
    )


class Direct:
    def __init__(self, me, count, buffer, pieces, send, recv):
        self.me, self.count = me, count
        self.buffer, self.pieces, self.send, self.recv = buffer, pieces, send, recv

    def peers(self):
        return direct_peers(self.me, self.count)

    def copy(self, place, piece):
        shift = SHIFTS[place]
        return remote(
            self.buffer.at[REACH, piece],
            self.buffer.at[REACH - shift, piece],
            self.send.at[place, piece],
            self.recv.at[place, piece],
            self.me + shift,
        )

    def start(self, piece):
        for place, shift in enumerate(SHIFTS):
            pl.when(within(self.me + shift, self.count))(self.copy(place, piece).start)

    def finish(self):
        for piece in self.pieces:
            for place, shift in enumerate(SHIFTS):
                pl.when(within(self.me + shift, self.count))(self.copy(place, piece).wait_send)
                pl.when(within(self.me - shift, self.count))(self.copy(place, piece).wait_recv)


class Relay:
    def __init__(self, me, count, buffer, pieces, send, recv):
        self.buffer, self.pieces, self.send, self.recv = buffer, pieces, send, recv
        core, x = me % 2, me // 2 % 2
        to, origin = me + 4 - 8 * x, me - 4 + 8 * x
        self.late = x != core
        self.onward, self.second = within(to, count), within(origin, count)
        self.others = [(me + shift, within(me + shift, count)) for shift in (4, -4)]
        self.steps = (
            (me + 2 - 4 * x, REACH, 4 * x, 4 * (1 - x)),
            (me + 1 - 2 * core, REACH, 1 + 2 * core, 3 - 2 * core),
            (to, 4 * (1 - x), 4 * x, 4 * x),
            (me + 1 - 2 * core, 4 * (1 - core), 3 - 2 * core, 1 + 2 * core),
        )

    def copy(self, step, piece, arrived):
        other, source, there, here = self.steps[step]
        return remote(
            self.buffer.at[source, piece],
            self.buffer.at[here if arrived else there, piece],
            self.send.at[step, piece],
            self.recv.at[step, piece],
            other,
        )

    def sent(self, step, piece):
        return self.copy(step, piece, False)

    def arrived(self, step, piece):
        return self.copy(step, piece, True)

    def start(self, piece):
        self.sent(0, piece).start()

    def forward(self, piece):
        self.arrived(0, piece).wait_recv()
        pl.when(self.onward)(self.sent(2, piece).start)
        pl.when(jnp.logical_not(self.late))(self.sent(3, piece).start)
        self.sent(1, piece).start()

    def finish(self):
        for piece in self.pieces:

            @pl.when(self.second)
            def _second():
                self.arrived(2, piece).wait_recv()
                pl.when(self.late)(self.sent(3, piece).start)

        for piece in self.pieces:
            self.arrived(1, piece).wait_recv()
            pl.when(self.second | self.late)(self.arrived(3, piece).wait_recv)
            self.sent(0, piece).wait_send()
            self.sent(1, piece).wait_send()
            pl.when(self.onward)(self.sent(2, piece).wait_send)
            pl.when(self.second | jnp.logical_not(self.late))(self.sent(3, piece).wait_send)


def faces_kernel(
    count,
    fraction_ref,
    centroid_ref,
    velocity_ref,
    refine_ref,
    edge_ref,
    near_ref,
    table_ref,
    speed_ref,
    send,
    recv,
    send2,
    recv2,
):
    me = lax.axis_index("sfc")
    order = (4, 5, 0, 1, 2, 3)
    faces = Relay(me, count, near_ref, order, send, recv)
    barrier, number = greet(me, direct_peers(me, count) + faces.others)

    def extract_layers(slot, item, swap):
        for side in range(2):
            start = (1 - side if swap else side) * 3840 + (item - 4) * 128
            for field in range(4):
                near_ref[slot, item, pl.ds(side * 4 + field, 8, stride=8), :] = field_rows(
                    fraction_ref, centroid_ref, field, start, 128
                )

    extract_layers(REACH, 4, True)
    extract_layers(REACH, 5, True)
    speeds = select(
        jnp.concatenate(
            [velocity_ref[axis, :, pl.ds(pair * 512, 512)] for axis in (1, 2) for pair in range(8)],
            0,
        ),
        edge_ref[:, 128:],
    )
    for pair in range(8):
        speed_ref[pl.ds(8 + pair, 8, stride=16), :] = jnp.where(
            lanes() < 64, speeds[pair * 8 : pair * 8 + 8], speeds[64 + pair * 8 : 72 + pair * 8]
        )
    for part in range(8):
        start = part // 4 * 128
        speed_ref[pl.ds(part, 8, stride=16), :] = layer_parts(
            velocity_ref[0, :, start : start + 128],
            velocity_ref[0, :, 3840 + start : 3968 + start],
            part % 4,
        )
    pl.semaphore_wait(barrier, number)
    faces.start(4)
    faces.start(5)
    both = select(
        jnp.concatenate(
            [
                field_rows(fraction_ref, centroid_ref, field, pair * 512, 512)
                for field in range(4)
                for pair in range(8)
            ],
            0,
        ),
        edge_ref[...],
    )

    def put(slot, field, start):
        for pair in range(8):
            row = field * 64 + pair * 8
            near_ref[slot, field, pl.ds(pair, 8, stride=8), :] = both[
                row : row + 8, start : start + 128
            ]

    for field in range(4):
        put(REACH, field, 0)
        faces.start(field)

    def table_copy(place):
        shift = SHIFTS[place]
        return remote(
            refine_ref, table_ref.at[REACH - shift], send2.at[place], recv2.at[place], me + shift
        )

    table_ref[REACH] = refine_ref[...]
    for place, shift in enumerate(SHIFTS):
        pl.when(within(me + shift, count))(table_copy(place).start)

    for field in range(4):
        put(2 * REACH + 1, field, 128)
    extract_layers(2 * REACH + 1, 4, False)
    extract_layers(2 * REACH + 1, 5, False)
    faces.forward(4)
    faces.forward(5)
    faces.forward(0)
    faces.forward(1)
    faces.forward(2)
    faces.forward(3)
    faces.finish()
    for place, shift in enumerate(SHIFTS):
        pl.when(within(me + shift, count))(table_copy(place).wait_send)
        pl.when(within(me - shift, count))(table_copy(place).wait_recv)


def packets_kernel(count, own_ref, near_ref, send, recv):
    me = lax.axis_index("sfc")
    pieces = range(own_ref.shape[0])
    packets = Direct(me, count, near_ref, pieces, send, recv)
    barrier, number = greet(me, packets.peers())
    near_ref[REACH] = own_ref[...]
    pl.semaphore_wait(barrier, number)
    for piece in pieces:
        packets.start(piece)
    packets.finish()


def solve(h, g):
    (h00, h01, h02, h03, h11, h12, h13, h22, h23, h33) = h
    i0 = 1.0 / h00
    l10, l20, l30 = h01 * i0, h02 * i0, h03 * i0
    d1 = h11 - l10 * h01
    a21, a31 = h12 - l10 * h02, h13 - l10 * h03
    i1 = 1.0 / d1
    l21, l31 = a21 * i1, a31 * i1
    d2 = h22 - l20 * h02 - l21 * a21
    a32 = h23 - l20 * h03 - l21 * a31
    i2 = 1.0 / d2
    l32 = a32 * i2
    d3 = h33 - l30 * h03 - l31 * a31 - l32 * a32
    y1 = g[1] - l10 * g[0]
    y2 = g[2] - l20 * g[0] - l21 * y1
    y3 = g[3] - l30 * g[0] - l31 * y1 - l32 * y2
    x3 = y3 / d3
    x2 = y2 * i2 - l32 * x3
    x1 = y1 * i1 - l21 * x2 - l31 * x3
    x0 = g[0] * i0 - l10 * x1 - l20 * x2 - l30 * x3
    return x0, x1, x2, x3


def fit(points, params):
    width = 128

    def normal_equations(start, params):
        a, b, c, d = [p[:, start : start + width] for p in params]
        h = [None] * 10
        g = [None] * 4

        def add(total, place, term):
            total[place] = term if total[place] is None else total[place] + term

        for point in points:
            px, py, pz, f = [value[:, start : start + width] for value in point]
            t = jnp.tanh(a * px + b * py + c * pz + d)
            s = 1.0 - t * t
            q = s * s
            w = s * (t - f)
            qx, qy, qz = q * px, q * py, q * pz
            for place, term in enumerate(
                (qx * px, qx * py, qx * pz, qx, qy * py, qy * pz, qy, qz * pz, qz, q)
            ):
                add(h, place, term)
            for place, term in enumerate((w * px, w * py, w * pz, w)):
                add(g, place, term)
        for place in (0, 4, 7, 9):
            h[place] = h[place] + 4.0 * DAMPING
        return h + g

    def one_pass(_unused, params):
        parts = [normal_equations(start, params) for start in range(0, params[0].shape[1], width)]
        sums = [jnp.concatenate(part, 1) for part in zip(*parts)]
        step = solve(sums[:10], sums[10:])
        return tuple(p - s for p, s in zip(params, step))

    return lax.fori_loop(0, PASSES, one_pass, params)


def fit_kernel(
    fraction_ref,
    centroid_ref,
    speed_ref,
    edge_ref,
    ghost_ref,
    near_ref,
    neighbours_ref,
    refine_ref,
    planes_ref,
    fine_table,
    packets_ref,
    padded,
    ghost_edges,
    ghost_layers,
    ghost_z_cells,
    layers,
):
    me = lax.axis_index("sfc")
    lane = lanes()
    row = lax.broadcasted_iota(jnp.int32, VEC, 0)
    first_block = (me - REACH) * BLK

    for block in range(BLK):
        place = []
        for k in range(6):
            other = neighbours_ref[block, k]
            place.append(
                jnp.where(
                    other >= 0,
                    jnp.clip(other - first_block, 0, (2 * REACH + 1) * BLK - 1),
                    (2 * REACH + 1) * BLK + block,
                )
            )

        def face(k, item):
            return near_ref[place[k] // BLK, item, place[k] % BLK]

        for field in range(4):
            value = face(5, field)
            for k in (4, 3, 2):
                value = jnp.where(lane < (k - 1) * 32, face(k, field), value)
            ghost_edges[block * 32 + field * 8 : block * 32 + field * 8 + 8, :] = value
        for half in range(2):
            ghost_layers[half, block * 8 : block * 8 + 8, :] = jnp.where(
                row < 4, face(0, 4 + half), face(1, 4 + half)
            )

    for field in range(4):
        for half in range(2):
            for side in range(2):
                start = side * 4352 + half * 128
                padded[field, :, start : start + 128] = ghost_layers[
                    half, pl.ds(side * 4 + field, 8, stride=8), :
                ]
        padded[field, :, 256:4352] = field_rows(fraction_ref, centroid_ref, field, 0, CELLS)

    wide = lax.broadcasted_iota(jnp.int32, (8, 512), 1)
    y_pos = wide // 16 % 16
    z_pos = wide % 16
    z_cells = select(ghost_edges[...], ghost_ref[...])
    for tile in range(4):
        ghost_z_cells[tile] = z_cells[:, tile * 128 : tile * 128 + 128]

    def side_ghosts(ghost):
        shifts = (0, 80, 112, 64)
        return jnp.concatenate([pltpu.roll(ghost, i, 1) if i else ghost for i in shifts], 1)

    def stencil(pair):
        start = pl.multiple_of(pair * 512, 512)
        fields = [[] for _unused in range(7)]
        for field in range(4):
            center = padded[field, :, pl.ds(start + 256, 512)]
            ghost = ghost_edges[pl.ds(field * 8 + pair, 8, stride=32), :]
            ghost_y = side_ghosts(ghost)
            ghost_z = jnp.concatenate(
                [ghost_z_cells[i, pl.ds(field * 8 + pair, 8, stride=32), :] for i in range(4)], 1
            )
            fields[0].append(center)
            fields[1].append(padded[field, :, pl.ds(start, 512)])
            fields[2].append(padded[field, :, pl.ds(start + 512, 512)])
            fields[3].append(jnp.where(y_pos == 0, ghost_y, pltpu.roll(center, 16, 1)))
            fields[4].append(jnp.where(y_pos == 15, ghost_y, pltpu.roll(center, 496, 1)))
            fields[5].append(jnp.where(z_pos == 0, ghost_z, pltpu.roll(center, 1, 1)))
            fields[6].append(jnp.where(z_pos == 15, ghost_z, pltpu.roll(center, 511, 1)))
        a, b, c = [2.0 * (fields[2 + 2 * i][0] - fields[1 + 2 * i][0]) for i in range(3)]
        frac, cx, cy, cz = fields[0]
        d = 2.0 * (2.0 * frac - 1.0) - a * cx - b * cy - c * cz
        points = [(cx, cy, cz, 2.0 * frac - 1.0)]
        for k in range(6):
            f, *coords = fields[k + 1]
            coords[k // 2] = coords[k // 2] + (2.0 * (k % 2) - 1.0)
            points.append((*coords, 2.0 * f - 1.0))
        return points, (a, b, c, d)

    together = 4

    def some_pairs(number, carry):
        pairs = [number * together + i for i in range(together)]
        stencils = [stencil(pair) for pair in pairs]
        points = [
            tuple(jnp.concatenate(values, 1) for values in zip(*same))
            for same in zip(*[points for points, _unused in stencils])
        ]
        params = fit(
            points, tuple(jnp.concatenate(values, 1) for values in zip(*[p for _unused, p in stencils]))
        )
        for i, pair in enumerate(pairs):
            start = pl.multiple_of(pair * 512, 512)
            for comp in range(4):
                value = params[comp][:, i * 512 : i * 512 + 512]
                planes_ref[:, comp, pl.ds(start, 512)] = value
                layers[pl.ds(pl.multiple_of(pair * 32 + comp * 8, 8), 8), :] = value
        return carry

    lax.fori_loop(0, 8 // together, some_pairs, 0)

    edge_values = select(layers[...], edge_ref[:, 128:])
    for pair in range(8):
        for comp in range(4):
            row_at = pair * 32 + comp * 8
            fine_table[pl.ds(comp * 16 + 8 + pair, 8, stride=FINE_ROWS), :] = edge_values[
                row_at : row_at + 8
            ]
    for comp in range(4):
        for part in range(8):
            start = part // 4 * 128
            fine_table[pl.ds(comp * 16 + part, 8, stride=FINE_ROWS), :] = layer_parts(
                layers[comp * 8 : comp * 8 + 8, start : start + 128],
                layers[224 + comp * 8 : 232 + comp * 8, 256 + start : 384 + start],
                part % 4,
            )

    slots = refine_ref.shape[1]
    for first in range(0, slots, 4):
        whole = [jnp.zeros(VEC, jnp.float32)] * 3
        for slot in range(first, min(first + 4, slots)):
            block = jnp.clip(refine_ref[0, slot] - me * BLK, 0, BLK - 1)
            k = jnp.clip(refine_ref[1, slot], 0, 5)
            yz = (k >= 2).astype(jnp.int32)
            base = block * FINE_ROWS + yz * 8
            shift = (128 + 32 * (slot - first) - 32 * (k - 2 * yz)) % 128
            values = [
                fine_table[pl.ds(pl.multiple_of(base + comp * 16, 8), 8), :] for comp in (k // 2, 3)
            ]
            values.append(speed_ref[pl.ds(pl.multiple_of(block * 16 + yz * 8, 8), 8), :])
            whole = [
                jnp.where(lane // 32 == slot - first, pltpu.roll(value, shift, 1), other)
                for value, other in zip(values, whole)
            ]
        for item in range(3):
            start = (first // 4 * 3 + item) * 8
            packets_ref[start : start + 8, :] = whole[item]


def flux_kernel(faces_ref, speed_ref, packets_ref, table_ref, reflux_ref, live_list):
    me = lax.axis_index("sfc")
    lane = lanes()
    row = lax.broadcasted_iota(jnp.int32, VEC, 0)
    pos = lane % 32
    cell = pos % 16 // 2
    slots = table_ref.shape[2]

    found = 0
    for offset in range(2 * REACH + 1):
        other = me + offset - REACH
        there = (other >= 0) & (other < lax.axis_size("sfc"))

        def collect(slot, found):
            local = table_ref[offset, 2, slot] - me * BLK
            mine = there & (table_ref[offset, 0, slot] >= 0) & (local >= 0) & (local < BLK)
            live_list[found] = offset * slots + slot
            return found + mine.astype(jnp.int32)

        found = lax.fori_loop(0, slots, collect, found, unroll=4 if slots % 4 == 0 else 1)
    for extra in range(3):
        live_list[found + extra] = REACH * slots

    reflux_ref[...] = jnp.zeros_like(reflux_ref)

    offset_one = ((pos // 16).astype(jnp.float32) - 0.5) * 0.5
    offset_two = ((pos % 2).astype(jnp.float32) - 0.5) * 0.5

    def moments(item, weight):
        offset = item // slots
        slot = item % slots
        k = jnp.clip(table_ref[offset, 1, slot], 0, 5)
        block = jnp.clip(table_ref[offset, 2, slot] - me * BLK, 0, BLK - 1)
        quadrant = jnp.clip(table_ref[offset, 3, slot], 0, 3)
        qa, qb = quadrant // 2, quadrant % 2
        facing = k + 1 - 2 * (k % 2)
        axis = k // 2
        sign = (2 * (k % 2) - 1).astype(jnp.float32)
        yz = (k >= 2).astype(jnp.int32)
        from_row = qa * 4 + row // 2
        from_lane = (facing - 2 * yz) * 32 + row % 2 * 16 + qb * 8 + cell
        base = block * FINE_ROWS + yz * 8
        first = jnp.where(axis == 0, 1, 0)
        second = jnp.where(axis == 2, 1, 2)
        sources = [
            faces_ref[pl.ds(pl.multiple_of(base + comp * 16, 8), 8), :]
            for comp in (axis, first, second, 3)
        ]
        sources.append(speed_ref[pl.ds(pl.multiple_of(block * 16 + yz * 8, 8), 8), :])
        normal_c, one_c, two_c, d_c, u_c = [
            take(
                jnp.take_along_axis(source, from_row, axis=0, mode="promise_in_bounds"), from_lane
            )
            for source in sources
        ]
        back = (128 - 32 * (slot % 4)) % 128
        normal_f, d_f, u_f = [
            pltpu.roll(packets_ref[offset, slot // 4 * 3 + item], back, 1) for item in range(3)
        ]
        speed = sign * 0.5 * (u_f + u_c)
        depth = jnp.abs(speed) * TIME_STEP
        outflow = jnp.maximum(speed, 0.0)
        inflow = jnp.minimum(speed, 0.0)
        tangent = one_c * offset_one + two_c * offset_two + d_c
        volume = jnp.zeros(VEC, jnp.float32)
        moment = jnp.zeros(VEC, jnp.float32)
        for node in NODES:
            fine_model = 0.5 * (
                1.0 + jnp.tanh(normal_f * (sign * (0.5 - node * depth)) + d_f)
            )
            coarse_model = 0.5 * (
                1.0 + jnp.tanh(normal_c * (-sign * (0.5 - 0.5 * node * depth)) + tangent)
            )
            volume = volume + 0.5 * TIME_STEP * (outflow * fine_model + inflow * coarse_model)
            moment = moment + 0.5 * TIME_STEP * node * depth * sign * (
                inflow * coarse_model - outflow * fine_model
            )
        both = jnp.where(lane < 32, volume, pltpu.roll(moment, 32, 1))
        both = both + pltpu.roll(both, 127, 1)
        both = both + pltpu.roll(both, 112, 1)
        keep = (lane // 16 == row) & (lane % 16 // 8 == qb) & weight
        rows = []
        for m in range(2):
            placed = jnp.where(keep, take(both, m * 32 + 2 * (lane % 8)), 0.0)
            rows.append(jnp.sum(placed, axis=0, keepdims=True))
        return rows, block, facing, qa

    def group(number, carry):
        results = [
            moments(live_list[number * 4 + i], number * 4 + i < found) for i in range(4)
        ]
        for rows, block, facing, qa in results:
            start = pl.multiple_of(qa * 128, 128)
            for m in range(2):
                reflux_ref[block, facing, m : m + 1, pl.ds(start, 128)] += rows[m]
        return carry

    lax.fori_loop(0, (found + 3) // 4, group, 0)


def spec(space):
    return pl.BlockSpec(memory_space=space)


def per_device(fraction, centroid, velocity, neighbours, refinement):
    count = lax.axis_size("sfc")
    slots = refinement.shape[0]
    packet_rows = -(-slots // 4) * 3 * 8
    vmem, smem = spec(pltpu.VMEM), spec(pltpu.SMEM)
    f32 = jnp.float32
    refinement = refinement.T
    centroid, velocity = jnp.swapaxes(centroid, 0, 1), jnp.swapaxes(velocity, 0, 1)
    edge = edge_matrix()
    near, table, speeds = pl.pallas_call(
        lambda *refs: faces_kernel(count, *refs),
        out_shape=(
            jax.ShapeDtypeStruct((6, ITEMS, BLK * 8, 128), f32),
            jax.ShapeDtypeStruct((5, 4, slots), jnp.int32),
            jax.ShapeDtypeStruct((BLK * 16, 128), f32),
        ),
        in_specs=[vmem] * 5,
        out_specs=(vmem,) * 3,
        scratch_shapes=[pltpu.SemaphoreType.DMA((4, ITEMS))] * 2
        + [pltpu.SemaphoreType.DMA((4,))] * 2,
        compiler_params=pltpu.CompilerParams(collective_id=0, has_side_effects=True),
        name="exchange_faces",
    )(fraction, centroid, velocity, refinement, edge)
    planes, faces, packets = pl.pallas_call(
        fit_kernel,
        out_shape=(
            jax.ShapeDtypeStruct((BLK, 4, CELLS), f32),
            jax.ShapeDtypeStruct((BLK * FINE_ROWS, 128), f32),
            jax.ShapeDtypeStruct((packet_rows, 128), f32),
        ),
        in_specs=[vmem] * 6 + [smem] * 2,
        out_specs=(vmem,) * 3,
        scratch_shapes=[
            pltpu.VMEM((4, 8, CELLS + 512), f32),
            pltpu.VMEM((256, 128), f32),
            pltpu.VMEM((2, 64, 128), f32),
            pltpu.VMEM((4, 256, 128), f32),
            pltpu.VMEM((256, 512), f32),
        ],
        name="fit_planes",
    )(
        fraction,
        centroid,
        speeds,
        edge,
        ghost_matrix(),
        near.reshape(6, ITEMS, BLK, 8, 128),
        neighbours,
        refinement,
    )
    near_packets = pl.pallas_call(
        lambda *refs: packets_kernel(count, *refs),
        out_shape=jax.ShapeDtypeStruct((5, 1, packet_rows, 128), f32),
        in_specs=[vmem],
        out_specs=vmem,
        scratch_shapes=[pltpu.SemaphoreType.DMA((4, 1))] * 2,
        compiler_params=pltpu.CompilerParams(collective_id=1, has_side_effects=True),
        name="exchange_packets",
    )(packets.reshape(1, packet_rows, 128))
    reflux = pl.pallas_call(
        flux_kernel,
        out_shape=jax.ShapeDtypeStruct((BLK, 6, 2, 256), f32),
        in_specs=[vmem] * 3 + [smem],
        out_specs=vmem,
        scratch_shapes=[pltpu.SMEM((5 * slots + 4,), jnp.int32)],
        name="reflux_moments",
    )(faces, speeds, near_packets.reshape(5, packet_rows // 8, 8, 128), table)
    return planes, reflux


def solution(mesh):
    return jax.shard_map(
        per_device,
        mesh=mesh,
        in_specs=(
            P("sfc", None),
            P("sfc", None, None),
            P("sfc", None, None),
            P("sfc", None),
            P("sfc", None),
        ),
        out_specs=(P("sfc", None, None), P("sfc", None, None, None)),
        check_vma=False,
    )
```
